32 devices in a mesh: batch: 8 (over y, x, core), tp: 4 (over z).
Axes of the slice: x: 2, y: 2, z: 4, core: 2. Of those that a mesh axis runs over, the one named last changes fastest.
Arguments:
- tokens: bfloat16 [64, 256, 1152], P(('batch', 'tp')), may hold values from -6 to 6
- conditioning: bfloat16 [64, 1152], P('batch'), may hold values from -6 to 6
- bucket: int32 [64], P('batch'), may hold values from 0 to 2, as said below
- kept_index: int32 [64, 128], P(('batch', 'tp')), may hold values from 0 to 255, as said below
- w_ada: bfloat16 [1152, 6912], P(None, 'tp'), may hold values from -0.1875 to 0.1875
- ada_bias: bfloat16 [6912], P('tp'), may hold values from -3 to 3
- w_qkv: bfloat16 [3, 1152, 1152], P(None, None, 'tp'), may hold values from -0.1875 to 0.1875
- qv_bias: bfloat16 [2, 1152], P(None, 'tp'), may hold values from -3 to 3
- w_proj: bfloat16 [1152, 1152], P('tp'), may hold values from -0.75 to 0.75
- proj_bias: bfloat16 [1152], replicated, may hold values from -3 to 3
- w_expand: bfloat16 [1152, 4608], P(None, 'tp'), may hold values from -0.1875 to 0.1875
- expand_bias: bfloat16 [4608], P('tp'), may hold values from -3 to 3
- w_reduce: bfloat16 [4608, 1152], P('tp'), may hold values from -0.09375 to 0.09375
- reduce_bias: bfloat16 [1152], replicated, may hold values from -3 to 3
- out_grad: bfloat16 [64, 256, 1152], P(('batch', 'tp')), may hold values from -6 to 6
Outputs:
- output: bfloat16 [64, 256, 1152], P(('batch', 'tp'))
- tokens_grad: bfloat16 [64, 256, 1152], P(('batch', 'tp'))
- w_ada_grad: float32 [1152, 6912], P(None, 'tp')
- ada_bias_grad: float32 [6912], P('tp')
- w_qkv_grad: float32 [3, 1152, 1152], P(None, None, 'tp')
- qv_bias_grad: float32 [2, 1152], P(None, 'tp')
- w_proj_grad: float32 [1152, 1152], P('tp')
- proj_bias_grad: float32 [1152], replicated
- w_expand_grad: float32 [1152, 4608], P(None, 'tp')
- expand_bias_grad: float32 [4608], P('tp')
- w_reduce_grad: float32 [4608, 1152], P('tp')
- reduce_bias_grad: float32 [1152], replicated
The draws below stay inside these ranges and needn't reach their ends.
Inputs may be any that keep to these rules, and one draw needn't show every extreme that they name: The bucket of each latent: 0 for a 16 x 16 grid of 256 real tokens, 1 for 12 x 20 and 2 for 20 x 12, both of 240 real tokens; real tokens take the first slots, padding the rest. `kept_index`: row l lists distinct slots of latent l. Its first (real tokens) // 2 entries are real slots, the tokens that pass through the block; any later entries name padding slots and are ignored.
All inputs are finite; a program needn't handle non-finite values.
Results may differ from the reference program's by a relative error of at most 0.02.
Values may be sent and summed in bfloat16 or wider, within the bound.
A program may use at most 192 MiB of HBM per device.

```python
import math
import jax
import jax.numpy as jnp
from jax import lax

D = 1152
HEAD_SIZE = 72
FF = 4608
POS = 256
KEEP = 128
LATENTS = 64
MOD = 6912


def shuffle_one(order_key):
    return jax.random.permutation(order_key, POS).astype(jnp.int32)


def shared_routes(key):
    bucket_key, order_key = jax.random.split(key)
    bucket = jax.random.randint(bucket_key, (LATENTS,), 0, 3).astype(jnp.int32)
    real = POS - POS // 16 * (bucket > 0).astype(jnp.int32)
    orders = jax.vmap(shuffle_one)(jax.random.split(order_key, LATENTS))
    slots = jnp.arange(POS, dtype=jnp.int32)[None, :]
    ranking = orders + POS * (slots >= real[:, None]).astype(jnp.int32)
    picked = jnp.argsort(ranking, axis=1, stable=True)[:, :KEEP].astype(jnp.int32)
    kept_count = real // 2
    column = jnp.arange(KEEP, dtype=jnp.int32)[None, :]
    filler = real[:, None] + column - kept_count[:, None]
    chosen = jnp.where(column < kept_count[:, None], picked, filler).astype(jnp.int32)
    return (bucket, chosen)


def draw_bucket(key, part):
    return shared_routes(key)[0]


def draw_kept_index(key, part):
    return shared_routes(key)[1]


def gauss_values(key, shape, spread):
    return jnp.clip(jax.random.normal(key, shape, jnp.float32) * spread, -6.0 * spread, 6.0 * spread).astype(jnp.bfloat16)


def draw_tokens(key, part):
    key = jax.random.fold_in(key, 11)
    return gauss_values(key, (LATENTS, POS, D), 1.0)


def draw_conditioning(key, part):
    key = jax.random.fold_in(key, 12)
    return gauss_values(key, (LATENTS, D), 1.0)


def draw_out_grad(key, part):
    key = jax.random.fold_in(key, 13)
    return gauss_values(key, (LATENTS, POS, D), 1.0)


def draw_ada_bias(key, part):
    key = jax.random.fold_in(key, 14)
    return gauss_values(key, (6 * D,), 0.5)


def draw_qv_bias(key, part):
    key = jax.random.fold_in(key, 15)
    return gauss_values(key, (2, D), 0.5)


def draw_proj_bias(key, part):
    key = jax.random.fold_in(key, 16)
    return gauss_values(key, (D,), 0.5)


def draw_expand_bias(key, part):
    key = jax.random.fold_in(key, 17)
    return gauss_values(key, (FF,), 0.5)


def draw_reduce_bias(key, part):
    key = jax.random.fold_in(key, 18)
    return gauss_values(key, (D,), 0.5)


def shard_levels(stream_key, extent, cuts, smallest, high):
    gain = 1.0
    for position, blocks in cuts:
        heights = jax.random.uniform(jax.random.fold_in(jax.random.fold_in(stream_key, 6), position), (blocks,), jnp.float32, smallest / len(cuts), high / len(cuts))
        gain = gain * jnp.repeat(jnp.exp(heights), extent[position] // blocks).reshape((-1,) + (1,) * (len(extent) - 1 - position))
    return gain


def gaussian(rng, dims, scale, reach, cuts=(), kind=jnp.bfloat16):
    entries = scale * jax.random.normal(rng, dims, jnp.float32)
    if cuts:
        entries = entries * shard_levels(rng, dims, cuts, -0.22, 0.18)
    return jnp.clip(entries, -reach, reach).astype(kind)


def setup_inputs(seed: int = 0) -> dict:
    key_list = jax.random.split(jax.random.key(seed), 16)
    tokens = draw_tokens(jax.random.fold_in(key_list[15], 71), 0)
    conditioning = draw_conditioning(jax.random.fold_in(key_list[15], 71), 0)
    bucket = draw_bucket(jax.random.fold_in(key_list[15], 71), 0)
    kept_index = draw_kept_index(jax.random.fold_in(key_list[15], 71), 0)
    w_ada = gaussian(key_list[4], (D, MOD), D ** -0.5, 0.1875, ((1, 4),))
    ada_bias = draw_ada_bias(jax.random.fold_in(key_list[15], 71), 0)
    w_qkv = gaussian(key_list[6], (3, D, D), D ** -0.5, 0.1875, ((2, 4),))
    qv_bias = draw_qv_bias(jax.random.fold_in(key_list[15], 71), 0)
    w_proj = gaussian(key_list[8], (D, D), HEAD_SIZE ** -0.5, 0.75, ((0, 4),))
    proj_bias = draw_proj_bias(jax.random.fold_in(key_list[15], 71), 0)
    w_expand = gaussian(key_list[10], (D, FF), D ** -0.5, 0.1875, ((1, 4),))
    expand_bias = draw_expand_bias(jax.random.fold_in(key_list[15], 71), 0)
    w_reduce = gaussian(key_list[12], (FF, D), FF ** -0.5, 0.09375, ((0, 4),))
    reduce_bias = draw_reduce_bias(jax.random.fold_in(key_list[15], 71), 0)
    out_grad = draw_out_grad(jax.random.fold_in(key_list[15], 71), 0)
    return {"tokens": tokens, "conditioning": conditioning, "bucket": bucket, "kept_index": kept_index, "w_ada": w_ada, "ada_bias": ada_bias, "w_qkv": w_qkv, "qv_bias": qv_bias, "w_proj": w_proj, "proj_bias": proj_bias, "w_expand": w_expand, "expand_bias": expand_bias, "w_reduce": w_reduce, "reduce_bias": reduce_bias, "out_grad": out_grad}


@jax.custom_vjp
def low(v):
    return lax.optimization_barrier(v.astype(jnp.bfloat16)).astype(jnp.float32)

@jax.custom_vjp
def low_back(v):
    return v

def low_keep(v):
    return (low(v), None)

def low_pass(kept, grad):
    return (grad,)

def back_keep(v):
    return (v, None)

def back_low(kept, grad):
    return (low(grad),)
low.defvjp(low_keep, low_pass)
low_back.defvjp(back_keep, back_low)
layer_eps = 1e-06
highest = lax.Precision.HIGHEST

def normalize(rows):
    center = rows - lax.optimization_barrier(jnp.mean(rows, axis=-1, keepdims=True))
    spread = lax.optimization_barrier(jnp.mean(center * center, axis=-1, keepdims=True))
    return center * lax.rsqrt(spread + layer_eps)

def both_round(values):
    return low(low_back(values))

def head_view(rows):
    return rows.reshape(rows.shape[0], rows.shape[1], rows.shape[2] // HEAD_SIZE, HEAD_SIZE)

def place_one(base, where_at, extra):
    return base.at[where_at].add(extra)

def place_rows(base, index, extra):
    return jax.vmap(place_one)(base, index, extra)

def forward(params, tokens, conditioning, kept, valid):
    w_ada, ada_bias, w_qkv, qv_bias, w_proj, proj_bias, w_expand, expand_bias, w_reduce, reduce_bias = params
    count = tokens.shape[0]
    silu_low = low(jax.nn.silu(conditioning))
    modulation = (jnp.dot(silu_low, w_ada, precision=highest) + ada_bias).reshape(count, 6, 1, D)
    shift_a, scale_a, gate_a, shift_b, scale_b, gate_b = [modulation[:, index] for index in range(6)]
    selected = jnp.take_along_axis(tokens, kept[:, :, None], axis=1)
    attn_in = low(normalize(selected) * (1.0 + scale_a) + shift_a)
    queries = both_round(jnp.einsum('gkd,dc->gkc', attn_in, w_qkv[0], precision=highest) + qv_bias[0])
    key_rows = both_round(jnp.einsum('gkd,dc->gkc', attn_in, w_qkv[1], precision=highest))
    value_rows = both_round(jnp.einsum('gkd,dc->gkc', attn_in, w_qkv[2], precision=highest) + qv_bias[1])
    raw = jnp.einsum('gqhd,gkhd->ghqk', head_view(queries), head_view(key_rows), precision=highest)
    scores = jnp.where(valid[:, None, None, :] > 0, low_back(raw * HEAD_SIZE ** (-0.5)), -1000000000.0)
    top = lax.optimization_barrier(jnp.max(scores, axis=-1, keepdims=True))
    weights = jnp.exp(scores - top)
    total = lax.optimization_barrier(jnp.sum(weights, axis=-1, keepdims=True))
    probs = low(weights / total)
    mixed = jnp.einsum('ghqk,gkhd->gqhd', probs, head_view(value_rows), precision=highest)
    merged = both_round(mixed.reshape(queries.shape))
    attn_out = low_back(jnp.einsum('gkc,cd->gkd', merged, w_proj, precision=highest) + proj_bias)
    hidden = selected + gate_a * attn_out
    mlp_in = low(normalize(hidden) * (1.0 + scale_b) + shift_b)
    pre_act = low_back(jnp.einsum('gkd,df->gkf', mlp_in, w_expand, precision=highest) + expand_bias)
    activated = low(jax.nn.gelu(pre_act, approximate=True))
    mlp_out = low_back(jnp.einsum('gkf,fd->gkd', activated, w_reduce, precision=highest) + reduce_bias)
    delta = (gate_a * attn_out + gate_b * mlp_out) * valid[:, :, None]
    return place_rows(tokens, kept, delta)

def reference(tokens, conditioning, bucket, kept_index, w_ada, ada_bias, w_qkv, qv_bias, w_proj, proj_bias, w_expand, expand_bias, w_reduce, reduce_bias, out_grad):
    params = tuple((item.astype(jnp.float32) for item in (w_ada, ada_bias, w_qkv, qv_bias, w_proj, proj_bias, w_expand, expand_bias, w_reduce, reduce_bias)))
    group = math.gcd(LATENTS, 32)
    blocks = LATENTS // group
    real = POS - POS // 16 * (bucket > 0).astype(jnp.int32)
    valid = (jnp.arange(KEEP, dtype=jnp.int32)[None, :] < (real // 2)[:, None]).astype(jnp.float32)

    def split(values):
        return values.reshape((blocks, group) + values.shape[1:])

    def one_block(totals, pieces):
        block_tokens, block_cond, block_kept, block_valid, block_cot = pieces

        def local(weight_set, rows):
            return forward(weight_set, rows, block_cond.astype(jnp.float32), block_kept, block_valid)
        result, pull = jax.vjp(local, params, block_tokens.astype(jnp.float32))
        weight_grads, token_grads = pull(block_cot.astype(jnp.float32))
        summed = tuple((left + right for left, right in zip(totals, weight_grads)))
        return (summed, (result.astype(jnp.bfloat16), token_grads.astype(jnp.bfloat16)))
    start = tuple((jnp.zeros(item.shape, jnp.float32) for item in params))
    totals, (outputs, token_grad_all) = lax.scan(one_block, start, (split(tokens), split(conditioning), split(kept_index), split(valid), split(out_grad)))
    return (outputs.reshape(LATENTS, POS, D), token_grad_all.reshape(LATENTS, POS, D), totals[0], totals[1], totals[2], totals[3], totals[4], totals[5], totals[6], totals[7], totals[8], totals[9])
```

```python
import functools
import jax
import jax.numpy as jnp
from jax import lax
from jax.experimental import pallas as pl
from jax.experimental.pallas import tpu as pltpu
from jax.sharding import PartitionSpec as P

HEAD_SIZE = 72
EPS = 1e-06
F32 = jnp.float32
BF = jnp.bfloat16
MESH = pl.DeviceIdType.MESH
MIB = 2**20


def nn(a, b):
    return lax.dot_general(a, b, (((1,), (0,)), ((), ())), preferred_element_type=F32)


def nt(a, b):
    return lax.dot_general(a, b, (((1,), (1,)), ((), ())), preferred_element_type=F32)


def tn(a, b):
    return lax.dot_general(a, b, (((0,), (0,)), ((), ())), preferred_element_type=F32)


def flip(b, mask):
    out, bit = b, 1
    while bit <= mask:
        if mask & bit:
            out = out + bit - 2 * bit * ((b // bit) % 2)
        bit *= 2
    return out


def group_size(ff_shard, width_shard):
    for size in (8, 4, 2):
        rows = ff_shard // size
        if ff_shard % size == 0 and rows % 16 == 0 and 4 * width_shard == size * rows:
            return size
    raise ValueError("no group")


def link_orders(group):
    bits = []
    bit = 2
    while bit < group:
        bits.append(bit)
        bit *= 2
    return bits, bits[::-1]


def span(bits):
    out = [0]
    for bit in bits:
        out = out + [item ^ bit for item in out]
    return out


def near_shard(z, k, count):
    low = jnp.minimum(z, count - 1 - z)
    both = z + (k // 2 + 1) * (1 - 2 * (k % 2))
    one = z + jnp.where(2 * z < count - 1, 1, -1) * (k - low + 1)
    return jnp.where(k < 2 * low, both, one)


class Gather:
    def __init__(self, b, z, group, region, send_sem, recv_sem, halves=2):
        self.b, self.z = b, z
        self.region, self.send_sem, self.recv_sem = region, send_sem, recv_sem
        self.orders = link_orders(group)[:halves] if halves == 2 else link_orders(group)[:1]
        self.group = group
        self.sent = []

    def copy(self, m, bit, p):
        return pltpu.make_async_remote_copy(
            src_ref=self.region(m, p, m),
            dst_ref=self.region(m, p, m ^ bit),
            send_sem=self.send_sem(m ^ bit, p),
            recv_sem=self.recv_sem(m ^ bit, p),
            device_id=(flip(self.b, bit), self.z),
            device_id_type=MESH,
        )

    def send(self, m, bit, p):
        cp = self.copy(m, bit, p)
        cp.start()
        self.sent.append(cp)

    def wait(self, m, p):
        ref = self.region(m, p, m)
        pltpu.make_async_remote_copy(
            src_ref=ref, dst_ref=ref, send_sem=self.send_sem(m, p), recv_sem=self.recv_sem(m, p),
            device_id=(flip(self.b, 1), self.z), device_id_type=MESH,
        ).wait_recv()

    def step(self, i):
        for p, order in enumerate(self.orders):
            if i == 0:
                fresh = [0]
            elif i <= len(order):
                fresh = [item ^ order[i - 1] for item in span(order[: i - 1])]
                for m in fresh:
                    self.wait(m, p)
            else:
                continue
            if i < len(order):
                for m in span(order[:i]):
                    self.send(m, order[i], p)
            for m in fresh:
                self.send(m, 1, p)

    def steps(self):
        return len(self.orders[0]) + 1

    def wait_core(self, m=None):
        for p in range(len(self.orders)):
            for item in range(1, self.group, 2):
                if m is None or item == m:
                    self.wait(item, p)

    def wait_sent(self):
        for cp in self.sent:
            cp.wait_send()


class Scatter:
    def __init__(self, b, z, group, mine, inbox, send_sem, recv_sem, add):
        self.b, self.z, self.group = b, z, group
        self.mine, self.inbox, self.add = mine, inbox, add
        self.send_sem, self.recv_sem = send_sem, recv_sem
        self.orders = link_orders(group)
        self.sent = []

    def top(self, m, p):
        if m & 1:
            return 1
        for bit in reversed(self.orders[p]):
            if m & bit:
                return bit

    def copy(self, m, p):
        return pltpu.make_async_remote_copy(
            src_ref=self.mine(m, p),
            dst_ref=self.inbox(m, p),
            send_sem=self.send_sem(m, p),
            recv_sem=self.recv_sem(m, p),
            device_id=(flip(self.b, self.top(m, p)), self.z),
            device_id_type=MESH,
        )

    def keys(self, m, p):
        if m & 1:
            return []
        out = [m ^ 1]
        order = self.orders[p]
        above = order if m == 0 else order[order.index(self.top(m, p)) + 1 :]
        return out + [m ^ bit for bit in reversed(above)]

    def fold(self, m, p):
        for key in self.keys(m, p):
            self.copy(key, p).wait_recv()
            self.add(m, key, p)

    def send(self, m, p):
        cp = self.copy(m, p)
        cp.start()
        self.sent.append(cp)

    def wait_sent(self):
        for cp in self.sent:
            cp.wait_send()


def barrier(b, z, group, count):
    sem = pltpu.get_barrier_semaphore()
    for m in range(1, group):
        pl.semaphore_signal(sem, 1, device_id=(flip(b, m), z), device_id_type=MESH)
    for d in range(1, count):
        pl.semaphore_signal(sem, 1, device_id=(b, lax.rem(z + d, count)), device_id_type=MESH)
    pl.semaphore_wait(sem, group - 1 + count - 1)


def stats(rows):
    center = rows - jnp.mean(rows, axis=-1, keepdims=True)
    return center, lax.rsqrt(jnp.mean(center * center, axis=-1, keepdims=True) + EPS)


def head_window(h, width):
    start = jnp.minimum(h * HEAD_SIZE // 128, width // 128 - 2) * 128
    lane = lax.broadcasted_iota(jnp.int32, (1, 256), 1) + (start - h * HEAD_SIZE)
    own = jnp.where((lane >= 0) & (lane < HEAD_SIZE), 1.0, 0.0)
    return pl.ds(pl.multiple_of(start, 128), 256), own


def first_kernel(
    dims, lat, real_ref, cond_ref, wada_ref, abias_ref, tok_ref, cot_in_ref, kept_ref, qvb_ref, projb_ref,
    own_qkv, own_proj, own_1, own_2,
    attn_in_o, q_o, k_o, v_o, merged_o, attn_out_o, hidden_o, mlp_in_o, cot_o, mod_o,
    full_o, all_1, all_2, dmlp_o,
    full, sm_send, sm_recv, nrm, sel, mg, mod8,
    sm_ss, sm_rs, za_ss, za_rs, zm_ss, zm_rs, ga_ss, ga_rs, gd_ss, gd_rs, loc,
):
    group, count, rows_s, width = dims
    b, z = lax.axis_index("batch"), lax.axis_index("tp")
    g = b % group
    ds = width // count
    slots = kept_ref.shape[1]
    barrier(b, z, group, count)

    cut = (rows_s // 2 + 15) // 16 * 16
    parts = ((0, cut), (cut, rows_s - cut))

    def piece(member, shard, p):
        at = member * rows_s
        lo, ln = parts[p] if p is not None else (0, rows_s)
        return full.at[at // ds, shard, pl.ds(at % ds + lo, ln)]

    own_copy = [
        pltpu.make_async_copy(own_qkv, full.at[0:3, z], loc.at[0]),
        pltpu.make_async_copy(own_proj, full.at[3, z], loc.at[5]),
    ]
    for cp in own_copy:
        cp.start()

    def line_a(shard, src, step, k):
        return pltpu.make_async_remote_copy(
            src_ref=src, dst_ref=piece(g, shard, None), send_sem=za_ss.at[k], recv_sem=za_rs.at[shard],
            device_id=(b, z + step), device_id_type=MESH,
        )

    def line_m(shard, src1, src2, step, k):
        return [
            pltpu.make_async_remote_copy(
                src_ref=src, dst_ref=dst.at[shard], send_sem=zm_ss.at[i, k], recv_sem=zm_rs.at[i, shard],
                device_id=(b, z + step), device_id_type=MESH,
            )
            for i, (src, dst) in enumerate(((src1, all_1), (src2, all_2)))
        ]

    slice_at = pl.ds(pl.multiple_of(g * rows_s, 16), rows_s)
    own_m = [
        pltpu.make_async_copy(own_1.at[slice_at], all_1.at[z], loc.at[2]),
        pltpu.make_async_copy(own_2.at[slice_at], all_2.at[z], loc.at[3]),
    ]
    for cp in own_m:
        cp.start()

    def both_ways(fn):
        @pl.when(z < count - 1)
        def _():
            fn(1, 0)

        @pl.when(z > 0)
        def _():
            fn(-1, 1)

    for cp in own_copy:
        cp.wait()
    both_ways(lambda step, k: line_a(z, piece(g, z, None), step, k).start())

    cond = cond_ref[...].astype(F32)
    silu = (cond / (1.0 + jnp.exp(-cond))).astype(BF)
    mod8[...] = jnp.zeros_like(mod8)
    cols = wada_ref.shape[0]
    mod8[:, 0:cols] = nt(silu, wada_ref[...]) + abias_ref[...].astype(F32)
    framed = pltpu.roll(mod8[...], (z * cols) % width, 1)
    for t in range(count):
        for i in range(2):
            sm_send[t, i] = framed[lat * t : lat * (t + 1), i * width : (i + 1) * width]
        sm_send[t, 2] = qvb_ref[...]

    def small(d):
        peer = lax.rem(z + d, count)
        return pltpu.make_async_remote_copy(
            src_ref=sm_send.at[peer], dst_ref=sm_recv.at[z], send_sem=sm_ss.at[d], recv_sem=sm_rs.at[d],
            device_id=(b, peer), device_id_type=MESH,
        )

    for d in range(1, count):
        small(d).start()
    small_own = pltpu.make_async_copy(sm_send.at[z], sm_recv.at[z], loc.at[1])
    small_own.start()

    valid = []
    for l in range(lat):
        real = real_ref[z * lat + l]
        row = lax.broadcasted_iota(jnp.int32, (slots, 1), 0)
        valid.append(jnp.where(row < real, 1.0, 0.0))
        place = lax.broadcasted_iota(jnp.int32, (slots, tok_ref.shape[1]), 1)
        pick = jnp.where(place == kept_ref[l], 1.0, 0.0).astype(BF)
        at = slice(l * slots, (l + 1) * slots)
        rows = nn(pick, tok_ref[l])
        sel[at] = rows
        center, inv = stats(rows)
        nrm[at] = center * inv
        cot_o[at] = (nn(pick, cot_in_ref[l]) * valid[l]).astype(BF)

    gathers = []
    for k in range(count - 1):
        shard = near_shard(z, k, count)

        def region(m, p, slot, shard=shard):
            return piece(flip(g, m), shard, p)

        gathers.append(
            Gather(b, z, group, region, lambda m, p, k=k: ga_ss.at[k, p, m], lambda m, p, shard=shard: ga_rs.at[shard, p, m])
        )

    def arrive_a(k):
        shard = near_shard(z, k, count)
        ref = piece(g, shard, None)
        line_a(shard, ref, 0, 2 + k).wait_recv()
        gathers[k].step(0)

        @pl.when((shard < z) & (z < count - 1))
        def _():
            line_a(shard, ref, 1, 2 + k).start()

        @pl.when((shard > z) & (z > 0))
        def _():
            line_a(shard, ref, -1, 2 + k).start()

    def arrive_m(k):
        shard = near_shard(z, k, count)
        r1, r2 = all_1.at[shard], all_2.at[shard]
        for cp in line_m(shard, r1, r2, 0, 2 + k):
            cp.wait_recv()

        @pl.when((shard < z) & (z < count - 1))
        def _():
            for cp in line_m(shard, r1, r2, 1, 2 + k):
                cp.start()

        @pl.when((shard > z) & (z > 0))
        def _():
            for cp in line_m(shard, r1, r2, -1, 2 + k):
                cp.start()

    def send_m(step, k):
        for cp in line_m(z, all_1.at[z], all_2.at[z], step, k):
            cp.start()

    arrive_a(0)
    for cp in own_m:
        cp.wait()

    for d in range(1, count):
        peer = lax.rem(z + d, count)
        ref = sm_recv.at[lax.rem(z - d + count, count)]
        pltpu.make_async_remote_copy(
            src_ref=ref, dst_ref=ref, send_sem=sm_ss.at[d], recv_sem=sm_rs.at[d], device_id=(b, peer),
            device_id_type=MESH,
        ).wait_recv()
    small_own.wait()
    blocks = [None] * 6
    for t in range(count):
        first = t * cols // width
        for i in range(2):
            if first + i < 6:
                part = sm_recv[t, i]
                blocks[first + i] = part if blocks[first + i] is None else blocks[first + i] + part
    for i in range(6):
        mod_o[i] = blocks[i]
    qv_bias = sm_recv[0, 2]
    for t in range(1, count):
        qv_bias = qv_bias + sm_recv[t, 2]
    for l in range(lat):
        at = slice(l * slots, (l + 1) * slots)
        attn_in_o[at] = (nrm[at] * (1.0 + mod_o[1, l : l + 1]) + mod_o[0, l : l + 1]).astype(BF)
        dmlp_o[0, at] = (cot_o[at].astype(F32) * mod_o[5, l : l + 1]).astype(BF)

    for k in range(1, count - 1):
        arrive_a(k)
        if k == 1:
            both_ways(send_m)
        gathers[k - 1].step(1)
    depth = gathers[0].steps()
    todo = [(i, k) for k in range(count - 1) for i in range(1, depth) if not (i == 1 and k < count - 2)]
    half_rows = slots * lat // 2

    def dm_region(m, p, slot):
        return dmlp_o.at[slot, pl.ds(p * half_rows, half_rows)]

    dm = Gather(b, z, group, dm_region, lambda m, p: gd_ss.at[p, m], lambda m, p: gd_rs.at[p, m])
    links = depth - 1
    todo.sort(key=lambda item: (item[0] >= links, item[0] + item[1], item[1]))
    started = False
    for i, k in todo:
        if i >= links and not started:
            dm.step(0)
            arrive_m(0)
            started = True
        gathers[k].step(i)
    for k in range(count - 1):
        gathers[k].wait_core()
    full_out = pltpu.make_async_copy(full, full_o, loc.at[4])
    full_out.start()

    for k in range(1, count - 2):
        arrive_m(k)
    dm.step(1)

    x = attn_in_o[...]
    for j, out in enumerate((q_o, k_o, v_o)):
        y = nt(x, full[j].reshape(width, width))
        if j != 1:
            y = y + qv_bias[j // 2 : j // 2 + 1]
        out[...] = y.astype(BF)

    scale = HEAD_SIZE**-0.5

    heads = width // HEAD_SIZE

    def some_heads(step, _):
        for h in (step, step + heads // 2):
            win, own = head_window(h, width)
            for l in range(lat):
                at = pl.ds(l * slots, slots)
                q = (q_o[at, win].astype(F32) * own).astype(BF)
                s = nt(q, k_o[at, win]) * scale
                key = lax.broadcasted_iota(jnp.int32, (1, slots), 1)
                s = jnp.where(key < real_ref[z * lat + l], s, -1000000000.0)
                w = jnp.exp(s - jnp.max(s, axis=-1, keepdims=True))
                pr = (w / jnp.sum(w, axis=-1, keepdims=True)).astype(BF)
                o = nn(pr, v_o[at, win])
                mg[at, win] = jnp.where(own > 0, o, mg[at, win])
        return 0

    lax.fori_loop(0, heads // 2, some_heads, 0)
    for i in range(2, dm.steps()):
        dm.step(i)
    merged_o[...] = mg[...].astype(BF)
    a_out = nn(merged_o[...], full[3].reshape(width, width)) + projb_ref[...].astype(F32)
    attn_out_o[...] = a_out
    for l in range(lat):
        at = slice(l * slots, (l + 1) * slots)
        rows = sel[at] + mod_o[2, l : l + 1] * attn_out_o[at]
        hidden_o[at] = rows
        center, inv = stats(rows)
        mlp_in_o[at] = (center * inv * (1.0 + mod_o[4, l : l + 1]) + mod_o[3, l : l + 1]).astype(BF)

    arrive_m(count - 2)
    dm.wait_core()
    for d in range(1, count):
        small(d).wait_send()
    both_ways(lambda step, k: line_a(z, piece(g, z, None), step, k).wait_send())

    def sent_m(step, k):
        for cp in line_m(z, all_1.at[z], all_2.at[z], step, k):
            cp.wait_send()

    both_ways(sent_m)
    for k in range(count - 1):
        shard = near_shard(z, k, count)

        @pl.when(((shard < z) & (z < count - 1)) | ((shard > z) & (z > 0)))
        def _():
            line_a(shard, piece(g, shard, None), 0, 2 + k).wait_send()
            for cp in line_m(shard, all_1.at[shard], all_2.at[shard], 0, 2 + k):
                cp.wait_send()

        gathers[k].wait_sent()
    dm.wait_sent()
    full_out.wait()


def run_first(dims, lat, real, cond, wada, abias, tok, cot, kept, qvb, projb, own_qkv, own_proj, own_1, own_2):
    group, count, rows_s, width = dims
    slots = kept.shape[1]
    rows = lat * slots
    vm = pl.BlockSpec(memory_space=pltpu.VMEM)
    hb = pl.BlockSpec(memory_space=pl.ANY)
    sm = pl.BlockSpec(memory_space=pltpu.SMEM)
    sd = jax.ShapeDtypeStruct
    row_bf, row_f = sd((rows, width), BF), sd((rows, width), F32)
    dma = pltpu.SemaphoreType.DMA
    return pl.pallas_call(
        functools.partial(first_kernel, dims, lat),
        out_shape=(
            row_bf, row_bf, row_bf, row_bf, row_bf, row_f, row_f, row_bf, row_bf, sd((6, lat, width), F32),
            sd((4, count, width // count, width), BF),
            sd((count, rows_s, own_1.shape[1]), BF),
            sd((count, rows_s, width), BF),
            sd((group, rows, width), BF),
        ),
        in_specs=[sm] + [vm] * 8 + [hb] * 4,
        out_specs=tuple([vm] * 10 + [hb] + [vm] * 3),
        scratch_shapes=[
            pltpu.VMEM((4, count, width // count, width), BF),
            pltpu.VMEM((count, 3, lat, width), F32),
            pltpu.VMEM((count, 3, lat, width), F32),
            pltpu.VMEM((rows, width), F32),
            pltpu.VMEM((rows, width), F32),
            pltpu.VMEM((rows, width), F32),
            pltpu.VMEM((cond.shape[0], 2 * width), F32),
            dma((count,)), dma((count,)),
            dma((count + 1,)), dma((count,)),
            dma((2, count + 1)), dma((2, count)),
            dma((count - 1, 2, group)), dma((count, 2, group)),
            dma((2, group)), dma((2, group)),
            dma((6,)),
        ],
        compiler_params=pltpu.CompilerParams(collective_id=1, has_side_effects=True, vmem_limit_bytes=56 * MIB),
        name="forward_attention",
    )(real, cond, wada, abias, tok, cot, kept, qvb, projb, own_qkv, own_proj, own_1, own_2)


GELU_C = 0.7978845608028654


def gelu_pair(v):
    sq = v * v
    t = jnp.tanh(GELU_C * v * (1.0 + 0.044715 * sq))
    half = 0.5 + 0.5 * t
    slope = half + 0.5 * GELU_C * v * (1.0 - t * t) * (1.0 + 3 * 0.044715 * sq)
    return v * half, slope


def middle_kernel(
    dims, x_ref, d_ref, w1_ref, w2_ref,
    din_o, out_o, g1_o, g2_o,
    xb, act, dpre, y, inbox, yo, inbox_o,
    ag_ss, ag_rs, rs_ss, rs_rs, ro_ss, ro_rs,
):
    group, count, rows_s, width = dims
    b, z = lax.axis_index("batch"), lax.axis_index("tp")
    rows = x_ref.shape[0]
    half = rows // 2
    hid = w1_ref.shape[0]
    xb[0] = x_ref[...]
    barrier(b, z, group, count)

    def part(ref):
        return lambda m, p: ref.at[m, pl.ds(p * half, half)]

    gather = Gather(
        b, z, group, lambda m, p, slot: part(xb)(slot, p), lambda m, p: ag_ss.at[p, m], lambda m, p: ag_rs.at[p, m]
    )
    gather.step(0)
    bias = nt(jnp.ones((8, w1_ref.shape[1] - width), BF), w1_ref[:, width:])[0:1]

    def forward(pair):
        (m0, p0), (m1, p1) = pair
        at = [(m0, slice(p0 * half, (p0 + 1) * half)), (m1, slice(p1 * half, (p1 + 1) * half))]
        x = jnp.concatenate([xb[m, s] for m, s in at], axis=0)
        d = jnp.concatenate([d_ref[m, s] for m, s in at], axis=0)
        a, slope = gelu_pair(nt(x, w1_ref[:, 0:width]) + bias)
        dp = (slope * nt(d, w2_ref[...])).astype(BF)
        a = a.astype(BF)
        for i, (m, s) in enumerate(at):
            to = slice(m * rows + s.start, m * rows + s.stop)
            act[to] = a[i * half : (i + 1) * half]
            dpre[to] = dp[i * half : (i + 1) * half]

    forward(((0, 0), (0, 1)))
    for p in range(2):
        gather.wait(1, p)
    forward(((1, 0), (1, 1)))
    for i in range(1, gather.steps()):
        gather.step(i)
        fresh = [[m ^ order[i - 1] for m in span(order[: i - 1])] for order in gather.orders]
        for m0, m1 in zip(*fresh):
            forward(((m0, 0), (m1, 1)))
        for m0, m1 in zip(*fresh):
            gather.wait(m0 ^ 1, 0)
            gather.wait(m1 ^ 1, 1)
            forward(((m0 ^ 1, 0), (m1 ^ 1, 1)))

    def reduction(own, boxes, ss, rs):
        mine, arrived = part(own), part(boxes)

        def add(m, key, p):
            mine(m, p)[...] = (mine(m, p)[...].astype(F32) + arrived(key, p)[...].astype(F32)).astype(BF)

        return Scatter(b, z, group, mine, arrived, lambda m, p: ss.at[p, m], lambda m, p: rs.at[p, m], add)

    rs_in = reduction(y, inbox, rs_ss, rs_rs)
    rs_out = reduction(yo, inbox_o, ro_ss, ro_rs)
    links = len(rs_in.orders[0])

    def part_in(m):
        y[m] = nn(dpre[m * rows : (m + 1) * rows], w1_ref[:, 0:width]).astype(BF)

    def part_out(m):
        yo[m] = nn(act[m * rows : (m + 1) * rows], w2_ref[...]).astype(BF)

    def send_core(rs, make):
        for m in range(group - 1, 0, -2):
            make(m)
            for p in range(2):
                rs.send(m, p)

    def last_link(rs, m):
        for p in range(2):
            if rs.top(m, p) == rs.orders[p][-1]:
                rs.fold(m, p)
                rs.send(m, p)

    def next_link(rs, i):
        for p in range(2):
            order = rs.orders[p]
            for m in span(order[: i - 1]):
                rs.fold(m ^ order[i - 1], p)
                rs.send(m ^ order[i - 1], p)

    def finish(rs, out):
        for p in range(2):
            total = rs.mine(0, p)[...].astype(F32)
            for key in rs.keys(0, p):
                rs.copy(key, p).wait_recv()
                total = total + rs.inbox(key, p)[...].astype(F32)
            out[p * half : (p + 1) * half] = total

    chunks = [slice(c, min(c + 128, hid)) for c in range(0, hid, 128)]

    def grads_1():
        ones = jnp.ones((group * rows, g1_o.shape[1] - width), BF)
        x = xb[...].reshape(group * rows, width)
        for c in chunks:
            g1_o[c, 0:width] = tn(dpre[:, c], x).astype(BF)
            g1_o[c, width:] = tn(dpre[:, c], ones).astype(BF)

    def grads_2():
        d = d_ref[...].reshape(group * rows, width)
        for c in chunks:
            g2_o[c] = tn(act[:, c], d).astype(BF)

    send_core(rs_in, part_in)
    for m in range(group - 2, 0, -2):
        part_in(m)
        last_link(rs_in, m)
    part_in(0)
    send_core(rs_out, part_out)
    for m in range(group - 2, -1, -2):
        part_out(m)
    for i in range(links - 1, 0, -1):
        next_link(rs_in, i)
    for m in range(group - 2, 0, -2):
        last_link(rs_out, m)
    grads_1()
    finish(rs_in, din_o)
    grads_2()
    for i in range(links - 1, 0, -1):
        next_link(rs_out, i)
    finish(rs_out, out_o)
    gather.wait_sent()
    rs_in.wait_sent()
    rs_out.wait_sent()


def run_middle(dims, x, d_all, w1, w2):
    group, count, rows_s, width = dims
    rows, hid = x.shape[0], w1.shape[0]
    vm = pl.BlockSpec(memory_space=pltpu.VMEM)
    sd = jax.ShapeDtypeStruct
    dma = pltpu.SemaphoreType.DMA
    blocks = pltpu.VMEM((group, rows, width), BF)
    return pl.pallas_call(
        functools.partial(middle_kernel, dims),
        out_shape=(
            sd((rows, width), F32), sd((rows, width), F32), sd(w1.shape, BF), sd(w2.shape, BF),
        ),
        in_specs=[vm] * 4,
        out_specs=tuple([vm] * 4),
        scratch_shapes=[
            blocks, pltpu.VMEM((group * rows, hid), BF), pltpu.VMEM((group * rows, hid), BF), blocks, blocks,
            blocks, blocks,
            dma((2, group)), dma((2, group)), dma((2, group)), dma((2, group)), dma((2, group)), dma((2, group)),
        ],
        compiler_params=pltpu.CompilerParams(collective_id=2, has_side_effects=True, vmem_limit_bytes=58 * MIB),
        name="feed_forward",
    )(x, d_all, w1, w2)


def last_kernel(
    dims, lat, real_ref, kept_ref, tok_ref, cot_in_ref, attn_in_ref, q_ref, k_ref, v_ref, merged_ref,
    attn_out_ref, hidden_ref, cot_ref, mod_ref, d_in_ref, mlp_out_ref, redb_ref, cond_ref,
    full_ref, g1_ref, g2_ref,
    out_o, dtok_o, ga_o, gm1_o, gm2_o, small_o,
    wbuf, gbuf, abox, ar, gm1, gm2, mr1, mr2, back_b, d3, d_attn, dm, dain, sm_send, sm_recv, dmod,
    loc, ra_ss, ra_rs, za_ss, za_rs, zm_ss, zm_rs, gm_ss, gm_rs, ga_ss, ga_rs, sz_ss, sz_rs, sp_ss, sp_rs,
):
    group, count, rows_s, width = dims
    b, z = lax.axis_index("batch"), lax.axis_index("tp")
    g = b % group
    ds = width // count
    slots = kept_ref.shape[1]
    scale = HEAD_SIZE**-0.5
    loads = [
        pltpu.make_async_copy(g1_ref, gm1, loc.at[0]),
        pltpu.make_async_copy(g2_ref, gm2, loc.at[1]),
        pltpu.make_async_copy(full_ref.at[3], wbuf.at[0], loc.at[2]),
        pltpu.make_async_copy(full_ref.at[0], wbuf.at[1], loc.at[3]),
    ]
    for cp in loads:
        cp.start()
    barrier(b, z, group, count)
    cut = (rows_s // 2 + 15) // 16 * 16
    parts = ((0, cut), (cut, rows_s - cut))

    loads[0].wait()
    loads[1].wait()

    def line_m(d):
        peer = lax.rem(z + d, count)
        at = pl.ds(pl.multiple_of(peer * rows_s, 16), rows_s)
        return [
            pltpu.make_async_remote_copy(
                src_ref=src.at[at], dst_ref=dst.at[d], send_sem=zm_ss.at[i, d], recv_sem=zm_rs.at[i, d],
                device_id=(b, peer), device_id_type=MESH,
            )
            for i, (src, dst) in enumerate(((gm1, mr1), (gm2, mr2)))
        ]

    for d in range(1, count):
        for cp in line_m(d):
            cp.start()

    def rows_of(l):
        return slice(l * slots, (l + 1) * slots)

    def back(n, inv, grad):
        return (grad - jnp.mean(grad, axis=-1, keepdims=True) - n * jnp.mean(grad * n, axis=-1, keepdims=True)) * inv

    def total(rows):
        return jnp.sum(rows, axis=0, keepdims=True)

    valid = []
    for l in range(lat):
        at = rows_of(l)
        one = slice(l, l + 1)
        row = lax.broadcasted_iota(jnp.int32, (slots, 1), 0)
        valid.append(jnp.where(row < real_ref[z * lat + l], 1.0, 0.0))
        center, inv = stats(hidden_ref[at])
        n = center * inv
        d_in = d_in_ref[at]
        cot = cot_ref[at].astype(F32)
        back_b[at] = back(n, inv, d_in * (1.0 + mod_ref[4, one]))
        d_hidden = cot + back_b[at]
        d_attn[at] = (mod_ref[2, one] * d_hidden).astype(BF)
        dmod[3, one] = total(d_in)
        dmod[4, one] = total(d_in * n)
        dmod[2, one] = total(d_hidden * attn_out_ref[at])
        mlp_out = mlp_out_ref[at] + redb_ref[...].astype(F32)
        dmod[5, one] = total(cot * mlp_out)

    loads[2].wait()
    dm[...] = nt(d_attn[...], wbuf[0]).astype(BF)
    load_k = pltpu.make_async_copy(full_ref.at[1], wbuf.at[0], loc.at[2])
    load_k.start()
    chunk = 384

    def weight_grad(j, left, right):
        for c in range(0, width, chunk):
            to = slice(c, c + chunk)
            gbuf[j, to] = tn(left(to), right).astype(BF)

    weight_grad(3, lambda to: merged_ref[:, to], d_attn[...])

    heads = width // HEAD_SIZE

    def some_heads(step, _):
        for h in (step, step + heads // 2):
            win, own = head_window(h, width)
            for l in range(lat):
                at = pl.ds(l * slots, slots)
                q, k, v, dmh = q_ref[at, win], k_ref[at, win], v_ref[at, win], dm[at, win]
                s = nt((q.astype(F32) * own).astype(BF), k) * scale
                key = lax.broadcasted_iota(jnp.int32, (1, slots), 1)
                s = jnp.where(key < real_ref[z * lat + l], s, -1000000000.0)
                w = jnp.exp(s - jnp.max(s, axis=-1, keepdims=True))
                pr = w / jnp.sum(w, axis=-1, keepdims=True)
                dp = nt((dmh.astype(F32) * own).astype(BF), v)
                dsc = (pr * (dp - jnp.sum(pr * dp, axis=-1, keepdims=True))).astype(BF)
                for j, grad in enumerate(
                    (nn(dsc, k) * scale, tn(dsc, q) * scale, tn(pr.astype(BF), dmh))
                ):
                    d3[j, at, win] = jnp.where(own > 0, grad, d3[j, at, win].astype(F32)).astype(BF)
        return 0

    lax.fori_loop(0, heads // 2, some_heads, 0)

    for j in range(3):
        weight_grad(j, lambda to, j=j: d3[j, :, to], attn_in_ref[...])

    def wave_shard(w):
        return lax.rem(z + 1 + w, count)

    waves = []
    for w in range(count):
        def mine(m, p, w=w):
            at = flip(g, m) * rows_s
            lo, ln = parts[p]
            return gbuf.at[at // ds, pl.ds(pl.multiple_of(ds * wave_shard(w) + at % ds + lo, 16), ln)]

        def box(m, p, w=w):
            lo, ln = parts[p]
            return abox.at[w, m - 1, pl.ds(lo, ln)]

        def add(m, key, p, mine=mine, box=box):
            mine(m, p)[...] = (mine(m, p)[...].astype(F32) + box(key, p)[...].astype(F32)).astype(BF)

        waves.append(
            Scatter(b, z, group, mine, box, lambda m, p, w=w: ra_ss.at[w, p, m], lambda m, p, w=w: ra_rs.at[w, p, m], add)
        )
    links = len(waves[0].orders[0])

    def own_slice(shard):
        at = g * rows_s
        return gbuf.at[at // ds, pl.ds(pl.multiple_of(ds * shard + at % ds, 16), rows_s)]

    def line_a(w):
        return pltpu.make_async_remote_copy(
            src_ref=own_slice(wave_shard(w)), dst_ref=ar.at[w], send_sem=za_ss.at[w], recv_sem=za_rs.at[w],
            device_id=(b, wave_shard(w)), device_id_type=MESH,
        )

    def wave_step(w, st):
        rs = waves[w]
        if 0 <= st < links:
            for p in range(2):
                order = rs.orders[p]
                i = links - st
                for m in span(order[: i - 1]):
                    rs.fold(m ^ order[i - 1], p)
                    rs.send(m ^ order[i - 1], p)
        elif st == links:
            for p in range(2):
                rs.fold(0, p)
            if w < count - 1:
                line_a(w).start()

    for rs in waves:
        for m in range(group - 1, 0, -2):
            for p in range(2):
                rs.send(m, p)

    def wave_round(t):
        for w in range(count):
            wave_step(w, t - w)

    loads[3].wait()
    dain[...] = nn(d3[0], wbuf[1])
    load_v = pltpu.make_async_copy(full_ref.at[2], wbuf.at[1], loc.at[3])
    load_v.start()
    wave_round(0)
    load_k.wait()
    dain[...] += nn(d3[1], wbuf[0])
    load_v.wait()
    dain[...] += nn(d3[2], wbuf[1])
    wave_round(1)

    place = lax.broadcasted_iota(jnp.int32, (slots, tok_ref.shape[1]), 1)

    def put(pick, rows):
        high = rows.astype(BF)
        return tn(pick, high) + tn(pick, (rows - high.astype(F32)).astype(BF))

    for l in range(lat):
        at = rows_of(l)
        one = slice(l, l + 1)
        pick = jnp.where(place == kept_ref[l], 1.0, 0.0).astype(BF)
        center, inv = stats(nn(pick, tok_ref[l]))
        n = center * inv
        d_ai = dain[at]
        dmod[0, one] = total(d_ai)
        dmod[1, one] = total(d_ai * n)
        d_sel = back_b[at] + back(n, inv, d_ai * (1.0 + mod_ref[1, one]))
        dtok_o[l] = (cot_in_ref[l].astype(F32) + put(pick, d_sel)).astype(BF)

    cols = 6 * width // count
    vectors = [
        sum(total((cot_ref[rows_of(l)].astype(F32) * mod_ref[5, l : l + 1]).astype(BF).astype(F32)) for l in range(lat)),
        total(d_attn[...].astype(F32)),
        total(d3[0].astype(F32)),
        total(d3[2].astype(F32)),
    ]
    for t in range(count):
        first = t * cols // width
        for i in range(2):
            sm_send[t, i] = dmod[min(first + i, 5)]
        for i in range(4):
            sm_send[t, 2 + i // 2, i % 2 : i % 2 + 1] = vectors[i]

    def small(d):
        peer = lax.rem(z + d, count)
        return pltpu.make_async_remote_copy(
            src_ref=sm_send.at[peer], dst_ref=sm_recv.at[z], send_sem=sz_ss.at[d], recv_sem=sz_rs.at[d],
            device_id=(b, peer), device_id_type=MESH,
        )

    for d in range(1, count):
        small(d).start()
    small_own = pltpu.make_async_copy(sm_send.at[z], sm_recv.at[z], loc.at[4])
    small_own.start()
    wave_round(2)
    for l in range(lat):
        at = rows_of(l)
        one = slice(l, l + 1)
        pick = jnp.where(place == kept_ref[l], 1.0, 0.0).astype(BF)
        mlp_out = mlp_out_ref[at] + redb_ref[...].astype(F32)
        delta = (mod_ref[2, one] * attn_out_ref[at] + mod_ref[5, one] * mlp_out) * valid[l]
        out_o[l] = (tok_ref[l].astype(F32) + put(pick, delta)).astype(BF)
    for d in range(1, count):
        ref = sm_recv.at[lax.rem(z - d + count, count)]
        pltpu.make_async_remote_copy(
            src_ref=ref, dst_ref=ref, send_sem=sz_ss.at[d], recv_sem=sz_rs.at[d],
            device_id=(b, lax.rem(z + d, count)), device_id_type=MESH,
        ).wait_recv()
    small_own.wait()
    small_o[0] = jnp.zeros(small_o.shape[1:], F32)
    for i in range(2):
        for t in range(count):
            small_o[0, i, lat * t : lat * (t + 1)] = sm_recv[t, i]
    for i in range(2):
        acc = sm_recv[0, 2 + i]
        for t in range(1, count):
            acc = acc + sm_recv[t, 2 + i]
        small_o[0, 2, lat * i : lat * (i + 1)] = acc
    cond = cond_ref[...].astype(F32)
    small_o[0, 3] = (cond / (1.0 + jnp.exp(-cond))).astype(BF).astype(F32)
    sp = Gather(
        b, z, group, lambda m, p, slot: small_o.at[slot], lambda m, p: sp_ss.at[m], lambda m, p: sp_rs.at[m], halves=1
    )
    sp.step(0)
    for t in range(3, count + links):
        wave_round(t)
        if t - 2 < sp.steps():
            sp.step(t - 2)

    def spread(out, ss, rs):
        def region(m, p, slot):
            lo, ln = parts[p]
            return out.at[pl.ds(pl.multiple_of(flip(g, m) * rows_s + lo, 16), ln)]

        return Gather(b, z, group, region, lambda m, p: ss.at[p, m], lambda m, p: rs.at[p, m])

    g_at = pl.ds(pl.multiple_of(g * rows_s, 16), rows_s)
    z_at = pl.ds(pl.multiple_of(z * rows_s, 16), rows_s)
    acc = own_slice(z)[...].astype(F32)
    for w in range(count - 1):
        line_a(w).wait_recv()
        acc = acc + ar[w].astype(F32)
    ga_o[g_at] = acc.astype(BF)
    spread_a = spread(ga_o, ga_ss, ga_rs)
    spread_a.step(0)
    for d in range(1, count):
        for cp in line_m(d):
            cp.wait_recv()
    for own, box, out in ((gm1, mr1, gm1_o), (gm2, mr2, gm2_o)):
        acc = own[z_at].astype(F32)
        for d in range(1, count):
            acc = acc + box[d].astype(F32)
        out[g_at] = acc.astype(BF)
    spread_1 = spread(gm1_o, gm_ss.at[0], gm_rs.at[0])
    spread_2 = spread(gm2_o, gm_ss.at[1], gm_rs.at[1])
    spread_1.step(0)
    spread_2.step(0)
    for i in range(1, spread_a.steps()):
        for item in (spread_a, spread_1, spread_2):
            item.step(i)
    for i in range(max(1, count + links - 2), sp.steps()):
        sp.step(i)
    for item in (sp, spread_a, spread_1, spread_2):
        item.wait_core()
        item.wait_sent()
    for rs in waves:
        rs.wait_sent()
    for w in range(count - 1):
        line_a(w).wait_send()
    for d in range(1, count):
        small(d).wait_send()
        for cp in line_m(d):
            cp.wait_send()


def run_last(dims, lat, real, kept, tok, cot_in, attn_in, q, k, v, merged, attn_out, hidden, cot, mod, d_in, mlp_out, redb, cond, full, g1, g2):
    group, count, rows_s, width = dims
    rows = attn_in.shape[0]
    vm = pl.BlockSpec(memory_space=pltpu.VMEM)
    hb = pl.BlockSpec(memory_space=pl.ANY)
    sm = pl.BlockSpec(memory_space=pltpu.SMEM)
    sd = jax.ShapeDtypeStruct
    dma = pltpu.SemaphoreType.DMA
    ext = g1.shape[1]
    small = (group, 4, cond.shape[0], width)
    return pl.pallas_call(
        functools.partial(last_kernel, dims, lat),
        out_shape=(
            sd(tok.shape, BF), sd(tok.shape, BF), sd((group * rows_s, width), BF),
            sd((group * rows_s, ext), BF), sd((group * rows_s, width), BF), sd(small, F32),
        ),
        in_specs=[sm] + [vm] * 16 + [hb] * 3,
        out_specs=tuple([vm] * 6),
        scratch_shapes=[
            pltpu.VMEM((2, width, width), BF),
            pltpu.VMEM((4, width, width), BF),
            pltpu.VMEM((count, group - 1, rows_s, width), BF),
            pltpu.VMEM((count, rows_s, width), BF),
            pltpu.VMEM(g1.shape, BF), pltpu.VMEM(g2.shape, BF),
            pltpu.VMEM((count, rows_s, ext), BF), pltpu.VMEM((count, rows_s, width), BF),
            pltpu.VMEM((rows, width), F32),
            pltpu.VMEM((3, rows, width), BF),
            pltpu.VMEM((rows, width), BF), pltpu.VMEM((rows, width), BF),
            pltpu.VMEM((rows, width), F32),
            pltpu.VMEM((count, 4, lat, width), F32), pltpu.VMEM((count, 4, lat, width), F32),
            pltpu.VMEM((6, lat, width), F32),
            dma((5,)),
            dma((count, 2, group)), dma((count, 2, group)),
            dma((count,)), dma((count,)),
            dma((2, count)), dma((2, count)),
            dma((2, 2, group)), dma((2, 2, group)),
            dma((2, group)), dma((2, group)),
            dma((count,)), dma((count,)),
            dma((group,)), dma((group,)),
        ],
        compiler_params=pltpu.CompilerParams(collective_id=3, has_side_effects=True, vmem_limit_bytes=63 * MIB),
        name="backward_attention",
    )(real, kept, tok, cot_in, attn_in, q, k, v, merged, attn_out, hidden, cot, mod, d_in, mlp_out, redb, cond, full, g1, g2)


def own_frame(part, total, axis):
    size = part.shape[-1]
    frame = jnp.zeros(part.shape[:-1] + (total,), F32)
    return lax.dynamic_update_slice_in_dim(frame, part.astype(F32), lax.axis_index("tp") * size, frame.ndim - 1)


def body(
    tokens, conditioning, bucket, kept_index, w_ada, ada_bias, w_qkv, qv_bias, w_proj, proj_bias,
    w_expand, expand_bias, w_reduce, reduce_bias, out_grad, count, batch,
):
    lat, positions, width = tokens.shape
    shard_w, shard_f = w_qkv.shape[2], w_expand.shape[1]
    group = group_size(shard_f, shard_w)
    rows_s = shard_f // group
    dims = (group, count, rows_s, width)
    real = (positions - positions // 16 * (bucket > 0).astype(jnp.int32)) // 2
    own_1 = jnp.concatenate(
        [w_expand.T, jnp.pad(expand_bias[:, None], ((0, 0), (0, 127)))], axis=1
    )
    out1 = run_first(
        dims, lat, real, conditioning, w_ada.T, ada_bias[None], tokens, out_grad, kept_index[:, :, None],
        own_frame(qv_bias, width, "tp"), proj_bias[None], jnp.swapaxes(w_qkv, 1, 2), w_proj, own_1, w_reduce,
    )
    (attn_in, queries, key_rows, value_rows, merged, attn_out, hidden, mlp_in, cot, mod, full, all_1, all_2, d_all) = out1
    flat = lambda a: a.reshape((-1,) + a.shape[2:])
    d_in, mlp_out, g1, g2 = run_middle(dims, mlp_in, d_all, flat(all_1), flat(all_2))
    output, tokens_grad, ga, gm1, gm2, small = run_last(
        dims, lat, real, kept_index[:, :, None], tokens, out_grad, attn_in, queries, key_rows, value_rows, merged,
        attn_out, hidden, cot, mod, d_in, mlp_out, reduce_bias[None], conditioning,
        full.reshape(4, width, width), g1, g2,
    )

    cols = 6 * width // count
    start = lax.axis_index("tp") * cols % width
    pair = jnp.concatenate([flat(small[:, 0]), flat(small[:, 1])], axis=1)
    d_mod = lax.dynamic_slice_in_dim(pair, start, cols, 1)
    ada_grad = tn(flat(small[:, 3]).astype(BF), d_mod.astype(BF))
    ada_add_grad = jnp.sum(d_mod, axis=0)
    sums = jnp.sum(small[:, 2, 0:4], axis=0)
    pair_grad = lax.dynamic_slice_in_dim(sums[2:4], lax.axis_index("tp") * shard_w, shard_w, 1)
    grads = (
        ada_grad, ada_add_grad, ga, gm1, gm2, pair_grad, sums[0], sums[1],
    )
    if batch > group:
        grads = tuple(lax.psum(item * (1.0 / group), "batch") for item in grads)
    ada_grad, ada_add_grad, ga, gm1, gm2, pair_grad, reduce_add, proj_add = grads
    ga = ga.reshape(4, shard_w, width)
    return (
        output,
        tokens_grad,
        ada_grad,
        ada_add_grad,
        jnp.swapaxes(ga[:3], 1, 2).astype(F32),
        pair_grad,
        ga[3].astype(F32),
        proj_add,
        gm1[:, :width].T.astype(F32),
        gm1[:, width].astype(F32),
        gm2.astype(F32),
        reduce_add,
    )


def solution(mesh):
    rows = P(("batch", "tp"), None, None)
    return jax.shard_map(
        functools.partial(body, count=mesh.shape["tp"], batch=mesh.shape["batch"]),
        mesh=mesh,
        in_specs=(
            rows, P("batch", None), P("batch"), P(("batch", "tp"), None), P(None, "tp"), P("tp"),
            P(None, None, "tp"), P(None, "tp"), P("tp", None), P(), P(None, "tp"), P("tp"), P("tp", None), P(), rows,
        ),
        out_specs=(
            rows, rows, P(None, "tp"), P("tp"), P(None, None, "tp"), P(None, "tp"), P("tp", None), P(),
            P(None, "tp"), P("tp"), P("tp", None), P(),
        ),
        check_vma=False,
    )
```

```python
import functools
import jax
import jax.numpy as jnp
from jax import lax
from jax.experimental import pallas as pl
from jax.experimental.pallas import tpu as pltpu
from jax.sharding import PartitionSpec as P

HEAD_SIZE = 72
EPS = 1e-06
F32 = jnp.float32
BF = jnp.bfloat16
MESH = pl.DeviceIdType.MESH
MIB = 2**20


def nn(a, b):
    return lax.dot_general(a, b, (((1,), (0,)), ((), ())), preferred_element_type=F32)


def nt(a, b):
    return lax.dot_general(a, b, (((1,), (1,)), ((), ())), preferred_element_type=F32)


def tn(a, b):
    return lax.dot_general(a, b, (((0,), (0,)), ((), ())), preferred_element_type=F32)


def flip(b, mask):
    out, bit = b, 1
    while bit <= mask:
        if mask & bit:
            out = out + bit - 2 * bit * ((b // bit) % 2)
        bit *= 2
    return out


def group_size(ff_shard, width_shard):
    for size in (8, 4, 2):
        rows = ff_shard // size
        if ff_shard % size == 0 and rows % 16 == 0 and 4 * width_shard == size * rows:
            return size
    raise ValueError("no group")


def link_orders(group):
    bits = []
    bit = 2
    while bit < group:
        bits.append(bit)
        bit *= 2
    return bits, bits[::-1]


def span(bits):
    out = [0]
    for bit in bits:
        out = out + [item ^ bit for item in out]
    return out


def near_shard(z, k, count):
    low = jnp.minimum(z, count - 1 - z)
    both = z + (k // 2 + 1) * (1 - 2 * (k % 2))
    one = z + jnp.where(2 * z < count - 1, 1, -1) * (k - low + 1)
    return jnp.where(k < 2 * low, both, one)


class Gather:
    def __init__(self, b, z, group, region, send_sem, recv_sem, halves=2):
        self.b, self.z = b, z
        self.region, self.send_sem, self.recv_sem = region, send_sem, recv_sem
        self.orders = link_orders(group)[:halves] if halves == 2 else link_orders(group)[:1]
        self.group = group
        self.sent = []

    def copy(self, m, bit, p):
        return pltpu.make_async_remote_copy(
            src_ref=self.region(m, p, m),
            dst_ref=self.region(m, p, m ^ bit),
            send_sem=self.send_sem(m ^ bit, p),
            recv_sem=self.recv_sem(m ^ bit, p),
            device_id=(flip(self.b, bit), self.z),
            device_id_type=MESH,
        )

    def send(self, m, bit, p):
        cp = self.copy(m, bit, p)
        cp.start()
        self.sent.append(cp)

    def wait(self, m, p):
        ref = self.region(m, p, m)
        pltpu.make_async_remote_copy(
            src_ref=ref, dst_ref=ref, send_sem=self.send_sem(m, p), recv_sem=self.recv_sem(m, p),
            device_id=(flip(self.b, 1), self.z), device_id_type=MESH,
        ).wait_recv()

    def step(self, i):
        for p, order in enumerate(self.orders):
            if i == 0:
                fresh = [0]
            elif i <= len(order):
                fresh = [item ^ order[i - 1] for item in span(order[: i - 1])]
                for m in fresh:
                    self.wait(m, p)
            else:
                continue
            if i < len(order):
                for m in span(order[:i]):
                    self.send(m, order[i], p)
            for m in fresh:
                self.send(m, 1, p)

    def steps(self):
        return len(self.orders[0]) + 1

    def wait_core(self, m=None):
        for p in range(len(self.orders)):
            for item in range(1, self.group, 2):
                if m is None or item == m:
                    self.wait(item, p)

    def wait_sent(self):
        for cp in self.sent:
            cp.wait_send()


class Scatter:
    def __init__(self, b, z, group, mine, inbox, send_sem, recv_sem, add):
        self.b, self.z, self.group = b, z, group
        self.mine, self.inbox, self.add = mine, inbox, add
        self.send_sem, self.recv_sem = send_sem, recv_sem
        self.orders = link_orders(group)
        self.sent = []

    def top(self, m, p):
        if m & 1:
            return 1
        for bit in reversed(self.orders[p]):
            if m & bit:
                return bit

    def copy(self, m, p):
        return pltpu.make_async_remote_copy(
            src_ref=self.mine(m, p),
            dst_ref=self.inbox(m, p),
            send_sem=self.send_sem(m, p),
            recv_sem=self.recv_sem(m, p),
            device_id=(flip(self.b, self.top(m, p)), self.z),
            device_id_type=MESH,
        )

    def keys(self, m, p):
        if m & 1:
            return []
        out = [m ^ 1]
        order = self.orders[p]
        above = order if m == 0 else order[order.index(self.top(m, p)) + 1 :]
        return out + [m ^ bit for bit in reversed(above)]

    def fold(self, m, p):
        for key in self.keys(m, p):
            self.copy(key, p).wait_recv()
            self.add(m, key, p)

    def send(self, m, p):
        cp = self.copy(m, p)
        cp.start()
        self.sent.append(cp)

    def wait_sent(self):
        for cp in self.sent:
            cp.wait_send()


def barrier(b, z, group, count):
    sem = pltpu.get_barrier_semaphore()
    for m in range(1, group):
        pl.semaphore_signal(sem, 1, device_id=(flip(b, m), z), device_id_type=MESH)
    for d in range(1, count):
        pl.semaphore_signal(sem, 1, device_id=(b, lax.rem(z + d, count)), device_id_type=MESH)
    pl.semaphore_wait(sem, group - 1 + count - 1)


def stats(rows):
    center = rows - jnp.mean(rows, axis=-1, keepdims=True)
    return center, lax.rsqrt(jnp.mean(center * center, axis=-1, keepdims=True) + EPS)


def head_window(h, width):
    start = jnp.minimum(h * HEAD_SIZE // 128, width // 128 - 2) * 128
    lane = lax.broadcasted_iota(jnp.int32, (1, 256), 1) + (start - h * HEAD_SIZE)
    own = jnp.where((lane >= 0) & (lane < HEAD_SIZE), 1.0, 0.0)
    return pl.ds(pl.multiple_of(start, 128), 256), own


def kept_half(bucket, positions):
    return jnp.where(bucket > 0, (positions - positions // 16) // 2, positions // 2)


def row_mask(count, slots):
    return jnp.where(lax.broadcasted_iota(jnp.int32, (slots, 1), 0) < count, 1.0, 0.0)


def placing(kept_row, positions):
    place = lax.broadcasted_iota(jnp.int32, (positions, kept_row.shape[1]), 0)
    return jnp.where(place == kept_row, 1.0, 0.0).astype(BF)


GELU_C = 0.7978845608028654


def gelu_pair(v):
    sq = v * v
    t = jnp.tanh(GELU_C * v * (1.0 + 0.044715 * sq))
    half = 0.5 + 0.5 * t
    slope = half + 0.5 * GELU_C * v * (1.0 - t * t) * (1.0 + 3 * 0.044715 * sq)
    return v * half, slope


class Steps:
    def __init__(self, rs):
        self.rs = rs
        self.links = len(rs.orders[0])

    def send_core(self, make=None):
        for m in range(self.rs.group - 1, 0, -2):
            if make is not None:
                make(m)
            for p in range(2):
                self.rs.send(m, p)

    def last_link(self, m):
        for p in range(2):
            if self.rs.top(m, p) == self.rs.orders[p][-1]:
                self.rs.fold(m, p)
                self.rs.send(m, p)

    def link(self, i):
        for p in range(2):
            order = self.rs.orders[p]
            for m in span(order[: i - 1]):
                self.rs.fold(m ^ order[i - 1], p)
                self.rs.send(m ^ order[i - 1], p)

    def finish(self, out, half):
        for p in range(2):
            total = self.rs.mine(0, p)[...].astype(F32)
            for key in self.rs.keys(0, p):
                self.rs.copy(key, p).wait_recv()
                total = total + self.rs.inbox(key, p)[...].astype(F32)
            out[p * half : (p + 1) * half] = total


def forward_kernel(
    dims, lat, bucket_ref, cond_ref, tok_ref, cot_in_ref, kept_ref, vec_ref,
    wada_hbm, own_qkv, own_proj, own_1, own_2,
    attn_in_o, q_o, k_o, v_o, merged_o, attn_out_o, hidden_o, cot_o, mod_o, din_o, zp_o, g1_o, g2_o, full_o,
    full, sm_send, sm_recv, nrm, sel, mg, mod8, all_1, all_2, d_all, xb, act, dpre, y, inbox, bcol,
    sm_ss, sm_rs, za_ss, za_rs, zm_ss, zm_rs, ga_ss, ga_rs, gd_ss, gd_rs, ag_ss, ag_rs, rs_ss, rs_rs, loc,
):
    group, count, rows_s, width = dims
    b, z = lax.axis_index("batch"), lax.axis_index("tp")
    g = b % group
    ds = width // count
    slots = kept_ref.shape[1]
    positions = tok_ref.shape[1]
    rows = lat * slots
    half = rows // 2
    cols = wada_hbm.shape[0]
    load_ada = pltpu.make_async_copy(wada_hbm, y.at[0:cols], loc.at[1])
    load_ada.start()
    real = [kept_half(bucket_ref[z * lat + l], positions) for l in range(lat)]
    barrier(b, z, group, count)

    cut = (rows_s // 2 + 15) // 16 * 16
    parts = ((0, cut), (cut, rows_s - cut))

    def piece(member, shard, p):
        at = member * rows_s
        lo, ln = parts[p] if p is not None else (0, rows_s)
        return full.at[at // ds, shard, pl.ds(at % ds + lo, ln)]

    own_copy = [
        pltpu.make_async_copy(own_qkv, full.at[0:3, z], loc.at[0]),
        pltpu.make_async_copy(own_proj, full.at[3, z], loc.at[5]),
    ]
    for cp in own_copy:
        cp.start()

    def line_a(shard, src, step, k):
        return pltpu.make_async_remote_copy(
            src_ref=src, dst_ref=piece(g, shard, None), send_sem=za_ss.at[k], recv_sem=za_rs.at[shard],
            device_id=(b, z + step), device_id_type=MESH,
        )

    def line_m(shard, src1, src2, step, k):
        return [
            pltpu.make_async_remote_copy(
                src_ref=src, dst_ref=dst.at[shard], send_sem=zm_ss.at[i, k], recv_sem=zm_rs.at[i, shard],
                device_id=(b, z + step), device_id_type=MESH,
            )
            for i, (src, dst) in enumerate(((src1, all_1), (src2, all_2)))
        ]

    slice_at = pl.ds(pl.multiple_of(g * rows_s, 16), rows_s)
    own_m = [
        pltpu.make_async_copy(own_1.at[slice_at], all_1.at[z, :, 0:width], loc.at[2]),
        pltpu.make_async_copy(own_2.at[slice_at], all_2.at[z], loc.at[3]),
    ]
    for cp in own_m:
        cp.start()

    def both_ways(fn):
        @pl.when(z < count - 1)
        def _():
            fn(1, 0)

        @pl.when(z > 0)
        def _():
            fn(-1, 1)

    for cp in own_copy:
        cp.wait()
    both_ways(lambda step, k: line_a(z, piece(g, z, None), step, k).start())

    cond = cond_ref[...].astype(F32)
    silu = (cond / (1.0 + jnp.exp(-cond))).astype(BF)
    mod8[...] = jnp.concatenate([vec_ref[4:5], vec_ref[5:6]], axis=1) + jnp.zeros_like(mod8)
    load_ada.wait()
    mod8[:, 0:cols] += nt(silu, y[0:cols])
    framed = pltpu.roll(mod8[...], (z * cols) % width, 1)
    for t in range(count):
        for i in range(2):
            sm_send[t, i] = framed[lat * t : lat * (t + 1), i * width : (i + 1) * width]
        sm_send[t, 2] = vec_ref[2:4]

    def small(d):
        peer = lax.rem(z + d, count)
        return pltpu.make_async_remote_copy(
            src_ref=sm_send.at[peer], dst_ref=sm_recv.at[z], send_sem=sm_ss.at[d], recv_sem=sm_rs.at[d],
            device_id=(b, peer), device_id_type=MESH,
        )

    for d in range(1, count):
        small(d).start()
    small_own = pltpu.make_async_copy(sm_send.at[z], sm_recv.at[z], loc.at[6])
    small_own.start()

    for l in range(lat):
        pick = placing(kept_ref[l : l + 1], positions)
        at = slice(l * slots, (l + 1) * slots)
        picked = tn(pick, tok_ref[l])
        sel[at] = picked
        center, inv = stats(picked)
        nrm[at] = center * inv
        cot_o[at] = (tn(pick, cot_in_ref[l]) * row_mask(real[l], slots)).astype(BF)

    hid_s = own_1.shape[0]
    first_row = lax.broadcasted_iota(jnp.int32, (8, 1), 0) == 0
    corner = jnp.where(first_row & (lax.broadcasted_iota(jnp.int32, (1, 128), 1) == 0), 1.0, 0.0)
    bias_row = jnp.where(first_row, vec_ref[6:7, 0:hid_s], 0.0)
    bcol[...] = tn(bias_row.astype(BF), corner.astype(BF)).astype(BF)
    all_1[z, :, width:] = bcol[slice_at]

    gathers = []
    for k in range(count - 1):
        shard = near_shard(z, k, count)

        def region(m, p, slot, shard=shard):
            return piece(flip(g, m), shard, p)

        gathers.append(
            Gather(b, z, group, region, lambda m, p, k=k: ga_ss.at[k, p, m], lambda m, p, shard=shard: ga_rs.at[shard, p, m])
        )

    def arrive_a(k):
        shard = near_shard(z, k, count)
        ref = piece(g, shard, None)
        line_a(shard, ref, 0, 2 + k).wait_recv()
        gathers[k].step(0)

        @pl.when((shard < z) & (z < count - 1))
        def _():
            line_a(shard, ref, 1, 2 + k).start()

        @pl.when((shard > z) & (z > 0))
        def _():
            line_a(shard, ref, -1, 2 + k).start()

    def arrive_m(k):
        shard = near_shard(z, k, count)
        r1, r2 = all_1.at[shard], all_2.at[shard]
        for cp in line_m(shard, r1, r2, 0, 2 + k):
            cp.wait_recv()

        @pl.when((shard < z) & (z < count - 1))
        def _():
            for cp in line_m(shard, r1, r2, 1, 2 + k):
                cp.start()

        @pl.when((shard > z) & (z > 0))
        def _():
            for cp in line_m(shard, r1, r2, -1, 2 + k):
                cp.start()

    def send_m(step, k):
        for cp in line_m(z, all_1.at[z], all_2.at[z], step, k):
            cp.start()

    arrive_a(0)
    for cp in own_m:
        cp.wait()

    for d in range(1, count):
        peer = lax.rem(z + d, count)
        ref = sm_recv.at[lax.rem(z - d + count, count)]
        pltpu.make_async_remote_copy(
            src_ref=ref, dst_ref=ref, send_sem=sm_ss.at[d], recv_sem=sm_rs.at[d], device_id=(b, peer),
            device_id_type=MESH,
        ).wait_recv()
    small_own.wait()
    blocks = [None] * 6
    for t in range(count):
        first = t * cols // width
        for i in range(2):
            if first + i < 6:
                part = sm_recv[t, i]
                blocks[first + i] = part if blocks[first + i] is None else blocks[first + i] + part
    for i in range(6):
        mod_o[i] = blocks[i]
    qv_bias = sm_recv[0, 2]
    for t in range(1, count):
        qv_bias = qv_bias + sm_recv[t, 2]
    for l in range(lat):
        at = slice(l * slots, (l + 1) * slots)
        attn_in_o[at] = (nrm[at] * (1.0 + mod_o[1, l : l + 1]) + mod_o[0, l : l + 1]).astype(BF)
        d_all[0, at] = (cot_o[at].astype(F32) * mod_o[5, l : l + 1]).astype(BF)

    for k in range(1, count - 1):
        arrive_a(k)
        if k == 1:
            both_ways(send_m)
        gathers[k - 1].step(1)
    depth = gathers[0].steps()
    todo = [(i, k) for k in range(count - 1) for i in range(1, depth) if not (i == 1 and k < count - 2)]
    def dm_region(m, p, slot):
        return d_all.at[slot, pl.ds(p * half, half)]

    dm = Gather(b, z, group, dm_region, lambda m, p: gd_ss.at[p, m], lambda m, p: gd_rs.at[p, m])
    links = depth - 1
    todo.sort(key=lambda item: (item[0] >= links, item[0] + item[1], item[1]))
    started = False
    for i, k in todo:
        if i >= links and not started:
            dm.step(0)
            arrive_m(0)
            started = True
        gathers[k].step(i)
    for k in range(count - 1):
        gathers[k].wait_core()
    full_out = pltpu.make_async_copy(full, full_o, loc.at[4])
    full_out.start()

    for k in range(1, count - 2):
        arrive_m(k)
    dm.step(1)

    x = attn_in_o[...]
    for j, out in enumerate((q_o, k_o, v_o)):
        part_j = nt(x, full[j].reshape(width, width))
        if j != 1:
            part_j = part_j + qv_bias[j // 2 : j // 2 + 1]
        out[...] = part_j.astype(BF)

    scale = HEAD_SIZE**-0.5

    heads = width // HEAD_SIZE

    def some_heads(step, _):
        for h in (step, step + heads // 2):
            win, own = head_window(h, width)
            for l in range(lat):
                at = pl.ds(l * slots, slots)
                q = (q_o[at, win].astype(F32) * own).astype(BF)
                s = nt(q, k_o[at, win]) * scale
                key = lax.broadcasted_iota(jnp.int32, (1, slots), 1)
                s = jnp.where(key < real[l], s, -1000000000.0)
                w = jnp.exp(s - jnp.max(s, axis=-1, keepdims=True))
                pr = (w / jnp.sum(w, axis=-1, keepdims=True)).astype(BF)
                o = nn(pr, v_o[at, win])
                mg[at, win] = jnp.where(own > 0, o, mg[at, win])
        return 0

    lax.fori_loop(0, heads // 2, some_heads, 0)
    for i in range(2, dm.steps()):
        dm.step(i)
    merged_o[...] = mg[...].astype(BF)
    a_out = nn(merged_o[...], full[3].reshape(width, width)) + vec_ref[0:1]
    attn_out_o[...] = a_out
    for l in range(lat):
        at = slice(l * slots, (l + 1) * slots)
        mixed = sel[at] + mod_o[2, l : l + 1] * attn_out_o[at]
        hidden_o[at] = mixed
        center, inv = stats(mixed)
        xb[0, at] = (center * inv * (1.0 + mod_o[4, l : l + 1]) + mod_o[3, l : l + 1]).astype(BF)

    def part(ref):
        return lambda m, p: ref.at[m, pl.ds(p * half, half)]

    gather = Gather(
        b, z, group, lambda m, p, slot: part(xb)(slot, p), lambda m, p: ag_ss.at[p, m], lambda m, p: ag_rs.at[p, m]
    )
    gather.step(0)
    arrive_m(count - 2)
    hid = count * rows_s
    bias = nt(jnp.ones((8, all_1.shape[2] - width), BF), all_1[:, :, width:].reshape(hid, all_1.shape[2] - width))[0:1]

    def forward(pair):
        (m0, p0), (m1, p1) = pair
        at = [(m0, slice(p0 * half, (p0 + 1) * half)), (m1, slice(p1 * half, (p1 + 1) * half))]
        x = jnp.concatenate([xb[m, s] for m, s in at], axis=0)
        d = jnp.concatenate([d_all[m, s] for m, s in at], axis=0)
        a, slope = gelu_pair(nt(x, all_1[:, :, 0:width].reshape(hid, width)) + bias)
        dp = (slope * nt(d, all_2[...].reshape(hid, width))).astype(BF)
        a = a.astype(BF)
        for i, (m, s) in enumerate(at):
            to = slice(m * rows + s.start, m * rows + s.stop)
            act[to] = a[i * half : (i + 1) * half]
            dpre[to] = dp[i * half : (i + 1) * half]

    forward(((0, 0), (0, 1)))
    for p in range(2):
        gather.wait(1, p)
        dm.wait(1, p)
    forward(((1, 0), (1, 1)))
    for i in range(1, gather.steps()):
        gather.step(i)
        fresh = [[m ^ order[i - 1] for m in span(order[: i - 1])] for order in gather.orders]
        for m0, m1 in zip(*fresh):
            forward(((m0, 0), (m1, 1)))
        for m0, m1 in zip(*fresh):
            for item in (gather, dm):
                item.wait(m0 ^ 1, 0)
                item.wait(m1 ^ 1, 1)
            forward(((m0 ^ 1, 0), (m1 ^ 1, 1)))

    mine = lambda m, p: y.at[pl.ds(m * rows + p * half, half)]
    arrived = lambda m, p: inbox.at[m - 1, pl.ds(p * half, half)]

    def add(m, key, p):
        mine(m, p)[...] = (mine(m, p)[...].astype(F32) + arrived(key, p)[...].astype(F32)).astype(BF)

    rs = Steps(Scatter(b, z, group, mine, arrived, lambda m, p: rs_ss.at[p, m], lambda m, p: rs_rs.at[p, m], add))

    def part_in(m):
        at = slice(m * rows, (m + 1) * rows)
        y[at] = nn(dpre[at], all_1[:, :, 0:width].reshape(hid, width)).astype(BF)

    chunks = [slice(c, min(c + 128, hid)) for c in range(0, hid, 128)]
    rs.send_core(part_in)
    for m in range(group - 2, 0, -2):
        part_in(m)
        rs.last_link(m)
    part_in(0)
    ones = jnp.ones((group * rows, g1_o.shape[1] - width), BF)
    for c in chunks:
        g1_o[c, 0:width] = tn(dpre[:, c], xb[...].reshape(group * rows, width)).astype(BF)
        g1_o[c, width:] = tn(dpre[:, c], ones).astype(BF)
    for i in range(rs.links - 1, 0, -1):
        rs.link(i)
    for c in chunks:
        g2_o[c] = tn(act[:, c], d_all[...].reshape(group * rows, width)).astype(BF)
    for m in range(group):
        zp_o[m] = nn(act[m * rows : (m + 1) * rows], all_2[...].reshape(hid, width)).astype(BF)
    rs.finish(din_o, half)
    gather.wait_sent()
    rs.rs.wait_sent()

    for d in range(1, count):
        small(d).wait_send()
    both_ways(lambda step, k: line_a(z, piece(g, z, None), step, k).wait_send())

    def sent_m(step, k):
        for cp in line_m(z, all_1.at[z], all_2.at[z], step, k):
            cp.wait_send()

    both_ways(sent_m)
    for k in range(count - 1):
        shard = near_shard(z, k, count)

        @pl.when(((shard < z) & (z < count - 1)) | ((shard > z) & (z > 0)))
        def _():
            line_a(shard, piece(g, shard, None), 0, 2 + k).wait_send()
            for cp in line_m(shard, all_1.at[shard], all_2.at[shard], 0, 2 + k):
                cp.wait_send()

        gathers[k].wait_sent()
    dm.wait_sent()
    full_out.wait()


def run_forward(dims, lat, bucket, cond, tok, cot, kept, vec, wada, own_qkv, own_proj, own_1, own_2):
    group, count, rows_s, width = dims
    slots = kept.shape[1]
    rows = lat * slots
    hid = count * rows_s
    ext = width + 128
    vm = pl.BlockSpec(memory_space=pltpu.VMEM)
    hb = pl.BlockSpec(memory_space=pl.ANY)
    sm = pl.BlockSpec(memory_space=pltpu.SMEM)
    sd = jax.ShapeDtypeStruct
    row_bf, row_f = sd((rows, width), BF), sd((rows, width), F32)
    blocks = sd((group, rows, width), BF)
    dma = pltpu.SemaphoreType.DMA
    vmem = pltpu.VMEM
    return pl.pallas_call(
        functools.partial(forward_kernel, dims, lat),
        out_shape=(
            row_bf, row_bf, row_bf, row_bf, row_bf, row_f, row_f, row_bf, sd((6, lat, width), F32),
            row_f, blocks, sd((hid, ext), BF), sd((hid, width), BF), sd((4, count, width // count, width), BF),
        ),
        in_specs=[sm] + [vm] * 5 + [hb] * 5,
        out_specs=tuple([vm] * 13 + [hb]),
        scratch_shapes=[
            vmem((4, count, width // count, width), BF),
            vmem((count, 3, lat, width), F32), vmem((count, 3, lat, width), F32),
            vmem((rows, width), F32), vmem((rows, width), F32), vmem((rows, width), F32),
            vmem((cond.shape[0], 2 * width), F32),
            vmem((count, rows_s, ext), BF), vmem((count, rows_s, width), BF),
            vmem((group, rows, width), BF), vmem((group, rows, width), BF),
            vmem((group * rows, hid), BF), vmem((group * rows, hid), BF),
            vmem((group * rows, width), BF), vmem((group - 1, rows, width), BF),
            vmem((own_1.shape[0], 128), BF),
            dma((count,)), dma((count,)),
            dma((count + 1,)), dma((count,)),
            dma((2, count + 1)), dma((2, count)),
            dma((count - 1, 2, group)), dma((count, 2, group)),
            dma((2, group)), dma((2, group)), dma((2, group)), dma((2, group)), dma((2, group)), dma((2, group)),
            dma((7,)),
        ],
        compiler_params=pltpu.CompilerParams(collective_id=1, has_side_effects=True, vmem_limit_bytes=63 * MIB),
        name="forward_attention",
    )(bucket, cond, tok, cot, kept, vec, wada, own_qkv, own_proj, own_1, own_2)


def backward_kernel(
    dims, lat, bucket_ref, kept_ref, tok_ref, cot_in_ref, attn_in_ref, q_ref, k_ref, v_ref, merged_ref,
    attn_out_ref, hidden_ref, cot_ref, mod_ref, d_in_ref, vec_ref, cond_ref,
    full_ref, g1_ref, g2_ref, zp_ref,
    out_o, dtok_o, ga_o, gm1_o, gm2_o, small_o,
    wbuf, gbuf, abox, ar, gm1, gm2, mr1, mr2, back_b, d3, d_attn, dm, dain, mlp, inbox, sm_send, sm_recv, dmod,
    loc, ro_ss, ro_rs, ra_ss, ra_rs, za_ss, za_rs, zm_ss, zm_rs, gm_ss, gm_rs, ga_ss, ga_rs, sz_ss, sz_rs, sp_ss, sp_rs,
):
    group, count, rows_s, width = dims
    b, z = lax.axis_index("batch"), lax.axis_index("tp")
    g = b % group
    ds = width // count
    slots = kept_ref.shape[1]
    positions = tok_ref.shape[1]
    rows = lat * slots
    half = rows // 2
    scale = HEAD_SIZE**-0.5
    loads = [
        pltpu.make_async_copy(g1_ref, gm1, loc.at[0]),
        pltpu.make_async_copy(g2_ref, gm2, loc.at[1]),
        pltpu.make_async_copy(full_ref.at[3], wbuf.at[0], loc.at[2]),
        pltpu.make_async_copy(full_ref.at[0], wbuf.at[1], loc.at[3]),
        pltpu.make_async_copy(zp_ref, gbuf.at[0 : group * rows], loc.at[5]),
    ]
    for cp in loads:
        cp.start()
    real = [kept_half(bucket_ref[z * lat + l], positions) for l in range(lat)]
    barrier(b, z, group, count)

    mine_out = lambda m, p: gbuf.at[pl.ds(m * rows + p * half, half)]
    box_out = lambda m, p: inbox.at[m - 1, pl.ds(p * half, half)]

    def add_out(m, key, p):
        mine_out(m, p)[...] = (mine_out(m, p)[...].astype(F32) + box_out(key, p)[...].astype(F32)).astype(BF)

    rs_out = Steps(
        Scatter(b, z, group, mine_out, box_out, lambda m, p: ro_ss.at[p, m], lambda m, p: ro_rs.at[p, m], add_out)
    )
    loads[4].wait()
    rs_out.send_core()
    cut = (rows_s // 2 + 15) // 16 * 16
    parts = ((0, cut), (cut, rows_s - cut))

    loads[0].wait()
    loads[1].wait()

    def line_m(d):
        peer = lax.rem(z + d, count)
        at = pl.ds(pl.multiple_of(peer * rows_s, 16), rows_s)
        return [
            pltpu.make_async_remote_copy(
                src_ref=src.at[at], dst_ref=dst.at[d - 1], send_sem=zm_ss.at[i, d], recv_sem=zm_rs.at[i, d],
                device_id=(b, peer), device_id_type=MESH,
            )
            for i, (src, dst) in enumerate(((gm1, mr1), (gm2, mr2)))
        ]

    for d in range(1, count):
        for cp in line_m(d):
            cp.start()

    def rows_of(l):
        return slice(l * slots, (l + 1) * slots)

    def back(n, inv, grad):
        return (grad - jnp.mean(grad, axis=-1, keepdims=True) - n * jnp.mean(grad * n, axis=-1, keepdims=True)) * inv

    def total(rows):
        return jnp.sum(rows, axis=0, keepdims=True)

    for m in range(group - 2, 0, -2):
        rs_out.last_link(m)
    for l in range(lat):
        at = rows_of(l)
        one = slice(l, l + 1)
        center, inv = stats(hidden_ref[at])
        n = center * inv
        d_in = d_in_ref[at]
        cot = cot_ref[at].astype(F32)
        back_b[at] = back(n, inv, d_in * (1.0 + mod_ref[4, one]))
        d_hidden = cot + back_b[at]
        d_attn[at] = (mod_ref[2, one] * d_hidden).astype(BF)
        dmod[3, one] = total(d_in)
        dmod[4, one] = total(d_in * n)
        dmod[2, one] = total(d_hidden * attn_out_ref[at])

    loads[2].wait()
    dm[...] = nt(d_attn[...], wbuf[0]).astype(BF)
    load_k = pltpu.make_async_copy(full_ref.at[1], wbuf.at[0], loc.at[2])
    load_k.start()
    chunk = 384

    def weight_grad(j, left, right):
        for c in range(0, width, chunk):
            to = slice(c, c + chunk)
            gbuf[j * width + c : j * width + c + chunk] = tn(left(to), right).astype(BF)

    weight_grad(3, lambda to: merged_ref[:, to], d_attn[...])

    heads = width // HEAD_SIZE

    def some_heads(step, _):
        for h in (step, step + heads // 2):
            win, own = head_window(h, width)
            for l in range(lat):
                at = pl.ds(l * slots, slots)
                q, k, v, dmh = q_ref[at, win], k_ref[at, win], v_ref[at, win], dm[at, win]
                s = nt((q.astype(F32) * own).astype(BF), k) * scale
                key = lax.broadcasted_iota(jnp.int32, (1, slots), 1)
                s = jnp.where(key < real[l], s, -1000000000.0)
                w = jnp.exp(s - jnp.max(s, axis=-1, keepdims=True))
                pr = w / jnp.sum(w, axis=-1, keepdims=True)
                dp = nt((dmh.astype(F32) * own).astype(BF), v)
                dsc = (pr * (dp - jnp.sum(pr * dp, axis=-1, keepdims=True))).astype(BF)
                for j, grad in enumerate(
                    (nn(dsc, k) * scale, tn(dsc, q) * scale, tn(pr.astype(BF), dmh))
                ):
                    d3[j, at, win] = jnp.where(own > 0, grad, d3[j, at, win].astype(F32)).astype(BF)
        return 0

    lax.fori_loop(0, heads // 4, some_heads, 0)
    for i in range(rs_out.links - 1, 0, -1):
        rs_out.link(i)
    lax.fori_loop(heads // 4, heads // 2, some_heads, 0)
    rs_out.finish(mlp, half)
    mlp[...] += vec_ref[1:2]
    for l in range(lat):
        dmod[5, l : l + 1] = total(cot_ref[rows_of(l)].astype(F32) * mlp[rows_of(l)])
    rs_out.rs.wait_sent()

    for j in range(3):
        weight_grad(j, lambda to, j=j: d3[j, :, to], attn_in_ref[...])

    def wave_shard(w):
        return lax.rem(z + 1 + w, count)

    waves = []
    for w in range(count):
        def mine(m, p, w=w):
            at = flip(g, m) * rows_s
            lo, ln = parts[p]
            return gbuf.at[pl.ds(pl.multiple_of(at // ds * width + ds * wave_shard(w) + at % ds + lo, 16), ln)]

        def box(m, p, w=w):
            lo, ln = parts[p]
            return abox.at[w, m - 1, pl.ds(lo, ln)]

        def add(m, key, p, mine=mine, box=box):
            mine(m, p)[...] = (mine(m, p)[...].astype(F32) + box(key, p)[...].astype(F32)).astype(BF)

        waves.append(
            Scatter(b, z, group, mine, box, lambda m, p, w=w: ra_ss.at[w, p, m], lambda m, p, w=w: ra_rs.at[w, p, m], add)
        )
    links = len(waves[0].orders[0])

    def own_slice(shard):
        at = g * rows_s
        return gbuf.at[pl.ds(pl.multiple_of(at // ds * width + ds * shard + at % ds, 16), rows_s)]

    def line_a(w):
        return pltpu.make_async_remote_copy(
            src_ref=own_slice(wave_shard(w)), dst_ref=ar.at[w], send_sem=za_ss.at[w], recv_sem=za_rs.at[w],
            device_id=(b, wave_shard(w)), device_id_type=MESH,
        )

    def wave_step(w, st):
        rs = waves[w]
        if 0 <= st < links:
            for p in range(2):
                order = rs.orders[p]
                i = links - st
                for m in span(order[: i - 1]):
                    rs.fold(m ^ order[i - 1], p)
                    rs.send(m ^ order[i - 1], p)
        elif st == links:
            for p in range(2):
                rs.fold(0, p)
            if w < count - 1:
                line_a(w).start()

    for rs in waves:
        for m in range(group - 1, 0, -2):
            for p in range(2):
                rs.send(m, p)

    def wave_round(t):
        for w in reversed(range(count)):
            wave_step(w, t - w)

    loads[3].wait()
    dain[...] = nn(d3[0], wbuf[1])
    load_v = pltpu.make_async_copy(full_ref.at[2], wbuf.at[1], loc.at[3])
    load_v.start()
    wave_round(0)
    load_k.wait()
    dain[...] += nn(d3[1], wbuf[0])
    load_v.wait()
    dain[...] += nn(d3[2], wbuf[1])
    wave_round(1)

    def put(pick, rows):
        high = rows.astype(BF)
        return nn(pick, high) + nn(pick, (rows - high.astype(F32)).astype(BF))

    for l in range(lat):
        at = rows_of(l)
        one = slice(l, l + 1)
        pick = placing(kept_ref[one], positions)
        center, inv = stats(tn(pick, tok_ref[l]))
        n = center * inv
        d_ai = dain[at]
        dmod[0, one] = total(d_ai)
        dmod[1, one] = total(d_ai * n)
        d_sel = back_b[at] + back(n, inv, d_ai * (1.0 + mod_ref[1, one]))
        dtok_o[l] = (cot_in_ref[l].astype(F32) + put(pick, d_sel)).astype(BF)

    cols = 6 * width // count
    vectors = [
        sum(total((cot_ref[rows_of(l)].astype(F32) * mod_ref[5, l : l + 1]).astype(BF).astype(F32)) for l in range(lat)),
        total(d_attn[...].astype(F32)),
        total(d3[0].astype(F32)),
        total(d3[2].astype(F32)),
    ]
    for t in range(count):
        first = t * cols // width
        for i in range(2):
            sm_send[t, i] = dmod[min(first + i, 5)]
        for i in range(4):
            sm_send[t, 2 + i // 2, i % 2 : i % 2 + 1] = vectors[i]

    def small(d):
        peer = lax.rem(z + d, count)
        return pltpu.make_async_remote_copy(
            src_ref=sm_send.at[peer], dst_ref=sm_recv.at[z], send_sem=sz_ss.at[d], recv_sem=sz_rs.at[d],
            device_id=(b, peer), device_id_type=MESH,
        )

    for d in range(1, count):
        small(d).start()
    small_own = pltpu.make_async_copy(sm_send.at[z], sm_recv.at[z], loc.at[4])
    small_own.start()
    wave_round(2)
    for l in range(lat):
        at = rows_of(l)
        one = slice(l, l + 1)
        pick = placing(kept_ref[one], positions)
        delta = (mod_ref[2, one] * attn_out_ref[at] + mod_ref[5, one] * mlp[at]) * row_mask(real[l], slots)
        out_o[l] = (tok_ref[l].astype(F32) + put(pick, delta)).astype(BF)
    for d in range(1, count):
        ref = sm_recv.at[lax.rem(z - d + count, count)]
        pltpu.make_async_remote_copy(
            src_ref=ref, dst_ref=ref, send_sem=sz_ss.at[d], recv_sem=sz_rs.at[d],
            device_id=(b, lax.rem(z + d, count)), device_id_type=MESH,
        ).wait_recv()
    small_own.wait()
    small_o[0] = jnp.zeros(small_o.shape[1:], F32)
    for i in range(2):
        for t in range(count):
            small_o[0, i, lat * t : lat * (t + 1)] = sm_recv[t, i]
    for i in range(2):
        acc = sm_recv[0, 2 + i]
        for t in range(1, count):
            acc = acc + sm_recv[t, 2 + i]
        small_o[0, 2, lat * i : lat * (i + 1)] = acc
    cond = cond_ref[...].astype(F32)
    small_o[0, 3] = (cond / (1.0 + jnp.exp(-cond))).astype(BF).astype(F32)
    sp = Gather(
        b, z, group, lambda m, p, slot: small_o.at[slot], lambda m, p: sp_ss.at[m], lambda m, p: sp_rs.at[m], halves=1
    )
    sp.step(0)
    for t in range(3, count + links - 1):
        wave_round(t)
        if t - 2 < sp.steps():
            sp.step(t - 2)

    def spread(out, ss, rs):
        def region(m, p, slot):
            lo, ln = parts[p]
            return out.at[pl.ds(pl.multiple_of(flip(g, m) * rows_s + lo, 16), ln)]

        return Gather(b, z, group, region, lambda m, p: ss.at[p, m], lambda m, p: rs.at[p, m])

    g_at = pl.ds(pl.multiple_of(g * rows_s, 16), rows_s)
    z_at = pl.ds(pl.multiple_of(z * rows_s, 16), rows_s)
    for d in range(1, count):
        for cp in line_m(d):
            cp.wait_recv()
    for own, box, out in ((gm1, mr1, gm1_o), (gm2, mr2, gm2_o)):
        acc = own[z_at].astype(F32)
        for d in range(count - 1):
            acc = acc + box[d].astype(F32)
        out[g_at] = acc.astype(BF)
    spread_1 = spread(gm1_o, gm_ss.at[0], gm_rs.at[0])
    spread_2 = spread(gm2_o, gm_ss.at[1], gm_rs.at[1])
    spread_1.step(0)
    spread_2.step(0)
    wave_round(count + links - 1)
    acc = own_slice(z)[...].astype(F32)
    for w in range(count - 1):
        line_a(w).wait_recv()
        acc = acc + ar[w].astype(F32)
    ga_o[g_at] = acc.astype(BF)
    spread_a = spread(ga_o, ga_ss, ga_rs)
    spread_a.step(0)
    for i in range(1, spread_a.steps()):
        for item in (spread_1, spread_2, spread_a):
            item.step(i)
    for i in range(max(1, count + links - 3), sp.steps()):
        sp.step(i)
    for item in (sp, spread_a, spread_1, spread_2):
        item.wait_core()
        item.wait_sent()
    for rs in waves:
        rs.wait_sent()
    for w in range(count - 1):
        line_a(w).wait_send()
    for d in range(1, count):
        small(d).wait_send()
        for cp in line_m(d):
            cp.wait_send()


def run_backward(
    dims, lat, bucket, kept, tok, cot_in, attn_in, q, k, v, merged, attn_out, hidden, cot, mod, d_in, vec, cond,
    full, g1, g2, zp,
):
    group, count, rows_s, width = dims
    rows = attn_in.shape[0]
    vm = pl.BlockSpec(memory_space=pltpu.VMEM)
    hb = pl.BlockSpec(memory_space=pl.ANY)
    sm = pl.BlockSpec(memory_space=pltpu.SMEM)
    sd = jax.ShapeDtypeStruct
    dma = pltpu.SemaphoreType.DMA
    vmem = pltpu.VMEM
    ext = g1.shape[1]
    small = (group, 4, cond.shape[0], width)
    return pl.pallas_call(
        functools.partial(backward_kernel, dims, lat),
        out_shape=(
            sd(tok.shape, BF), sd(tok.shape, BF), sd((group * rows_s, width), BF),
            sd((group * rows_s, ext), BF), sd((group * rows_s, width), BF), sd(small, F32),
        ),
        in_specs=[sm] + [vm] * 15 + [hb] * 4,
        out_specs=tuple([vm] * 6),
        scratch_shapes=[
            vmem((2, width, width), BF),
            vmem((4 * width, width), BF),
            vmem((count, group - 1, rows_s, width), BF),
            vmem((count - 1, rows_s, width), BF),
            vmem(g1.shape, BF), vmem(g2.shape, BF),
            vmem((count - 1, rows_s, ext), BF), vmem((count - 1, rows_s, width), BF),
            vmem((rows, width), F32),
            vmem((3, rows, width), BF),
            vmem((rows, width), BF), vmem((rows, width), BF),
            vmem((rows, width), F32), vmem((rows, width), F32),
            vmem((group - 1, rows, width), BF),
            vmem((count, 4, lat, width), F32), vmem((count, 4, lat, width), F32),
            vmem((6, lat, width), F32),
            dma((6,)),
            dma((2, group)), dma((2, group)),
            dma((count, 2, group)), dma((count, 2, group)),
            dma((count,)), dma((count,)),
            dma((2, count)), dma((2, count)),
            dma((2, 2, group)), dma((2, 2, group)),
            dma((2, group)), dma((2, group)),
            dma((count,)), dma((count,)),
            dma((group,)), dma((group,)),
        ],
        compiler_params=pltpu.CompilerParams(collective_id=3, has_side_effects=True, vmem_limit_bytes=63 * MIB),
        name="backward_attention",
    )(bucket, kept, tok, cot_in, attn_in, q, k, v, merged, attn_out, hidden, cot, mod, d_in, vec, cond, full, g1, g2, zp)


def widen_kernel(dims, ga_ref, gm1_ref, gm2_ref, small_ref, qkv_o, proj_o, exp_o, red_o, ada_o, vec_o, addb_o,
                 qkv, proj, exp, red, ada, sem):
    group, count, rows_s, width = dims
    ds = width // count
    cols = ada.shape[0]
    members = small_ref.shape[0] * small_ref.shape[2]

    def out(src, dst, k):
        cp = pltpu.make_async_copy(src, dst, sem.at[k])
        cp.start()
        return cp

    def item(k):
        return small_ref[:, k].reshape(members, width)

    pair = jnp.concatenate([item(0), item(1)], axis=1)
    start = lax.rem(lax.axis_index("tp") * cols, width)
    pair = pltpu.roll(pair, lax.rem(2 * width - start, 2 * width), 1)[:, 0:cols]
    addb_o[...] = jnp.sum(pair, axis=0, keepdims=True)
    ada[...] = tn(pair.astype(BF), item(3).astype(BF))
    done = [out(ada, ada_o, 0)]
    red[...] = gm2_ref[...].astype(F32)
    done.append(out(red, red_o, 1))
    qkv[...] = ga_ref[0 : 3 * ds].astype(F32)
    done.append(out(qkv, qkv_o, 2))
    proj[...] = ga_ref[3 * ds :].astype(F32)
    done.append(out(proj, proj_o, 3))
    exp[...] = gm1_ref[:, 0:width].T.astype(F32)
    done.append(out(exp, exp_o, 4))
    acc = small_ref[0, 2]
    for i in range(1, small_ref.shape[0]):
        acc = acc + small_ref[i, 2]
    vec_o[...] = acc
    for cp in done:
        cp.wait()


def run_widen(dims, cols, ga, gm1, gm2, small):
    group, count, rows_s, width = dims
    ds = width // count
    vm = pl.BlockSpec(memory_space=pltpu.VMEM)
    hb = pl.BlockSpec(memory_space=pl.ANY)
    big = [(3 * ds, width), (ds, width), (width, gm1.shape[0]), gm2.shape, (cols, width)]
    vecs = [small.shape[2:], (1, cols)]
    return pl.pallas_call(
        functools.partial(widen_kernel, dims),
        out_shape=tuple(jax.ShapeDtypeStruct(item, F32) for item in big + vecs),
        in_specs=[vm] * 4,
        out_specs=tuple([hb] * 5 + [vm] * 2),
        scratch_shapes=[pltpu.VMEM(item, F32) for item in big] + [pltpu.SemaphoreType.DMA((5,))],
        compiler_params=pltpu.CompilerParams(vmem_limit_bytes=60 * MIB),
        name="widen_gradients",
    )(ga, gm1, gm2, small)


def body(
    tokens, conditioning, bucket, kept_index, w_ada, ada_bias, w_qkv, qv_bias, w_proj, proj_bias,
    w_expand, expand_bias, w_reduce, reduce_bias, out_grad, count, batch,
):
    lat, positions, width = tokens.shape
    shard_w, shard_f = w_qkv.shape[2], w_expand.shape[1]
    group = group_size(shard_f, shard_w)
    dims = (group, count, shard_f // group, width)
    cols = ada_bias.shape[0]

    def padded(part, size):
        return jnp.pad(part.astype(F32), (0, size - part.shape[0]))

    def framed(part):
        return lax.dynamic_update_slice(jnp.zeros((width,), F32), part.astype(F32), (lax.axis_index("tp") * shard_w,))

    vec = jnp.concatenate(
        [
            proj_bias.astype(F32), reduce_bias.astype(F32), framed(qv_bias[0]), framed(qv_bias[1]),
            padded(ada_bias, 2 * width), padded(expand_bias, 2 * width),
        ]
    ).reshape(8, width)
    (attn_in, queries, key_rows, value_rows, merged, attn_out, hidden, cot, mod, d_in, zp, g1, g2, full) = run_forward(
        dims, lat, bucket, conditioning, tokens, out_grad, kept_index, vec,
        w_ada.T, jnp.swapaxes(w_qkv, 1, 2), w_proj, w_expand.T, w_reduce,
    )
    output, tokens_grad, ga, gm1, gm2, small = run_backward(
        dims, lat, bucket, kept_index, tokens, out_grad, attn_in, queries, key_rows, value_rows, merged,
        attn_out, hidden, cot, mod, d_in, vec, conditioning,
        full.reshape(4, width, width), g1, g2, zp.reshape(-1, width),
    )

    def over_batch(items):
        if batch > group:
            return tuple(lax.psum(item * (1.0 / group), "batch") for item in items)
        return items

    ga, gm1, gm2 = over_batch((ga, gm1, gm2))
    qkv_grad, proj_grad, expand_grad, reduce_grad, ada_grad, sums, ada_add = run_widen(dims, cols, ga, gm1, gm2, small)
    ada_grad, sums, ada_add = over_batch((ada_grad, sums, ada_add))
    pair_grad = lax.dynamic_slice_in_dim(sums[2:4], lax.axis_index("tp") * shard_w, shard_w, 1)
    return (
        output,
        tokens_grad,
        ada_grad.T,
        ada_add.reshape(cols),
        jnp.swapaxes(qkv_grad.reshape(3, shard_w, width), 1, 2),
        pair_grad,
        proj_grad,
        sums[1],
        expand_grad,
        gm1[:, width].astype(F32),
        reduce_grad,
        sums[0],
    )


def solution(mesh):
    rows = P(("batch", "tp"), None, None)
    return jax.shard_map(
        functools.partial(body, count=mesh.shape["tp"], batch=mesh.shape["batch"]),
        mesh=mesh,
        in_specs=(
            rows, P("batch", None), P("batch"), P(("batch", "tp"), None), P(None, "tp"), P("tp"),
            P(None, None, "tp"), P(None, "tp"), P("tp", None), P(), P(None, "tp"), P("tp"), P("tp", None), P(), rows,
        ),
        out_specs=(
            rows, rows, P(None, "tp"), P("tp"), P(None, None, "tp"), P(None, "tp"), P("tp", None), P(),
            P(None, "tp"), P("tp"), P("tp", None), P(),
        ),
        check_vma=False,
    )
```

```python
import functools
import jax
import jax.numpy as jnp
from jax import lax
from jax.experimental import pallas as pl
from jax.experimental.pallas import tpu as pltpu
from jax.sharding import PartitionSpec as P

HEAD_SIZE = 72
EPS = 1e-06
F32 = jnp.float32
BF = jnp.bfloat16
MESH = pl.DeviceIdType.MESH
MIB = 2**20


def nn(a, b):
    return lax.dot_general(a, b, (((1,), (0,)), ((), ())), preferred_element_type=F32)


def nt(a, b):
    return lax.dot_general(a, b, (((1,), (1,)), ((), ())), preferred_element_type=F32)


def tn(a, b):
    return lax.dot_general(a, b, (((0,), (0,)), ((), ())), preferred_element_type=F32)


def flip(b, mask):
    out, bit = b, 1
    while bit <= mask:
        if mask & bit:
            out = out + bit - 2 * bit * ((b // bit) % 2)
        bit *= 2
    return out


def group_size(ff_shard, width_shard):
    for size in (8, 4, 2):
        rows = ff_shard // size
        if ff_shard % size == 0 and rows % 16 == 0 and 4 * width_shard == size * rows:
            return size
    raise ValueError("no group")


def link_orders(group):
    bits = []
    bit = 2
    while bit < group:
        bits.append(bit)
        bit *= 2
    return bits, bits[::-1]


def span(bits):
    out = [0]
    for bit in bits:
        out = out + [item ^ bit for item in out]
    return out


def near_shard(z, k, count):
    low = jnp.minimum(z, count - 1 - z)
    both = z + (k // 2 + 1) * (1 - 2 * (k % 2))
    one = z + jnp.where(2 * z < count - 1, 1, -1) * (k - low + 1)
    return jnp.where(k < 2 * low, both, one)


class Gather:
    def __init__(self, b, z, group, region, send_sem, recv_sem, halves=2):
        self.b, self.z = b, z
        self.region, self.send_sem, self.recv_sem = region, send_sem, recv_sem
        self.orders = link_orders(group)[:halves] if halves == 2 else link_orders(group)[:1]
        self.group = group
        self.sent = []

    def copy(self, m, bit, p):
        return pltpu.make_async_remote_copy(
            src_ref=self.region(m, p, m),
            dst_ref=self.region(m, p, m ^ bit),
            send_sem=self.send_sem(m ^ bit, p),
            recv_sem=self.recv_sem(m ^ bit, p),
            device_id=(flip(self.b, bit), self.z),
            device_id_type=MESH,
        )

    def send(self, m, bit, p):
        cp = self.copy(m, bit, p)
        cp.start()
        self.sent.append(cp)

    def wait(self, m, p):
        ref = self.region(m, p, m)
        pltpu.make_async_remote_copy(
            src_ref=ref, dst_ref=ref, send_sem=self.send_sem(m, p), recv_sem=self.recv_sem(m, p),
            device_id=(flip(self.b, 1), self.z), device_id_type=MESH,
        ).wait_recv()

    def step(self, i, only=None):
        for p, order in enumerate(self.orders):
            if only is not None and p != only:
                continue
            if i == 0:
                fresh = [0]
            elif i <= len(order):
                fresh = [item ^ order[i - 1] for item in span(order[: i - 1])]
                for m in fresh:
                    self.wait(m, p)
            else:
                continue
            if i < len(order):
                for m in span(order[:i]):
                    self.send(m, order[i], p)
            for m in fresh:
                self.send(m, 1, p)

    def steps(self):
        return len(self.orders[0]) + 1

    def wait_core(self, m=None):
        for p in range(len(self.orders)):
            for item in range(1, self.group, 2):
                if m is None or item == m:
                    self.wait(item, p)

    def wait_sent(self):
        for cp in self.sent:
            cp.wait_send()


class Scatter:
    def __init__(self, b, z, group, mine, inbox, send_sem, recv_sem, add):
        self.b, self.z, self.group = b, z, group
        self.mine, self.inbox, self.add = mine, inbox, add
        self.send_sem, self.recv_sem = send_sem, recv_sem
        self.orders = link_orders(group)
        self.sent = []

    def top(self, m, p):
        if m & 1:
            return 1
        for bit in reversed(self.orders[p]):
            if m & bit:
                return bit

    def copy(self, m, p):
        return pltpu.make_async_remote_copy(
            src_ref=self.mine(m, p),
            dst_ref=self.inbox(m, p),
            send_sem=self.send_sem(m, p),
            recv_sem=self.recv_sem(m, p),
            device_id=(flip(self.b, self.top(m, p)), self.z),
            device_id_type=MESH,
        )

    def keys(self, m, p):
        if m & 1:
            return []
        out = [m ^ 1]
        order = self.orders[p]
        above = order if m == 0 else order[order.index(self.top(m, p)) + 1 :]
        return out + [m ^ bit for bit in reversed(above)]

    def fold(self, m, p):
        for key in self.keys(m, p):
            self.copy(key, p).wait_recv()
            self.add(m, key, p)

    def send(self, m, p):
        cp = self.copy(m, p)
        cp.start()
        self.sent.append(cp)

    def wait_sent(self):
        for cp in self.sent:
            cp.wait_send()


def barrier(b, z, group, count):
    sem = pltpu.get_barrier_semaphore()
    for m in range(1, group):
        pl.semaphore_signal(sem, 1, device_id=(flip(b, m), z), device_id_type=MESH)
    for d in range(1, count):
        pl.semaphore_signal(sem, 1, device_id=(b, lax.rem(z + d, count)), device_id_type=MESH)
    pl.semaphore_wait(sem, group - 1 + count - 1)


def stats(rows):
    center = rows - jnp.mean(rows, axis=-1, keepdims=True)
    return center, lax.rsqrt(jnp.mean(center * center, axis=-1, keepdims=True) + EPS)


def head_window(h, width):
    start = jnp.minimum(h * HEAD_SIZE // 128, width // 128 - 2) * 128
    lane = lax.broadcasted_iota(jnp.int32, (1, 256), 1) + (start - h * HEAD_SIZE)
    own = jnp.where((lane >= 0) & (lane < HEAD_SIZE), 1.0, 0.0)
    return pl.ds(pl.multiple_of(start, 128), 256), own


def kept_half(bucket, positions):
    return jnp.where(bucket > 0, (positions - positions // 16) // 2, positions // 2)


def row_mask(count, slots):
    return jnp.where(lax.broadcasted_iota(jnp.int32, (slots, 1), 0) < count, 1.0, 0.0)


def placing(kept_row, positions):
    place = lax.broadcasted_iota(jnp.int32, (positions, kept_row.shape[1]), 0)
    return jnp.where(place == kept_row, 1.0, 0.0).astype(BF)


GELU_C = 0.7978845608028654


def gelu_pair(v):
    sq = v * v
    t = jnp.tanh(GELU_C * v * (1.0 + 0.044715 * sq))
    half = 0.5 + 0.5 * t
    slope = half + 0.5 * GELU_C * v * (1.0 - t * t) * (1.0 + 3 * 0.044715 * sq)
    return v * half, slope


class Steps:
    def __init__(self, rs):
        self.rs = rs
        self.links = len(rs.orders[0])

    def send_core(self, make=None):
        for m in range(self.rs.group - 1, 0, -2):
            if make is not None:
                make(m)
            for p in range(2):
                self.rs.send(m, p)

    def last_link(self, m):
        for p in range(2):
            if self.rs.top(m, p) == self.rs.orders[p][-1]:
                self.rs.fold(m, p)
                self.rs.send(m, p)

    def link(self, i):
        for p in range(2):
            order = self.rs.orders[p]
            for m in span(order[: i - 1]):
                self.rs.fold(m ^ order[i - 1], p)
                self.rs.send(m ^ order[i - 1], p)

    def finish(self, out, half):
        for p in range(2):
            total = self.rs.mine(0, p)[...].astype(F32)
            for key in self.rs.keys(0, p):
                self.rs.copy(key, p).wait_recv()
                total = total + self.rs.inbox(key, p)[...].astype(F32)
            out[p * half : (p + 1) * half] = total


def forward_kernel(
    dims, lat, bucket_ref, cond_ref, tok_ref, cot_in_ref, kept_ref, projb_ref, qvb_ref, adab_ref, expb_ref,
    wada_hbm, own_qkv, own_proj, own_1, own_2, *rest,
):
    outs, rest = rest[:14], rest[14:]
    kept, rest = rest[:13], rest[13:]
    (attn_in_o, q_o, k_o, v_o, merged_o, attn_out_o, hidden_o, cot_o, mod_o, din_o, zp_o, g1_o, g2_o) = kept
    (full, sm_send, sm_recv, nrm, sel, mg, mod8, all_1, all_2, d_all, xb, act, dpre, y, inbox, wexp, qvs,
     sm_ss, sm_rs, za_ss, za_rs, zm_ss, zm_rs, ga_ss, ga_rs, gd_ss, gd_rs, ag_ss, ag_rs, rs_ss, rs_rs, loc, out_sem) = rest
    full_o = outs[13]
    given = []

    def give(first, last):
        for k in range(first, last):
            cp = pltpu.make_async_copy(kept[k], outs[k], out_sem.at[k])
            cp.start()
            given.append(cp)

    group, count, rows_s, width = dims
    b, z = lax.axis_index("batch"), lax.axis_index("tp")
    g = b % group
    ds = width // count
    slots = kept_ref.shape[1]
    positions = tok_ref.shape[1]
    rows = lat * slots
    half = rows // 2
    cols = wada_hbm.shape[0]
    load_ada = pltpu.make_async_copy(wada_hbm, y.at[0:cols], loc.at[1])
    load_ada.start()
    hid_s = expb_ref.shape[0]
    if hid_s == width:
        wexp = y.at[0:width]
    load_exp = pltpu.make_async_copy(own_1, wexp, loc.at[2])
    real = [kept_half(bucket_ref[z * lat + l], positions) for l in range(lat)]
    barrier(b, z, group, count)

    cut = (rows_s // 2 + 15) // 16 * 16
    parts = ((0, cut), (cut, rows_s - cut))

    def piece(member, shard, p):
        at = member * rows_s
        lo, ln = parts[p] if p is not None else (0, rows_s)
        return full.at[at // ds, shard, pl.ds(at % ds + lo, ln)]

    own_copy = [
        pltpu.make_async_copy(own_qkv, full.at[0:3, z], loc.at[0]),
        pltpu.make_async_copy(own_proj, full.at[3, z], loc.at[5]),
    ]
    for cp in own_copy:
        cp.start()

    def line_a(shard, step, k, p):
        ref = piece(g, shard, p)
        return pltpu.make_async_remote_copy(
            src_ref=ref, dst_ref=ref, send_sem=za_ss.at[p, k], recv_sem=za_rs.at[p, shard],
            device_id=(b, z + step), device_id_type=MESH,
        )

    def line_m(shard, step, k, i):
        ref = (all_1, all_2)[i].at[shard]
        return pltpu.make_async_remote_copy(
            src_ref=ref, dst_ref=ref, send_sem=zm_ss.at[i, k], recv_sem=zm_rs.at[i, shard],
            device_id=(b, z + step), device_id_type=MESH,
        )

    def passes_on(shard):
        return ((shard < z) & (z < count - 1)) | ((shard > z) & (z > 0))

    def pass_on(shard, fn):
        @pl.when((shard < z) & (z < count - 1))
        def _():
            fn(1)

        @pl.when((shard > z) & (z > 0))
        def _():
            fn(-1)

    slice_at = pl.ds(pl.multiple_of(g * rows_s, 16), rows_s)
    own_m = [pltpu.make_async_copy(own_2.at[slice_at], all_2.at[z], loc.at[3])]
    for cp in own_m:
        cp.start()

    def both_ways(fn):
        @pl.when(z < count - 1)
        def _():
            fn(1, 0)

        @pl.when(z > 0)
        def _():
            fn(-1, 1)

    for cp in own_copy:
        cp.wait()
    def start_own_a(step, k):
        for p in range(2):
            line_a(z, step, k, p).start()

    both_ways(start_own_a)

    cond = cond_ref[...].astype(F32)
    silu = (cond / (1.0 + jnp.exp(-cond))).astype(BF)
    mod8[...] = jnp.zeros_like(mod8)
    mod8[:, 0:cols] = adab_ref[...].astype(F32).reshape(1, cols) + jnp.zeros((mod8.shape[0], cols), F32)
    qvs[...] = jnp.zeros_like(qvs)
    qvs[0:2, 0:ds] = qvb_ref[...].astype(F32)
    qv_own = pltpu.roll(qvs[...], z * ds, 1)[0:2]
    load_ada.wait()
    mod8[:, 0:cols] += nt(silu, y[0:cols])
    load_exp.start()
    framed = pltpu.roll(mod8[...], (z * cols) % width, 1)
    for t in range(count):
        for i in range(2):
            sm_send[t, i] = framed[lat * t : lat * (t + 1), i * width : (i + 1) * width]
        sm_send[t, 2] = qv_own

    def small(d):
        peer = lax.rem(z + d, count)
        return pltpu.make_async_remote_copy(
            src_ref=sm_send.at[peer], dst_ref=sm_recv.at[z], send_sem=sm_ss.at[d], recv_sem=sm_rs.at[d],
            device_id=(b, peer), device_id_type=MESH,
        )

    for d in range(1, count):
        small(d).start()
    small_own = pltpu.make_async_copy(sm_send.at[z], sm_recv.at[z], loc.at[6])
    small_own.start()

    for l in range(lat):
        pick = placing(kept_ref[l : l + 1], positions)
        at = slice(l * slots, (l + 1) * slots)
        picked = tn(pick, tok_ref[l])
        sel[at] = picked
        center, inv = stats(picked)
        nrm[at] = center * inv
        cot_o[at] = (tn(pick, cot_in_ref[l]) * row_mask(real[l], slots)).astype(BF)

    take = lax.broadcasted_iota(jnp.int32, (rows_s, hid_s), 1) - lax.broadcasted_iota(jnp.int32, (rows_s, hid_s), 0)
    take = jnp.where(take == g * rows_s, 1.0, 0.0).astype(BF)
    load_exp.wait()
    all_1[z, :, 0:width] = nt(take, wexp[...]).astype(BF)
    bias_row = jnp.where(
        lax.broadcasted_iota(jnp.int32, (128, 1), 0) == 0, expb_ref[...].astype(F32).reshape(1, hid_s), 0.0
    )
    all_1[z, :, width:] = nt(take, bias_row.astype(BF)).astype(BF)

    gathers = []
    for k in range(count - 1):
        shard = near_shard(z, k, count)

        def region(m, p, slot, shard=shard):
            return piece(flip(g, m), shard, p)

        gathers.append(
            Gather(b, z, group, region, lambda m, p, k=k: ga_ss.at[k, p, m], lambda m, p, shard=shard: ga_rs.at[shard, p, m])
        )

    def arrive_a(k):
        shard = near_shard(z, k, count)
        for p in range(2):
            line_a(shard, 0, 2 + k, p).wait_recv()
            pass_on(shard, lambda step, p=p: line_a(shard, step, 2 + k, p).start())
            gathers[k].step(0, p)

    four = count == 4
    inner = (z > 0) & (z < count - 1)
    across = lax.rem(z + 2, count)

    def far_m(i):
        return line_m(z, across - z, 2, i)

    def relay_m(i):
        return line_m(across, 2 * z - 3, 3, i)

    def arrive_m(k, i):
        if four:
            return
        shard = near_shard(z, k, count)

        @pl.when(passes_on(shard))
        def _():
            line_m(shard, 0, 2 + k, i).wait_recv()

        pass_on(shard, lambda step: line_m(shard, step, 2 + k, i).start())

    def send_far():
        if four:
            for i in range(2):
                far_m(i).start()

    def relay():
        if four:

            @pl.when(inner)
            def _():
                for i in range(2):
                    relay_m(i).wait_recv()
                    relay_m(i).start()

    def send_m(step, k):
        for i in range(2):
            line_m(z, step, k, i).start()

    ends = (z == 0) | (z == count - 1)
    arrive_a(0)
    for cp in own_m:
        cp.wait()

    @pl.when(ends)
    def _():
        send_far()
        both_ways(send_m)

    for d in range(1, count):
        peer = lax.rem(z + d, count)
        ref = sm_recv.at[lax.rem(z - d + count, count)]
        pltpu.make_async_remote_copy(
            src_ref=ref, dst_ref=ref, send_sem=sm_ss.at[d], recv_sem=sm_rs.at[d], device_id=(b, peer),
            device_id_type=MESH,
        ).wait_recv()
    small_own.wait()
    blocks = [None] * 6
    for t in range(count):
        first = t * cols // width
        for i in range(2):
            if first + i < 6:
                part = sm_recv[t, i]
                blocks[first + i] = part if blocks[first + i] is None else blocks[first + i] + part
    for i in range(6):
        mod_o[i] = blocks[i]
    qv_bias = sm_recv[0, 2]
    for t in range(1, count):
        qv_bias = qv_bias + sm_recv[t, 2]
    for l in range(lat):
        at = slice(l * slots, (l + 1) * slots)
        attn_in_o[at] = (nrm[at] * (1.0 + mod_o[1, l : l + 1]) + mod_o[0, l : l + 1]).astype(BF)
        d_all[0, at] = (cot_o[at].astype(F32) * mod_o[5, l : l + 1]).astype(BF)

    for k in range(1, count - 1):
        arrive_a(k)
        if k == 1:

            @pl.when(jnp.logical_not(ends))
            def _():
                both_ways(send_m)

        gathers[k - 1].step(1)
    depth = gathers[0].steps()
    todo = [(i, k) for k in range(count - 1) for i in range(1, depth) if not (i == 1 and k < count - 2)]
    def dm_region(m, p, slot):
        return d_all.at[slot, pl.ds(p * half, half)]

    dm = Gather(b, z, group, dm_region, lambda m, p: gd_ss.at[p, m], lambda m, p: gd_rs.at[p, m])
    links = depth - 1
    todo.sort(key=lambda item: (item[0] >= links, item[0] + item[1], item[1]))
    started = False
    for i, k in todo:
        if i >= links and not started:
            dm.step(0)

            @pl.when(inner)
            def _():
                send_far()

            arrive_m(0, 0)
            arrive_m(0, 1)
            started = True
        gathers[k].step(i)
    for k in range(count - 1):
        gathers[k].wait_core()
    full_out = pltpu.make_async_copy(full, full_o, loc.at[4])
    full_out.start()

    if count > 2:
        arrive_m(1, 0)
        arrive_m(1, 1)
    relay()
    dm.step(1)

    x = attn_in_o[...]
    for j, out in enumerate((q_o, k_o, v_o)):
        part_j = nt(x, full[j].reshape(width, width))
        if j != 1:
            part_j = part_j + qv_bias[j // 2 : j // 2 + 1]
        out[...] = part_j.astype(BF)

    scale = HEAD_SIZE**-0.5

    heads = width // HEAD_SIZE

    def some_heads(step, _):
        for h in (step, step + heads // 2):
            win, own = head_window(h, width)
            for l in range(lat):
                at = pl.ds(l * slots, slots)
                q = (q_o[at, win].astype(F32) * own).astype(BF)
                s = nt(q, k_o[at, win]) * scale
                key = lax.broadcasted_iota(jnp.int32, (1, slots), 1)
                s = jnp.where(key < real[l], s, -1000000000.0)
                w = jnp.exp(s - jnp.max(s, axis=-1, keepdims=True))
                pr = (w / jnp.sum(w, axis=-1, keepdims=True)).astype(BF)
                o = nn(pr, v_o[at, win])
                mg[at, win] = jnp.where(own > 0, o, mg[at, win])
        return 0

    lax.fori_loop(0, heads // 4, some_heads, 0)
    for k in range(2, count - 1):
        arrive_m(k, 0)
    for i in range(2, dm.steps()):
        dm.step(i)
    lax.fori_loop(heads // 4, heads // 2, some_heads, 0)
    for k in range(2, count - 1):
        arrive_m(k, 1)
    merged_o[...] = mg[...].astype(BF)
    a_out = nn(merged_o[...], full[3].reshape(width, width)) + projb_ref[...].astype(F32).reshape(1, width)
    attn_out_o[...] = a_out
    for l in range(lat):
        at = slice(l * slots, (l + 1) * slots)
        mixed = sel[at] + mod_o[2, l : l + 1] * attn_out_o[at]
        hidden_o[at] = mixed
        center, inv = stats(mixed)
        xb[0, at] = (center * inv * (1.0 + mod_o[4, l : l + 1]) + mod_o[3, l : l + 1]).astype(BF)

    give(0, 9)

    def part(ref):
        return lambda m, p: ref.at[m, pl.ds(p * half, half)]

    gather = Gather(
        b, z, group, lambda m, p, slot: part(xb)(slot, p), lambda m, p: ag_ss.at[p, m], lambda m, p: ag_rs.at[p, m]
    )
    gather.step(0)
    for k in range(count - 1):
        shard = near_shard(z, k, count)

        @pl.when(jnp.logical_not(inner & (shard == across)) if four else jnp.logical_not(passes_on(shard)))
        def _():
            for i in range(2):
                line_m(shard, 0, 2 + k, i).wait_recv()

    hid = count * rows_s
    bias = nt(jnp.ones((8, all_1.shape[2] - width), BF), all_1[:, :, width:].reshape(hid, all_1.shape[2] - width))[0:1]

    def forward(pair):
        (m0, p0), (m1, p1) = pair
        at = [(m0, slice(p0 * half, (p0 + 1) * half)), (m1, slice(p1 * half, (p1 + 1) * half))]
        x = jnp.concatenate([xb[m, s] for m, s in at], axis=0)
        d = jnp.concatenate([d_all[m, s] for m, s in at], axis=0)
        a, slope = gelu_pair(nt(x, all_1[:, :, 0:width].reshape(hid, width)) + bias)
        dp = (slope * nt(d, all_2[...].reshape(hid, width))).astype(BF)
        a = a.astype(BF)
        for i, (m, s) in enumerate(at):
            to = slice(m * rows + s.start, m * rows + s.stop)
            act[to] = a[i * half : (i + 1) * half]
            dpre[to] = dp[i * half : (i + 1) * half]

    forward(((0, 0), (0, 1)))
    for p in range(2):
        gather.wait(1, p)
        dm.wait(1, p)
    forward(((1, 0), (1, 1)))
    for i in range(1, gather.steps()):
        gather.step(i)
        fresh = [[m ^ order[i - 1] for m in span(order[: i - 1])] for order in gather.orders]
        for m0, m1 in zip(*fresh):
            forward(((m0, 0), (m1, 1)))
        for m0, m1 in zip(*fresh):
            for item in (gather, dm):
                item.wait(m0 ^ 1, 0)
                item.wait(m1 ^ 1, 1)
            forward(((m0 ^ 1, 0), (m1 ^ 1, 1)))

    mine = lambda m, p: y.at[pl.ds(m * rows + p * half, half)]
    arrived = lambda m, p: inbox.at[m - 1, pl.ds(p * half, half)]

    def add(m, key, p):
        mine(m, p)[...] = (mine(m, p)[...].astype(F32) + arrived(key, p)[...].astype(F32)).astype(BF)

    rs = Steps(Scatter(b, z, group, mine, arrived, lambda m, p: rs_ss.at[p, m], lambda m, p: rs_rs.at[p, m], add))

    def part_in(m):
        at = slice(m * rows, (m + 1) * rows)
        y[at] = nn(dpre[at], all_1[:, :, 0:width].reshape(hid, width)).astype(BF)

    chunks = [slice(c, min(c + 128, hid)) for c in range(0, hid, 128)]
    rs.send_core(part_in)
    for m in range(group - 2, 0, -2):
        part_in(m)
        rs.last_link(m)
    part_in(0)
    ones = jnp.ones((group * rows, g1_o.shape[1] - width), BF)
    for c in chunks:
        g1_o[c, 0:width] = tn(dpre[:, c], xb[...].reshape(group * rows, width)).astype(BF)
        g1_o[c, width:] = tn(dpre[:, c], ones).astype(BF)
    for i in range(rs.links - 1, 0, -1):
        rs.link(i)
    for c in chunks:
        g2_o[c] = tn(act[:, c], d_all[...].reshape(group * rows, width)).astype(BF)
    for m in range(group):
        zp_o[m] = nn(act[m * rows : (m + 1) * rows], all_2[...].reshape(hid, width)).astype(BF)
    give(10, 13)
    rs.finish(din_o, half)
    give(9, 10)
    gather.wait_sent()
    rs.rs.wait_sent()

    for d in range(1, count):
        small(d).wait_send()

    def sent_own(step, k):
        for i in range(2):
            line_a(z, step, k, i).wait_send()
            line_m(z, step, k, i).wait_send()

    both_ways(sent_own)
    if four:
        for i in range(2):
            far_m(i).wait_send()

        @pl.when(inner)
        def _():
            for i in range(2):
                relay_m(i).wait_send()

    for k in range(count - 1):
        shard = near_shard(z, k, count)

        @pl.when(passes_on(shard))
        def _():
            for i in range(2):
                line_a(shard, 0, 2 + k, i).wait_send()
                if not four:
                    line_m(shard, 0, 2 + k, i).wait_send()

        gathers[k].wait_sent()
    dm.wait_sent()
    full_out.wait()
    for cp in given:
        cp.wait()


def run_forward(dims, lat, bucket, cond, tok, cot, kept, projb, qvb, adab, expb, wada, own_qkv, own_proj, own_1, own_2):
    group, count, rows_s, width = dims
    slots = kept.shape[1]
    rows = lat * slots
    hid = count * rows_s
    ext = width + 128
    vm = pl.BlockSpec(memory_space=pltpu.VMEM)
    hb = pl.BlockSpec(memory_space=pl.ANY)
    sm = pl.BlockSpec(memory_space=pltpu.SMEM)
    sd = jax.ShapeDtypeStruct
    row_bf, row_f = sd((rows, width), BF), sd((rows, width), F32)
    blocks = sd((group, rows, width), BF)
    dma = pltpu.SemaphoreType.DMA
    vmem = pltpu.VMEM
    outs = (
        row_bf, row_bf, row_bf, row_bf, row_bf, row_f, row_f, row_bf, sd((6, lat, width), F32),
        row_f, blocks, sd((hid, ext), BF), sd((hid, width), BF), sd((4, count, width // count, width), BF),
    )
    return pl.pallas_call(
        functools.partial(forward_kernel, dims, lat),
        out_shape=outs,
        in_specs=[sm] + [vm] * 8 + [hb] * 5,
        out_specs=tuple([hb] * 14),
        scratch_shapes=[vmem(item.shape, item.dtype) for item in outs[:13]] + [
            vmem((4, count, width // count, width), BF),
            vmem((count, 3, lat, width), F32), vmem((count, 3, lat, width), F32),
            vmem((rows, width), F32), vmem((rows, width), F32), vmem((rows, width), F32),
            vmem((cond.shape[0], 2 * width), F32),
            vmem((count, rows_s, ext), BF), vmem((count, rows_s, width), BF),
            vmem((group, rows, width), BF), vmem((group, rows, width), BF),
            vmem((group * rows, hid), BF), vmem((group * rows, hid), BF),
            vmem((group * rows, width), BF), vmem((group - 1, rows, width), BF),
            vmem((16, 128) if own_1.shape[1] == width else own_1.shape, BF), vmem((8, width), F32),
            dma((count,)), dma((count,)),
            dma((2, count + 1)), dma((2, count)),
            dma((2, count + 1)), dma((2, count)),
            dma((count - 1, 2, group)), dma((count, 2, group)),
            dma((2, group)), dma((2, group)), dma((2, group)), dma((2, group)), dma((2, group)), dma((2, group)),
            dma((7,)), dma((14,)),
        ],
        compiler_params=pltpu.CompilerParams(collective_id=1, has_side_effects=True, vmem_limit_bytes=63 * MIB),
        name="forward_attention",
    )(bucket, cond, tok, cot, kept, projb, qvb, adab, expb, wada, own_qkv, own_proj, own_1, own_2)


def backward_kernel(dims, lat, bucket_ref, kept_ref, redb_ref, cond_ref, *rest):
    held, rest = rest[:12], rest[12:]
    (full_ref, g1_ref, g2_ref, zp_ref), rest = rest[:4], rest[4:]
    outs, rest = rest[:3], rest[3:]
    (ga_o, gm1_o, gm2_o), rest = rest[:3], rest[3:]
    local, rest = rest[:12], rest[12:]
    (tok_ref, cot_in_ref, attn_in_ref, q_ref, k_ref, v_ref, merged_ref, attn_out_ref, hidden_ref, cot_ref, mod_ref,
     d_in_ref) = local
    small_o, rest = rest[0], rest[1:]
    out_o, dtok_o, dain, mlp = tok_ref, cot_in_ref, d_in_ref, hidden_ref
    (wbuf, gbuf, abox, ar, gm1, gm2, mr1, mr2, back_b, d3, d_attn, dm, inbox, sm_send, sm_recv, dmod,
     loc, in_sem, out_sem, ro_ss, ro_rs, ra_ss, ra_rs, za_ss, za_rs, zm_ss, zm_rs, gm_ss, gm_rs, ga_ss, ga_rs, sz_ss, sz_rs,
     sp_ss, sp_rs) = rest
    takes = [pltpu.make_async_copy(held[k], local[k], in_sem.at[k]) for k in range(12)]

    def need(*which):
        for k in which:
            takes[k].wait()

    gives = [
        pltpu.make_async_copy(src, dst, out_sem.at[k])
        for k, (src, dst) in enumerate(zip((out_o, dtok_o, small_o), outs))
    ]
    group, count, rows_s, width = dims
    b, z = lax.axis_index("batch"), lax.axis_index("tp")
    g = b % group
    ds = width // count
    slots = kept_ref.shape[1]
    positions = tok_ref.shape[1]
    rows = lat * slots
    half = rows // 2
    scale = HEAD_SIZE**-0.5
    loads = [
        pltpu.make_async_copy(g1_ref, gm1, loc.at[0]),
        pltpu.make_async_copy(g2_ref, gm2, loc.at[1]),
        pltpu.make_async_copy(full_ref.at[3], wbuf.at[0], loc.at[2]),
        pltpu.make_async_copy(full_ref.at[0], wbuf.at[1], loc.at[3]),
        pltpu.make_async_copy(zp_ref, gbuf.at[0 : group * rows], loc.at[5]),
    ]
    for cp in (loads[4], loads[0], loads[1], takes[8], takes[9], takes[10], takes[11], takes[7], loads[2]):
        cp.start()
    for k in (6, 3, 4, 5, 2, 0, 1):
        takes[k].start()
    loads[3].start()
    real = [kept_half(bucket_ref[z * lat + l], positions) for l in range(lat)]
    barrier(b, z, group, count)

    mine_out = lambda m, p: gbuf.at[pl.ds(m * rows + p * half, half)]
    box_out = lambda m, p: inbox.at[m - 1, pl.ds(p * half, half)]

    def add_out(m, key, p):
        mine_out(m, p)[...] = (mine_out(m, p)[...].astype(F32) + box_out(key, p)[...].astype(F32)).astype(BF)

    rs_out = Steps(
        Scatter(b, z, group, mine_out, box_out, lambda m, p: ro_ss.at[p, m], lambda m, p: ro_rs.at[p, m], add_out)
    )
    loads[4].wait()
    rs_out.send_core()
    cut = (rows_s // 2 + 15) // 16 * 16
    parts = ((0, cut), (cut, rows_s - cut))

    loads[0].wait()
    loads[1].wait()

    four = count == 4
    inner = (z > 0) & (z < count - 1)
    across = lax.rem(z + 2, count)
    sums = ((gm1, mr1), (gm2, mr2))

    def rows_for(shard):
        return pl.ds(pl.multiple_of(shard * rows_s, 16), rows_s)

    def line_m(shard, peer, box, k):
        return [
            pltpu.make_async_remote_copy(
                src_ref=src.at[rows_for(shard)], dst_ref=dst.at[box], send_sem=zm_ss.at[i, k], recv_sem=zm_rs.at[i, box],
                device_id=(b, peer), device_id_type=MESH,
            )
            for i, (src, dst) in enumerate(sums)
        ]

    def start(copies):
        for cp in copies:
            cp.start()

    def wait_in(box):
        for cp in line_m(z, z, box, 0):
            cp.wait_recv()

    def wait_out(copies):
        for cp in copies:
            cp.wait_send()

    def line_sends(fn):
        if not four:
            for d in range(1, count):
                peer = lax.rem(z + d, count)
                fn(line_m(peer, peer, d - 1, d - 1))
            return

        @pl.when(jnp.logical_not(inner))
        def _():
            fn(line_m(count - 1 - z, jnp.where(z == 0, 1, count - 2), 3, 3))
            fn(line_m(across, across, 2, 2))

        @pl.when(z < count - 1)
        def _():
            fn(line_m(z + 1, z + 1, 0, 0))

        @pl.when(z > 0)
        def _():
            fn(line_m(z - 1, z - 1, 1, 1))

    def line_relay(fn):
        if four:

            @pl.when(inner)
            def _():
                fn(line_m(across, across, 2, 2))

    def relay_add():
        if four:

            @pl.when(inner)
            def _():
                wait_in(3)
                for src, box in sums:
                    at = rows_for(across)
                    src[at] = (src[at].astype(F32) + box[3].astype(F32)).astype(BF)

        line_relay(start)

    def line_total():
        def take(box):
            wait_in(box)
            for src, boxes in sums:
                at = rows_for(z)
                src[at] = (src[at].astype(F32) + boxes[box].astype(F32)).astype(BF)

        if four:
            pl.when(z > 0)(lambda: take(0))
            pl.when(z < count - 1)(lambda: take(1))
            take(2)
        else:
            for d in range(count - 1):
                take(d)

    line_sends(start)

    def rows_of(l):
        return slice(l * slots, (l + 1) * slots)

    def back(n, inv, grad):
        return (grad - jnp.mean(grad, axis=-1, keepdims=True) - n * jnp.mean(grad * n, axis=-1, keepdims=True)) * inv

    def total(rows):
        return jnp.sum(rows, axis=0, keepdims=True)

    for m in range(group - 2, 0, -2):
        rs_out.last_link(m)
    need(7, 8, 9, 10, 11)
    for l in range(lat):
        at = rows_of(l)
        one = slice(l, l + 1)
        center, inv = stats(hidden_ref[at])
        n = center * inv
        d_in = d_in_ref[at]
        cot = cot_ref[at].astype(F32)
        back_b[at] = back(n, inv, d_in * (1.0 + mod_ref[4, one]))
        d_hidden = cot + back_b[at]
        d_attn[at] = (mod_ref[2, one] * d_hidden).astype(BF)
        dmod[3, one] = total(d_in)
        dmod[4, one] = total(d_in * n)
        dmod[2, one] = total(d_hidden * attn_out_ref[at])

    loads[2].wait()
    dm[...] = nt(d_attn[...], wbuf[0]).astype(BF)
    load_k = pltpu.make_async_copy(full_ref.at[1], wbuf.at[0], loc.at[2])
    load_k.start()
    chunk = 384

    def weight_grad(j, left, right):
        for c in range(0, width, chunk):
            to = slice(c, c + chunk)
            gbuf[j * width + c : j * width + c + chunk] = tn(left(to), right).astype(BF)

    need(6)
    weight_grad(3, lambda to: merged_ref[:, to], d_attn[...])

    heads = width // HEAD_SIZE

    def some_heads(step, _):
        for h in (step, step + heads // 2):
            win, own = head_window(h, width)
            for l in range(lat):
                at = pl.ds(l * slots, slots)
                q, k, v, dmh = q_ref[at, win], k_ref[at, win], v_ref[at, win], dm[at, win]
                s = nt((q.astype(F32) * own).astype(BF), k) * scale
                key = lax.broadcasted_iota(jnp.int32, (1, slots), 1)
                s = jnp.where(key < real[l], s, -1000000000.0)
                w = jnp.exp(s - jnp.max(s, axis=-1, keepdims=True))
                pr = w / jnp.sum(w, axis=-1, keepdims=True)
                dp = nt((dmh.astype(F32) * own).astype(BF), v)
                dsc = (pr * (dp - jnp.sum(pr * dp, axis=-1, keepdims=True))).astype(BF)
                for j, grad in enumerate(
                    (nn(dsc, k) * scale, tn(dsc, q) * scale, tn(pr.astype(BF), dmh))
                ):
                    d3[j, at, win] = jnp.where(own > 0, grad, d3[j, at, win].astype(F32)).astype(BF)
        return 0

    need(3, 4, 5)
    lax.fori_loop(0, heads // 4, some_heads, 0)
    for i in range(rs_out.links - 1, 0, -1):
        rs_out.link(i)
    relay_add()
    lax.fori_loop(heads // 4, heads // 2, some_heads, 0)
    rs_out.finish(mlp, half)
    mlp[...] += redb_ref[...].astype(F32).reshape(1, width)
    for l in range(lat):
        dmod[5, l : l + 1] = total(cot_ref[rows_of(l)].astype(F32) * mlp[rows_of(l)])
    rs_out.rs.wait_sent()

    need(2)
    for j in range(3):
        weight_grad(j, lambda to, j=j: d3[j, :, to], attn_in_ref[...])

    def wave_shard(w):
        return lax.rem(z + 1 + w, count)

    waves = []
    for w in range(count):
        def mine(m, p, w=w):
            at = flip(g, m) * rows_s
            lo, ln = parts[p]
            return gbuf.at[pl.ds(pl.multiple_of(at // ds * width + ds * wave_shard(w) + at % ds + lo, 16), ln)]

        def box(m, p, w=w):
            lo, ln = parts[p]
            return abox.at[w, m - 1, pl.ds(lo, ln)]

        def add(m, key, p, mine=mine, box=box):
            mine(m, p)[...] = (mine(m, p)[...].astype(F32) + box(key, p)[...].astype(F32)).astype(BF)

        waves.append(
            Scatter(b, z, group, mine, box, lambda m, p, w=w: ra_ss.at[w, p, m], lambda m, p, w=w: ra_rs.at[w, p, m], add)
        )
    links = len(waves[0].orders[0])

    def own_slice(shard):
        at = g * rows_s
        return gbuf.at[pl.ds(pl.multiple_of(at // ds * width + ds * shard + at % ds, 16), rows_s)]

    def line_a(w):
        return pltpu.make_async_remote_copy(
            src_ref=own_slice(wave_shard(w)), dst_ref=ar.at[w], send_sem=za_ss.at[w], recv_sem=za_rs.at[w],
            device_id=(b, wave_shard(w)), device_id_type=MESH,
        )

    def wave_step(w, st):
        rs = waves[w]
        if 0 <= st < links:
            for p in range(2):
                order = rs.orders[p]
                i = links - st
                for m in span(order[: i - 1]):
                    rs.fold(m ^ order[i - 1], p)
                    rs.send(m ^ order[i - 1], p)
        elif st == links:
            for p in range(2):
                rs.fold(0, p)
            if w < count - 1:
                line_a(w).start()

    for rs in waves:
        for m in range(group - 1, 0, -2):
            for p in range(2):
                rs.send(m, p)

    def wave_round(t):
        for w in reversed(range(count)):
            wave_step(w, t - w)

    loads[3].wait()
    dain[...] = nn(d3[0], wbuf[1])
    load_v = pltpu.make_async_copy(full_ref.at[2], wbuf.at[1], loc.at[3])
    load_v.start()
    wave_round(0)
    load_k.wait()
    dain[...] += nn(d3[1], wbuf[0])
    load_v.wait()
    dain[...] += nn(d3[2], wbuf[1])
    wave_round(1)

    def put(pick, rows):
        high = rows.astype(BF)
        return nn(pick, high) + nn(pick, (rows - high.astype(F32)).astype(BF))

    need(0, 1)
    for l in range(lat):
        at = rows_of(l)
        one = slice(l, l + 1)
        pick = placing(kept_ref[one], positions)
        center, inv = stats(tn(pick, tok_ref[l]))
        n = center * inv
        d_ai = dain[at]
        dmod[0, one] = total(d_ai)
        dmod[1, one] = total(d_ai * n)
        d_sel = back_b[at] + back(n, inv, d_ai * (1.0 + mod_ref[1, one]))
        dtok_o[l] = (cot_in_ref[l].astype(F32) + put(pick, d_sel)).astype(BF)

    gives[1].start()

    cols = 6 * width // count
    vectors = [
        sum(total((cot_ref[rows_of(l)].astype(F32) * mod_ref[5, l : l + 1]).astype(BF).astype(F32)) for l in range(lat)),
        total(d_attn[...].astype(F32)),
        total(d3[0].astype(F32)),
        total(d3[2].astype(F32)),
    ]
    for t in range(count):
        first = t * cols // width
        for i in range(2):
            sm_send[t, i] = dmod[min(first + i, 5)]
        for i in range(4):
            sm_send[t, 2 + i // 2, i % 2 : i % 2 + 1] = vectors[i]

    def small(d):
        peer = lax.rem(z + d, count)
        return pltpu.make_async_remote_copy(
            src_ref=sm_send.at[peer], dst_ref=sm_recv.at[z], send_sem=sz_ss.at[d], recv_sem=sz_rs.at[d],
            device_id=(b, peer), device_id_type=MESH,
        )

    for d in range(1, count):
        small(d).start()
    small_own = pltpu.make_async_copy(sm_send.at[z], sm_recv.at[z], loc.at[4])
    small_own.start()
    wave_round(2)
    for l in range(lat):
        at = rows_of(l)
        one = slice(l, l + 1)
        pick = placing(kept_ref[one], positions)
        delta = (mod_ref[2, one] * attn_out_ref[at] + mod_ref[5, one] * mlp[at]) * row_mask(real[l], slots)
        out_o[l] = (tok_ref[l].astype(F32) + put(pick, delta)).astype(BF)
    gives[0].start()
    for d in range(1, count):
        ref = sm_recv.at[lax.rem(z - d + count, count)]
        pltpu.make_async_remote_copy(
            src_ref=ref, dst_ref=ref, send_sem=sz_ss.at[d], recv_sem=sz_rs.at[d],
            device_id=(b, lax.rem(z + d, count)), device_id_type=MESH,
        ).wait_recv()
    small_own.wait()
    small_o[0] = jnp.zeros(small_o.shape[1:], F32)
    for i in range(2):
        for t in range(count):
            small_o[0, i, lat * t : lat * (t + 1)] = sm_recv[t, i]
    for i in range(2):
        acc = sm_recv[0, 2 + i]
        for t in range(1, count):
            acc = acc + sm_recv[t, 2 + i]
        small_o[0, 2, lat * i : lat * (i + 1)] = acc
    cond = cond_ref[...].astype(F32)
    small_o[0, 3] = (cond / (1.0 + jnp.exp(-cond))).astype(BF).astype(F32)
    sp = Gather(
        b, z, group, lambda m, p, slot: small_o.at[slot], lambda m, p: sp_ss.at[m], lambda m, p: sp_rs.at[m], halves=1
    )
    sp.step(0)
    def spread(out, ss, rs):
        def region(m, p, slot):
            lo, ln = parts[p]
            return out.at[pl.ds(pl.multiple_of(flip(g, m) * rows_s + lo, 16), ln)]

        return Gather(b, z, group, region, lambda m, p: ss.at[p, m], lambda m, p: rs.at[p, m])

    g_at = pl.ds(pl.multiple_of(g * rows_s, 16), rows_s)
    line_total()
    for own, out in ((gm1, gm1_o), (gm2, gm2_o)):
        out[g_at] = own[rows_for(z)]
    spread_1 = spread(gm1_o, gm_ss.at[0], gm_rs.at[0])
    spread_2 = spread(gm2_o, gm_ss.at[1], gm_rs.at[1])
    spread_1.step(0)
    spread_2.step(0)
    for t in range(3, count + links):
        wave_round(t)
        if t - 2 < sp.steps():
            sp.step(t - 2)
        if t == 4:
            spread_1.step(1)
            spread_2.step(1)
    acc = own_slice(z)[...].astype(F32)
    for w in range(count - 1):
        line_a(w).wait_recv()
        acc = acc + ar[w].astype(F32)
    ga_o[g_at] = acc.astype(BF)
    spread_a = spread(ga_o, ga_ss, ga_rs)
    spread_a.step(0)
    for i in range(1, spread_a.steps()):
        for item in (spread_1, spread_2):
            if i > 1:
                item.step(i)
        spread_a.step(i)
    for i in range(max(1, count + links - 2), sp.steps()):
        sp.step(i)
    sp.wait_core()
    gives[2].start()
    for item in (spread_1, spread_2, spread_a):
        item.wait_core()
    for item in (sp, spread_a, spread_1, spread_2):
        item.wait_sent()
    for cp in gives:
        cp.wait()
    for rs in waves:
        rs.wait_sent()
    for w in range(count - 1):
        line_a(w).wait_send()
    for d in range(1, count):
        small(d).wait_send()
    line_sends(wait_out)
    line_relay(wait_out)


def run_backward(
    dims, lat, bucket, kept, tok, cot_in, attn_in, q, k, v, merged, attn_out, hidden, cot, mod, d_in, redb, cond,
    full, g1, g2, zp,
):
    group, count, rows_s, width = dims
    rows = attn_in.shape[0]
    vm = pl.BlockSpec(memory_space=pltpu.VMEM)
    hb = pl.BlockSpec(memory_space=pl.ANY)
    sm = pl.BlockSpec(memory_space=pltpu.SMEM)
    sd = jax.ShapeDtypeStruct
    dma = pltpu.SemaphoreType.DMA
    vmem = pltpu.VMEM
    ext = g1.shape[1]
    boxes = max(4, count - 1)
    small = (group, 4, cond.shape[0], width)
    held = (tok, cot_in, attn_in, q, k, v, merged, attn_out, hidden, cot, mod, d_in)
    return pl.pallas_call(
        functools.partial(backward_kernel, dims, lat),
        out_shape=(
            sd(tok.shape, BF), sd(tok.shape, BF), sd(small, F32),
            sd((group * rows_s, width), BF), sd((group * rows_s, ext), BF), sd((group * rows_s, width), BF),
        ),
        in_specs=[sm] + [vm] * 3 + [hb] * 16,
        out_specs=tuple([hb] * 3 + [vm] * 3),
        scratch_shapes=[vmem(item.shape, item.dtype) for item in held] + [
            vmem(small, F32),
            vmem((2, width, width), BF),
            vmem((4 * width, width), BF),
            vmem((count, group - 1, rows_s, width), BF),
            vmem((count - 1, rows_s, width), BF),
            vmem(g1.shape, BF), vmem(g2.shape, BF),
            vmem((boxes, rows_s, ext), BF), vmem((boxes, rows_s, width), BF),
            vmem((rows, width), F32),
            vmem((3, rows, width), BF),
            vmem((rows, width), BF), vmem((rows, width), BF),
            vmem((group - 1, rows, width), BF),
            vmem((count, 4, lat, width), F32), vmem((count, 4, lat, width), F32),
            vmem((6, lat, width), F32),
            dma((6,)), dma((12,)), dma((3,)),
            dma((2, group)), dma((2, group)),
            dma((count, 2, group)), dma((count, 2, group)),
            dma((count,)), dma((count,)),
            dma((2, boxes)), dma((2, boxes)),
            dma((2, 2, group)), dma((2, 2, group)),
            dma((2, group)), dma((2, group)),
            dma((count,)), dma((count,)),
            dma((group,)), dma((group,)),
        ],
        compiler_params=pltpu.CompilerParams(collective_id=3, has_side_effects=True, vmem_limit_bytes=63 * MIB),
        name="backward_attention",
    )(bucket, kept, redb, cond, *held, full, g1, g2, zp)


def widen_kernel(dims, ga_h, gm1_h, gm2_h, small_h, qkv_o, proj_o, exp_o, red_o, ada_o, adab_o, pair_o, projb_o, redb_o, expb_o,
                 ga_ref, gm1_ref, gm2_ref, small_ref, qkv, proj, exp, red, ada, sem):
    group, count, rows_s, width = dims
    ds = width // count
    cols = ada.shape[0]
    members = small_ref.shape[0] * small_ref.shape[2]
    z = lax.axis_index("tp")

    def move(src, dst, k):
        cp = pltpu.make_async_copy(src, dst, sem.at[k])
        cp.start()
        return cp

    loads = [move(small_h, small_ref, 5), move(gm2_h, gm2_ref, 6), move(gm1_h, gm1_ref, 7), move(ga_h, ga_ref, 8)]

    def item(k):
        return small_ref[:, k].reshape(members, width)

    loads[0].wait()
    pair = jnp.concatenate([item(0), item(1)], axis=1)
    start = lax.rem(z * cols, width)
    pair = pltpu.roll(pair, lax.rem(2 * width - start, 2 * width), 1)[:, 0:cols]
    ada[...] = tn(pair.astype(BF), item(3).astype(BF))
    done = [move(ada, ada_o, 0)]
    loads[1].wait()
    red[...] = gm2_ref[...].astype(F32)
    done.append(move(red, red_o, 1))
    loads[2].wait()
    exp[...] = gm1_ref[:, 0:width].T.astype(F32)
    done.append(move(exp, exp_o, 2))
    loads[3].wait()
    qkv[...] = ga_ref[0 : 3 * ds].astype(F32)
    done.append(move(qkv, qkv_o, 3))
    proj[...] = ga_ref[3 * ds :].astype(F32)
    done.append(move(proj, proj_o, 4))
    adab_o[...] = jnp.sum(pair, axis=0)
    acc = small_ref[0, 2]
    for i in range(1, small_ref.shape[0]):
        acc = acc + small_ref[i, 2]
    redb_o[...] = acc[0]
    projb_o[...] = acc[1]
    pair_o[...] = pltpu.roll(acc, lax.rem(width - z * ds, width), 1)[2:4, 0:ds]
    corner = lax.broadcasted_iota(jnp.int32, (8, 1), 0) + lax.broadcasted_iota(jnp.int32, (1, 128), 1)
    expb_o[...] = nt(jnp.where(corner == 0, 1.0, 0.0).astype(BF), gm1_ref[:, width:])[0]
    for cp in done:
        cp.wait()


def run_widen(dims, cols, ga, gm1, gm2, small):
    group, count, rows_s, width = dims
    ds = width // count
    vm = pl.BlockSpec(memory_space=pltpu.VMEM)
    hb = pl.BlockSpec(memory_space=pl.ANY)
    hid_s = gm1.shape[0]
    big = [(3 * ds, width), (ds, width), (width, hid_s), gm2.shape, (cols, width)]
    vecs = [(cols,), (2, ds), (width,), (width,), (hid_s,)]
    given = (ga, gm1, gm2, small)
    return pl.pallas_call(
        functools.partial(widen_kernel, dims),
        out_shape=tuple(jax.ShapeDtypeStruct(item, F32) for item in big + vecs),
        in_specs=[hb] * 4,
        out_specs=tuple([hb] * 5 + [vm] * 5),
        scratch_shapes=[pltpu.VMEM(item.shape, item.dtype) for item in given]
        + [pltpu.VMEM(item, F32) for item in big]
        + [pltpu.SemaphoreType.DMA((9,))],
        compiler_params=pltpu.CompilerParams(vmem_limit_bytes=60 * MIB),
        name="widen_gradients",
    )(*given)


def body(
    tokens, conditioning, bucket, kept_index, w_ada, ada_bias, w_qkv, qv_bias, w_proj, proj_bias,
    w_expand, expand_bias, w_reduce, reduce_bias, out_grad, count, batch,
):
    lat, positions, width = tokens.shape
    shard_w, shard_f = w_qkv.shape[2], w_expand.shape[1]
    group = group_size(shard_f, shard_w)
    dims = (group, count, shard_f // group, width)
    cols = ada_bias.shape[0]

    (attn_in, queries, key_rows, value_rows, merged, attn_out, hidden, cot, mod, d_in, zp, g1, g2, full) = run_forward(
        dims, lat, bucket, conditioning, tokens, out_grad, kept_index, proj_bias, qv_bias, ada_bias, expand_bias,
        w_ada.T, jnp.swapaxes(w_qkv, 1, 2), w_proj, w_expand, w_reduce,
    )
    output, tokens_grad, small, ga, gm1, gm2 = run_backward(
        dims, lat, bucket, kept_index, tokens, out_grad, attn_in, queries, key_rows, value_rows, merged,
        attn_out, hidden, cot, mod, d_in, reduce_bias, conditioning,
        full.reshape(4, width, width), g1, g2, zp.reshape(-1, width),
    )

    def over_batch(items):
        if batch > group:
            return tuple(lax.psum(item * (1.0 / group), "batch") for item in items)
        return items

    ga, gm1, gm2 = over_batch((ga, gm1, gm2))
    qkv_grad, proj_grad, expand_grad, reduce_grad, *sums = run_widen(dims, cols, ga, gm1, gm2, small)
    ada_grad, ada_add, pair_grad, proj_add, reduce_add = over_batch(tuple(sums[:5]))
    return (
        output,
        tokens_grad,
        ada_grad.T,
        ada_add,
        jnp.swapaxes(qkv_grad.reshape(3, shard_w, width), 1, 2),
        pair_grad,
        proj_grad,
        proj_add,
        expand_grad,
        sums[5],
        reduce_grad,
        reduce_add,
    )


def solution(mesh):
    rows = P(("batch", "tp"), None, None)
    return jax.shard_map(
        functools.partial(body, count=mesh.shape["tp"], batch=mesh.shape["batch"]),
        mesh=mesh,
        in_specs=(
            rows, P("batch", None), P("batch"), P(("batch", "tp"), None), P(None, "tp"), P("tp"),
            P(None, None, "tp"), P(None, "tp"), P("tp", None), P(), P(None, "tp"), P("tp"), P("tp", None), P(), rows,
        ),
        out_specs=(
            rows, rows, P(None, "tp"), P("tp"), P(None, None, "tp"), P(None, "tp"), P("tp", None), P(),
            P(None, "tp"), P("tp"), P("tp", None), P(),
        ),
        check_vma=False,
    )
```

```python
import functools
import jax
import jax.numpy as jnp
from jax import lax
from jax.experimental import pallas as pl
from jax.experimental.pallas import tpu as pltpu
from jax.sharding import PartitionSpec as P

HEAD_SIZE = 72
EPS = 1e-06
F32 = jnp.float32
BF = jnp.bfloat16
MESH = pl.DeviceIdType.MESH
MIB = 2**20


def nn(a, b):
    return lax.dot_general(a, b, (((1,), (0,)), ((), ())), preferred_element_type=F32)


def nt(a, b):
    return lax.dot_general(a, b, (((1,), (1,)), ((), ())), preferred_element_type=F32)


def tn(a, b):
    return lax.dot_general(a, b, (((0,), (0,)), ((), ())), preferred_element_type=F32)


def flip(b, mask):
    out, bit = b, 1
    while bit <= mask:
        if mask & bit:
            out = out + bit - 2 * bit * ((b // bit) % 2)
        bit *= 2
    return out


def group_size(ff_shard, width_shard):
    for size in (8, 4, 2):
        rows = ff_shard // size
        if ff_shard % size == 0 and rows % 16 == 0 and 4 * width_shard == size * rows:
            return size
    raise ValueError("no group")


def link_orders(group):
    bits = []
    bit = 2
    while bit < group:
        bits.append(bit)
        bit *= 2
    return bits, bits[::-1]


def span(bits):
    out = [0]
    for bit in bits:
        out = out + [item ^ bit for item in out]
    return out


def near_shard(z, k, count):
    low = jnp.minimum(z, count - 1 - z)
    both = z + (k // 2 + 1) * (1 - 2 * (k % 2))
    one = z + jnp.where(2 * z < count - 1, 1, -1) * (k - low + 1)
    return jnp.where(k < 2 * low, both, one)


class Gather:
    def __init__(self, b, z, group, region, send_sem, recv_sem, halves=2):
        self.b, self.z = b, z
        self.region, self.send_sem, self.recv_sem = region, send_sem, recv_sem
        self.orders = link_orders(group)[:halves] if halves == 2 else link_orders(group)[:1]
        self.group = group
        self.sent = []

    def copy(self, m, bit, p):
        return pltpu.make_async_remote_copy(
            src_ref=self.region(m, p, m),
            dst_ref=self.region(m, p, m ^ bit),
            send_sem=self.send_sem(m ^ bit, p),
            recv_sem=self.recv_sem(m ^ bit, p),
            device_id=(flip(self.b, bit), self.z),
            device_id_type=MESH,
        )

    def send(self, m, bit, p):
        cp = self.copy(m, bit, p)
        cp.start()
        self.sent.append(cp)

    def wait(self, m, p):
        ref = self.region(m, p, m)
        pltpu.make_async_remote_copy(
            src_ref=ref, dst_ref=ref, send_sem=self.send_sem(m, p), recv_sem=self.recv_sem(m, p),
            device_id=(flip(self.b, 1), self.z), device_id_type=MESH,
        ).wait_recv()

    def step(self, i, only=None):
        for p, order in enumerate(self.orders):
            if only is not None and p != only:
                continue
            if i == 0:
                fresh = [0]
            elif i <= len(order):
                fresh = [item ^ order[i - 1] for item in span(order[: i - 1])]
                for m in fresh:
                    self.wait(m, p)
            else:
                continue
            if i < len(order):
                for m in span(order[:i]):
                    self.send(m, order[i], p)
            for m in fresh:
                self.send(m, 1, p)

    def steps(self):
        return len(self.orders[0]) + 1

    def wait_core(self, m=None):
        for p in range(len(self.orders)):
            for item in range(1, self.group, 2):
                if m is None or item == m:
                    self.wait(item, p)

    def wait_sent(self):
        for cp in self.sent:
            cp.wait_send()


class Scatter:
    def __init__(self, b, z, group, mine, inbox, send_sem, recv_sem, add):
        self.b, self.z, self.group = b, z, group
        self.mine, self.inbox, self.add = mine, inbox, add
        self.send_sem, self.recv_sem = send_sem, recv_sem
        self.orders = link_orders(group)
        self.sent = []

    def top(self, m, p):
        if m & 1:
            return 1
        for bit in reversed(self.orders[p]):
            if m & bit:
                return bit

    def copy(self, m, p):
        return pltpu.make_async_remote_copy(
            src_ref=self.mine(m, p),
            dst_ref=self.inbox(m, p),
            send_sem=self.send_sem(m, p),
            recv_sem=self.recv_sem(m, p),
            device_id=(flip(self.b, self.top(m, p)), self.z),
            device_id_type=MESH,
        )

    def keys(self, m, p):
        if m & 1:
            return []
        out = [m ^ 1]
        order = self.orders[p]
        above = order if m == 0 else order[order.index(self.top(m, p)) + 1 :]
        return out + [m ^ bit for bit in reversed(above)]

    def fold(self, m, p):
        for key in self.keys(m, p):
            self.copy(key, p).wait_recv()
            self.add(m, key, p)

    def send(self, m, p):
        cp = self.copy(m, p)
        cp.start()
        self.sent.append(cp)

    def wait_sent(self):
        for cp in self.sent:
            cp.wait_send()


def barrier(b, z, group, count):
    sem = pltpu.get_barrier_semaphore()
    for m in range(1, group):
        pl.semaphore_signal(sem, 1, device_id=(flip(b, m), z), device_id_type=MESH)
    for d in range(1, count):
        pl.semaphore_signal(sem, 1, device_id=(b, lax.rem(z + d, count)), device_id_type=MESH)
    pl.semaphore_wait(sem, group - 1 + count - 1)


def stats(rows):
    center = rows - jnp.mean(rows, axis=-1, keepdims=True)
    return center, lax.rsqrt(jnp.mean(center * center, axis=-1, keepdims=True) + EPS)


def head_window(h, width):
    start = jnp.minimum(h * HEAD_SIZE // 128, width // 128 - 2) * 128
    lane = lax.broadcasted_iota(jnp.int32, (1, 256), 1) + (start - h * HEAD_SIZE)
    own = jnp.where((lane >= 0) & (lane < HEAD_SIZE), 1.0, 0.0)
    return pl.ds(pl.multiple_of(start, 128), 256), own


def kept_half(bucket, positions):
    return jnp.where(bucket > 0, (positions - positions // 16) // 2, positions // 2)


def row_mask(count, slots):
    return jnp.where(lax.broadcasted_iota(jnp.int32, (slots, 1), 0) < count, 1.0, 0.0)


def placing(kept_row, positions):
    place = lax.broadcasted_iota(jnp.int32, (positions, kept_row.shape[1]), 0)
    return jnp.where(place == kept_row, 1.0, 0.0).astype(BF)


GELU_C = 0.7978845608028654


def gelu_pair(v):
    sq = v * v
    t = jnp.tanh(GELU_C * v * (1.0 + 0.044715 * sq))
    half = 0.5 + 0.5 * t
    slope = half + 0.5 * GELU_C * v * (1.0 - t * t) * (1.0 + 3 * 0.044715 * sq)
    return v * half, slope


class Steps:
    def __init__(self, rs):
        self.rs = rs
        self.links = len(rs.orders[0])

    def send_core(self, make=None):
        for m in range(self.rs.group - 1, 0, -2):
            if make is not None:
                make(m)
            for p in range(2):
                self.rs.send(m, p)

    def last_link(self, m):
        for p in range(2):
            if self.rs.top(m, p) == self.rs.orders[p][-1]:
                self.rs.fold(m, p)
                self.rs.send(m, p)

    def link(self, i):
        for p in range(2):
            order = self.rs.orders[p]
            for m in span(order[: i - 1]):
                self.rs.fold(m ^ order[i - 1], p)
                self.rs.send(m ^ order[i - 1], p)

    def finish(self, out, half):
        for p in range(2):
            total = self.rs.mine(0, p)[...].astype(F32)
            for key in self.rs.keys(0, p):
                self.rs.copy(key, p).wait_recv()
                total = total + self.rs.inbox(key, p)[...].astype(F32)
            out[p * half : (p + 1) * half] = total


def forward_kernel(
    dims, lat, bucket_ref, cond_ref, tok_ref, cot_in_ref, kept_ref, projb_ref, qvb_ref, adab_ref, expb_ref,
    wada_hbm, own_qkv, own_proj, own_1, own_2, *rest,
):
    outs, rest = rest[:14], rest[14:]
    kept, rest = rest[:13], rest[13:]
    (attn_in_o, q_o, k_o, v_o, merged_o, attn_out_o, hidden_o, cot_o, mod_o, din_o, zp_o, g1_o, g2_o) = kept
    (full, sm_send, sm_recv, nrm, sel, mg, mod8, all_1, all_2, d_all, xb, act, dpre, y, inbox, wexp, qvs,
     sm_ss, sm_rs, za_ss, za_rs, zm_ss, zm_rs, ga_ss, ga_rs, gd_ss, gd_rs, ag_ss, ag_rs, rs_ss, rs_rs, loc, out_sem) = rest
    full_o = outs[13]
    given = []

    def give(first, last):
        for k in range(first, last):
            cp = pltpu.make_async_copy(kept[k], outs[k], out_sem.at[k])
            cp.start()
            given.append(cp)

    group, count, rows_s, width = dims
    b, z = lax.axis_index("batch"), lax.axis_index("tp")
    g = b % group
    ds = width // count
    slots = kept_ref.shape[1]
    positions = tok_ref.shape[1]
    rows = lat * slots
    half = rows // 2
    cols = wada_hbm.shape[0]
    load_ada = pltpu.make_async_copy(wada_hbm, y.at[0:cols], loc.at[1])
    load_ada.start()
    hid_s = expb_ref.shape[0]
    if hid_s == width:
        wexp = y.at[0:width]
    load_exp = pltpu.make_async_copy(own_1, wexp, loc.at[2])
    real = [kept_half(bucket_ref[z * lat + l], positions) for l in range(lat)]
    barrier(b, z, group, count)

    cut = (rows_s // 2 + 15) // 16 * 16
    parts = ((0, cut), (cut, rows_s - cut))

    def piece(member, shard, p):
        at = member * rows_s
        lo, ln = parts[p] if p is not None else (0, rows_s)
        return full.at[at // ds, shard, pl.ds(at % ds + lo, ln)]

    own_copy = [
        pltpu.make_async_copy(own_qkv, full.at[0:3, z], loc.at[0]),
        pltpu.make_async_copy(own_proj, full.at[3, z], loc.at[5]),
    ]
    for cp in own_copy:
        cp.start()

    def line_a(shard, step, k, p):
        ref = piece(g, shard, p)
        return pltpu.make_async_remote_copy(
            src_ref=ref, dst_ref=ref, send_sem=za_ss.at[p, k], recv_sem=za_rs.at[p, shard],
            device_id=(b, z + step), device_id_type=MESH,
        )

    def line_m(shard, step, k, i):
        ref = (all_1, all_2)[i].at[shard]
        return pltpu.make_async_remote_copy(
            src_ref=ref, dst_ref=ref, send_sem=zm_ss.at[i, k], recv_sem=zm_rs.at[i, shard],
            device_id=(b, z + step), device_id_type=MESH,
        )

    def passes_on(shard):
        return ((shard < z) & (z < count - 1)) | ((shard > z) & (z > 0))

    def pass_on(shard, fn):
        @pl.when((shard < z) & (z < count - 1))
        def _():
            fn(1)

        @pl.when((shard > z) & (z > 0))
        def _():
            fn(-1)

    slice_at = pl.ds(pl.multiple_of(g * rows_s, 16), rows_s)
    own_m = [pltpu.make_async_copy(own_2.at[slice_at], all_2.at[z], loc.at[3])]
    for cp in own_m:
        cp.start()

    def both_ways(fn):
        @pl.when(z < count - 1)
        def _():
            fn(1, 0)

        @pl.when(z > 0)
        def _():
            fn(-1, 1)

    for cp in own_copy:
        cp.wait()
    def start_own_a(step, k):
        for p in range(2):
            line_a(z, step, k, p).start()

    both_ways(start_own_a)

    cond = cond_ref[...].astype(F32)
    silu = (cond / (1.0 + jnp.exp(-cond))).astype(BF)
    mod8[...] = jnp.zeros_like(mod8)
    mod8[:, 0:cols] = adab_ref[...].astype(F32).reshape(1, cols) + jnp.zeros((mod8.shape[0], cols), F32)
    qvs[...] = jnp.zeros_like(qvs)
    qvs[0:2, 0:ds] = qvb_ref[...].astype(F32)
    qv_own = pltpu.roll(qvs[...], z * ds, 1)[0:2]
    load_ada.wait()
    mod8[:, 0:cols] += nt(silu, y[0:cols])
    load_exp.start()
    framed = pltpu.roll(mod8[...], (z * cols) % width, 1)
    for t in range(count):
        for i in range(2):
            sm_send[t, i] = framed[lat * t : lat * (t + 1), i * width : (i + 1) * width]
        sm_send[t, 2] = qv_own

    def small(d):
        peer = lax.rem(z + d, count)
        return pltpu.make_async_remote_copy(
            src_ref=sm_send.at[peer], dst_ref=sm_recv.at[z], send_sem=sm_ss.at[d], recv_sem=sm_rs.at[d],
            device_id=(b, peer), device_id_type=MESH,
        )

    for d in range(1, count):
        small(d).start()
    small_own = pltpu.make_async_copy(sm_send.at[z], sm_recv.at[z], loc.at[6])
    small_own.start()

    for l in range(lat):
        pick = placing(kept_ref[l : l + 1], positions)
        at = slice(l * slots, (l + 1) * slots)
        picked = tn(pick, tok_ref[l])
        sel[at] = picked
        center, inv = stats(picked)
        nrm[at] = center * inv
        cot_o[at] = (tn(pick, cot_in_ref[l]) * row_mask(real[l], slots)).astype(BF)

    take = lax.broadcasted_iota(jnp.int32, (rows_s, hid_s), 1) - lax.broadcasted_iota(jnp.int32, (rows_s, hid_s), 0)
    take = jnp.where(take == g * rows_s, 1.0, 0.0).astype(BF)
    load_exp.wait()
    all_1[z, :, 0:width] = nt(take, wexp[...]).astype(BF)
    bias_row = jnp.where(
        lax.broadcasted_iota(jnp.int32, (128, 1), 0) == 0, expb_ref[...].astype(F32).reshape(1, hid_s), 0.0
    )
    all_1[z, :, width:] = nt(take, bias_row.astype(BF)).astype(BF)

    gathers = []
    for k in range(count - 1):
        shard = near_shard(z, k, count)

        def region(m, p, slot, shard=shard):
            return piece(flip(g, m), shard, p)

        gathers.append(
            Gather(b, z, group, region, lambda m, p, k=k: ga_ss.at[k, p, m], lambda m, p, shard=shard: ga_rs.at[shard, p, m])
        )

    def arrive_a(k):
        shard = near_shard(z, k, count)
        for p in range(2):
            line_a(shard, 0, 2 + k, p).wait_recv()
            pass_on(shard, lambda step, p=p: line_a(shard, step, 2 + k, p).start())
            gathers[k].step(0, p)

    four = count == 4
    inner = (z > 0) & (z < count - 1)
    across = lax.rem(z + 2, count)

    def far_m(i):
        return line_m(z, across - z, 2, i)

    def relay_m(i):
        return line_m(across, 2 * z - 3, 3, i)

    def arrive_m(k, i):
        if four:
            return
        shard = near_shard(z, k, count)

        @pl.when(passes_on(shard))
        def _():
            line_m(shard, 0, 2 + k, i).wait_recv()

        pass_on(shard, lambda step: line_m(shard, step, 2 + k, i).start())

    def send_far():
        if four:
            for i in range(2):
                far_m(i).start()

    def relay():
        if four:

            @pl.when(inner)
            def _():
                for i in range(2):
                    relay_m(i).wait_recv()
                    relay_m(i).start()

    def send_m(step, k):
        for i in range(2):
            line_m(z, step, k, i).start()

    ends = (z == 0) | (z == count - 1)
    arrive_a(0)
    for cp in own_m:
        cp.wait()

    @pl.when(ends)
    def _():
        send_far()
        both_ways(send_m)

    for d in range(1, count):
        peer = lax.rem(z + d, count)
        ref = sm_recv.at[lax.rem(z - d + count, count)]
        pltpu.make_async_remote_copy(
            src_ref=ref, dst_ref=ref, send_sem=sm_ss.at[d], recv_sem=sm_rs.at[d], device_id=(b, peer),
            device_id_type=MESH,
        ).wait_recv()
    small_own.wait()
    blocks = [None] * 6
    for t in range(count):
        first = t * cols // width
        for i in range(2):
            if first + i < 6:
                part = sm_recv[t, i]
                blocks[first + i] = part if blocks[first + i] is None else blocks[first + i] + part
    for i in range(6):
        mod_o[i] = blocks[i]
    qv_bias = sm_recv[0, 2]
    for t in range(1, count):
        qv_bias = qv_bias + sm_recv[t, 2]
    for l in range(lat):
        at = slice(l * slots, (l + 1) * slots)
        attn_in_o[at] = (nrm[at] * (1.0 + mod_o[1, l : l + 1]) + mod_o[0, l : l + 1]).astype(BF)
        d_all[0, at] = (cot_o[at].astype(F32) * mod_o[5, l : l + 1]).astype(BF)

    for k in range(1, count - 1):
        arrive_a(k)
        if k == 1:

            @pl.when(jnp.logical_not(ends))
            def _():
                both_ways(send_m)

        gathers[k - 1].step(1)
    depth = gathers[0].steps()
    todo = [(i, k) for k in range(count - 1) for i in range(1, depth) if not (i == 1 and k < count - 2)]
    def dm_region(m, p, slot):
        return d_all.at[slot, pl.ds(p * half, half)]

    dm = Gather(b, z, group, dm_region, lambda m, p: gd_ss.at[p, m], lambda m, p: gd_rs.at[p, m])
    links = depth - 1
    todo.sort(key=lambda item: (item[0] >= links, item[0] + item[1], item[1]))
    started = False
    for i, k in todo:
        if i >= links and not started:
            dm.step(0)

            @pl.when(inner)
            def _():
                send_far()

            arrive_m(0, 0)
            arrive_m(0, 1)
            started = True
        if (i, k) == todo[-1]:
            relay()
        gathers[k].step(i)
    for k in range(count - 1):
        gathers[k].wait_core()
    full_out = pltpu.make_async_copy(full, full_o, loc.at[4])
    full_out.start()

    if count > 2:
        arrive_m(1, 0)
        arrive_m(1, 1)
    dm.step(1)

    x = attn_in_o[...]
    for j, out in enumerate((q_o, k_o, v_o)):
        part_j = nt(x, full[j].reshape(width, width))
        if j != 1:
            part_j = part_j + qv_bias[j // 2 : j // 2 + 1]
        out[...] = part_j.astype(BF)

    scale = HEAD_SIZE**-0.5

    heads = width // HEAD_SIZE

    def some_heads(step, _):
        for h in (step, step + heads // 2):
            win, own = head_window(h, width)
            for l in range(lat):
                at = pl.ds(l * slots, slots)
                q = (q_o[at, win].astype(F32) * own).astype(BF)
                s = nt(q, k_o[at, win]) * scale
                key = lax.broadcasted_iota(jnp.int32, (1, slots), 1)
                s = jnp.where(key < real[l], s, -1000000000.0)
                w = jnp.exp(s - jnp.max(s, axis=-1, keepdims=True))
                pr = (w / jnp.sum(w, axis=-1, keepdims=True)).astype(BF)
                o = nn(pr, v_o[at, win])
                mg[at, win] = jnp.where(own > 0, o, mg[at, win])
        return 0

    lax.fori_loop(0, heads // 4, some_heads, 0)
    for k in range(2, count - 1):
        arrive_m(k, 0)
    for i in range(2, dm.steps()):
        dm.step(i)
    lax.fori_loop(heads // 4, heads // 2, some_heads, 0)
    for k in range(2, count - 1):
        arrive_m(k, 1)
    merged_o[...] = mg[...].astype(BF)
    a_out = nn(merged_o[...], full[3].reshape(width, width)) + projb_ref[...].astype(F32).reshape(1, width)
    attn_out_o[...] = a_out
    for l in range(lat):
        at = slice(l * slots, (l + 1) * slots)
        mixed = sel[at] + mod_o[2, l : l + 1] * attn_out_o[at]
        hidden_o[at] = mixed
        center, inv = stats(mixed)
        xb[0, at] = (center * inv * (1.0 + mod_o[4, l : l + 1]) + mod_o[3, l : l + 1]).astype(BF)

    give(0, 9)

    def part(ref):
        return lambda m, p: ref.at[m, pl.ds(p * half, half)]

    gather = Gather(
        b, z, group, lambda m, p, slot: part(xb)(slot, p), lambda m, p: ag_ss.at[p, m], lambda m, p: ag_rs.at[p, m]
    )
    gather.step(0)
    gather.step(1)
    for k in range(count - 1):
        shard = near_shard(z, k, count)

        @pl.when(jnp.logical_not(inner & (shard == across)) if four else jnp.logical_not(passes_on(shard)))
        def _():
            for i in range(2):
                line_m(shard, 0, 2 + k, i).wait_recv()

    hid = count * rows_s
    bias = nt(jnp.ones((8, all_1.shape[2] - width), BF), all_1[:, :, width:].reshape(hid, all_1.shape[2] - width))[0:1]

    def forward(pair):
        (m0, p0), (m1, p1) = pair
        at = [(m0, slice(p0 * half, (p0 + 1) * half)), (m1, slice(p1 * half, (p1 + 1) * half))]
        x = jnp.concatenate([xb[m, s] for m, s in at], axis=0)
        d = jnp.concatenate([d_all[m, s] for m, s in at], axis=0)
        a, slope = gelu_pair(nt(x, all_1[:, :, 0:width].reshape(hid, width)) + bias)
        dp = (slope * nt(d, all_2[...].reshape(hid, width))).astype(BF)
        a = a.astype(BF)
        for i, (m, s) in enumerate(at):
            to = slice(m * rows + s.start, m * rows + s.stop)
            act[to] = a[i * half : (i + 1) * half]
            dpre[to] = dp[i * half : (i + 1) * half]

    forward(((0, 0), (0, 1)))
    for p in range(2):
        gather.wait(1, p)
        dm.wait(1, p)
    forward(((1, 0), (1, 1)))
    links = gather.steps() - 1

    def fresh_pairs(i):
        fresh = [[m ^ order[i - 1] for m in span(order[: i - 1])] for order in gather.orders]
        return list(zip(*fresh))

    def forward_both(m0, m1):
        forward(((m0, 0), (m1, 1)))
        for item in (gather, dm):
            item.wait(m0 ^ 1, 0)
            item.wait(m1 ^ 1, 1)
        forward(((m0 ^ 1, 0), (m1 ^ 1, 1)))

    for i in range(1, links):
        for m0, m1 in fresh_pairs(i):
            forward_both(m0, m1)
        gather.step(i + 1)

    mine = lambda m, p: y.at[pl.ds(m * rows + p * half, half)]
    arrived = lambda m, p: inbox.at[m - 1, pl.ds(p * half, half)]

    def add(m, key, p):
        mine(m, p)[...] = (mine(m, p)[...].astype(F32) + arrived(key, p)[...].astype(F32)).astype(BF)

    rs = Steps(Scatter(b, z, group, mine, arrived, lambda m, p: rs_ss.at[p, m], lambda m, p: rs_rs.at[p, m], add))

    def part_in(m):
        at = slice(m * rows, (m + 1) * rows)
        y[at] = nn(dpre[at], all_1[:, :, 0:width].reshape(hid, width)).astype(BF)

    chunks = [slice(c, min(c + 128, hid)) for c in range(0, hid, 128)]
    def to_sibling(m):
        part_in(m)
        for p in range(2):
            rs.rs.send(m, p)

    whole = [m for m in range(group - 2, 0, -2) if all(rs.rs.top(m, p) == rs.rs.orders[p][-1] for p in range(2))]
    pairs = fresh_pairs(links)
    for m in whole:
        forward_both(m, m)
        to_sibling(m ^ 1)
        part_in(m)
        rs.last_link(m)
    for m0, m1 in pairs:
        if m0 not in whole:
            forward_both(m0, m1)
    for m in range(group - 1, 0, -2):
        if m ^ 1 not in whole:
            to_sibling(m)
    for m in range(group - 2, 0, -2):
        if m not in whole:
            part_in(m)
            rs.last_link(m)
    part_in(0)
    ones = jnp.ones((group * rows, g1_o.shape[1] - width), BF)
    for c in chunks:
        g1_o[c, 0:width] = tn(dpre[:, c], xb[...].reshape(group * rows, width)).astype(BF)
        g1_o[c, width:] = tn(dpre[:, c], ones).astype(BF)
    for i in range(rs.links - 1, 0, -1):
        rs.link(i)
    for c in chunks:
        g2_o[c] = tn(act[:, c], d_all[...].reshape(group * rows, width)).astype(BF)
    for m in range(group):
        zp_o[m] = nn(act[m * rows : (m + 1) * rows], all_2[...].reshape(hid, width)).astype(BF)
    give(10, 13)
    rs.finish(din_o, half)
    give(9, 10)
    gather.wait_sent()
    rs.rs.wait_sent()

    for d in range(1, count):
        small(d).wait_send()

    def sent_own(step, k):
        for i in range(2):
            line_a(z, step, k, i).wait_send()
            line_m(z, step, k, i).wait_send()

    both_ways(sent_own)
    if four:
        for i in range(2):
            far_m(i).wait_send()

        @pl.when(inner)
        def _():
            for i in range(2):
                relay_m(i).wait_send()

    for k in range(count - 1):
        shard = near_shard(z, k, count)

        @pl.when(passes_on(shard))
        def _():
            for i in range(2):
                line_a(shard, 0, 2 + k, i).wait_send()
                if not four:
                    line_m(shard, 0, 2 + k, i).wait_send()

        gathers[k].wait_sent()
    dm.wait_sent()
    full_out.wait()
    for cp in given:
        cp.wait()


def run_forward(dims, lat, bucket, cond, tok, cot, kept, projb, qvb, adab, expb, wada, own_qkv, own_proj, own_1, own_2):
    group, count, rows_s, width = dims
    slots = kept.shape[1]
    rows = lat * slots
    hid = count * rows_s
    ext = width + 128
    vm = pl.BlockSpec(memory_space=pltpu.VMEM)
    hb = pl.BlockSpec(memory_space=pl.ANY)
    sm = pl.BlockSpec(memory_space=pltpu.SMEM)
    sd = jax.ShapeDtypeStruct
    row_bf, row_f = sd((rows, width), BF), sd((rows, width), F32)
    blocks = sd((group, rows, width), BF)
    dma = pltpu.SemaphoreType.DMA
    vmem = pltpu.VMEM
    outs = (
        row_bf, row_bf, row_bf, row_bf, row_bf, row_f, row_f, row_bf, sd((6, lat, width), F32),
        row_f, blocks, sd((hid, ext), BF), sd((hid, width), BF), sd((4, count, width // count, width), BF),
    )
    return pl.pallas_call(
        functools.partial(forward_kernel, dims, lat),
        out_shape=outs,
        in_specs=[sm] + [vm] * 8 + [hb] * 5,
        out_specs=tuple([hb] * 14),
        scratch_shapes=[vmem(item.shape, item.dtype) for item in outs[:13]] + [
            vmem((4, count, width // count, width), BF),
            vmem((count, 3, lat, width), F32), vmem((count, 3, lat, width), F32),
            vmem((rows, width), F32), vmem((rows, width), F32), vmem((rows, width), F32),
            vmem((cond.shape[0], 2 * width), F32),
            vmem((count, rows_s, ext), BF), vmem((count, rows_s, width), BF),
            vmem((group, rows, width), BF), vmem((group, rows, width), BF),
            vmem((group * rows, hid), BF), vmem((group * rows, hid), BF),
            vmem((group * rows, width), BF), vmem((group - 1, rows, width), BF),
            vmem((16, 128) if own_1.shape[1] == width else own_1.shape, BF), vmem((8, width), F32),
            dma((count,)), dma((count,)),
            dma((2, count + 1)), dma((2, count)),
            dma((2, count + 1)), dma((2, count)),
            dma((count - 1, 2, group)), dma((count, 2, group)),
            dma((2, group)), dma((2, group)), dma((2, group)), dma((2, group)), dma((2, group)), dma((2, group)),
            dma((7,)), dma((14,)),
        ],
        compiler_params=pltpu.CompilerParams(collective_id=1, has_side_effects=True, vmem_limit_bytes=63 * MIB),
        name="forward_attention",
    )(bucket, cond, tok, cot, kept, projb, qvb, adab, expb, wada, own_qkv, own_proj, own_1, own_2)


def backward_kernel(dims, lat, bucket_ref, kept_ref, redb_ref, cond_ref, *rest):
    held, rest = rest[:12], rest[12:]
    (full_ref, g1_ref, g2_ref, zp_ref), rest = rest[:4], rest[4:]
    outs, rest = rest[:6], rest[6:]
    local, rest = rest[:12], rest[12:]
    (tok_ref, cot_in_ref, attn_in_ref, q_ref, k_ref, v_ref, merged_ref, attn_out_ref, hidden_ref, cot_ref, mod_ref,
     d_in_ref) = local
    (small_o, ga_o, gm1_o, gm2_o), rest = rest[:4], rest[4:]
    out_o, dtok_o, dain, mlp = tok_ref, cot_in_ref, d_in_ref, hidden_ref
    (wbuf, gbuf, abox, ar, gm1, gm2, mr1, mr2, back_b, d3, d_attn, dm, inbox, sm_send, sm_recv, dmod,
     loc, in_sem, out_sem, ro_ss, ro_rs, ra_ss, ra_rs, za_ss, za_rs, zm_ss, zm_rs, gm_ss, gm_rs, ga_ss, ga_rs, sz_ss, sz_rs,
     sp_ss, sp_rs) = rest
    takes = [pltpu.make_async_copy(held[k], local[k], in_sem.at[k]) for k in range(12)]

    def need(*which):
        for k in which:
            takes[k].wait()

    gives = [
        pltpu.make_async_copy(src, dst, out_sem.at[k])
        for k, (src, dst) in enumerate(zip((out_o, dtok_o, small_o, ga_o, gm1_o, gm2_o), outs))
    ]
    group, count, rows_s, width = dims
    b, z = lax.axis_index("batch"), lax.axis_index("tp")
    g = b % group
    ds = width // count
    slots = kept_ref.shape[1]
    positions = tok_ref.shape[1]
    rows = lat * slots
    half = rows // 2
    scale = HEAD_SIZE**-0.5
    loads = [
        pltpu.make_async_copy(g1_ref, gm1, loc.at[0]),
        pltpu.make_async_copy(g2_ref, gm2, loc.at[1]),
        pltpu.make_async_copy(full_ref.at[3], wbuf.at[0], loc.at[2]),
        pltpu.make_async_copy(full_ref.at[0], wbuf.at[1], loc.at[3]),
        pltpu.make_async_copy(zp_ref, gbuf.at[0 : group * rows], loc.at[5]),
    ]
    for cp in (loads[4], loads[0], loads[1], takes[8], takes[9], takes[10], takes[11], takes[7], loads[2]):
        cp.start()
    for k in (6, 3, 4, 5, 2, 0, 1):
        takes[k].start()
    loads[3].start()
    real = [kept_half(bucket_ref[z * lat + l], positions) for l in range(lat)]
    barrier(b, z, group, count)

    mine_out = lambda m, p: gbuf.at[pl.ds(m * rows + p * half, half)]
    box_out = lambda m, p: inbox.at[m - 1, pl.ds(p * half, half)]

    def add_out(m, key, p):
        mine_out(m, p)[...] = (mine_out(m, p)[...].astype(F32) + box_out(key, p)[...].astype(F32)).astype(BF)

    rs_out = Steps(
        Scatter(b, z, group, mine_out, box_out, lambda m, p: ro_ss.at[p, m], lambda m, p: ro_rs.at[p, m], add_out)
    )
    loads[4].wait()
    rs_out.send_core()
    cut = (rows_s // 2 + 15) // 16 * 16
    parts = ((0, cut), (cut, rows_s - cut))

    loads[0].wait()
    loads[1].wait()

    four = count == 4
    inner = (z > 0) & (z < count - 1)
    across = lax.rem(z + 2, count)
    sums = ((gm1, mr1), (gm2, mr2))

    def rows_for(shard):
        return pl.ds(pl.multiple_of(shard * rows_s, 16), rows_s)

    def line_m(shard, peer, box, k):
        return [
            pltpu.make_async_remote_copy(
                src_ref=src.at[rows_for(shard)], dst_ref=dst.at[box], send_sem=zm_ss.at[i, k], recv_sem=zm_rs.at[i, box],
                device_id=(b, peer), device_id_type=MESH,
            )
            for i, (src, dst) in enumerate(sums)
        ]

    def start(copies):
        for cp in copies:
            cp.start()

    def wait_in(box):
        for cp in line_m(z, z, box, 0):
            cp.wait_recv()

    def wait_out(copies):
        for cp in copies:
            cp.wait_send()

    def line_sends(fn):
        if not four:
            for d in range(1, count):
                peer = lax.rem(z + d, count)
                fn(line_m(peer, peer, d - 1, d - 1))
            return

        @pl.when(jnp.logical_not(inner))
        def _():
            fn(line_m(count - 1 - z, jnp.where(z == 0, 1, count - 2), 3, 3))
            fn(line_m(across, across, 2, 2))

        @pl.when(z < count - 1)
        def _():
            fn(line_m(z + 1, z + 1, 0, 0))

        @pl.when(z > 0)
        def _():
            fn(line_m(z - 1, z - 1, 1, 1))

    def line_relay(fn):
        if four:

            @pl.when(inner)
            def _():
                fn(line_m(across, across, 2, 2))

    def relay_add():
        if four:

            @pl.when(inner)
            def _():
                wait_in(3)
                for src, box in sums:
                    at = rows_for(across)
                    src[at] = (src[at].astype(F32) + box[3].astype(F32)).astype(BF)

        line_relay(start)

    def line_total():
        def take(box):
            wait_in(box)
            for src, boxes in sums:
                at = rows_for(z)
                src[at] = (src[at].astype(F32) + boxes[box].astype(F32)).astype(BF)

        if four:
            pl.when(z > 0)(lambda: take(0))
            pl.when(z < count - 1)(lambda: take(1))
            take(2)
        else:
            for d in range(count - 1):
                take(d)

    line_sends(start)

    def rows_of(l):
        return slice(l * slots, (l + 1) * slots)

    def back(n, inv, grad):
        return (grad - jnp.mean(grad, axis=-1, keepdims=True) - n * jnp.mean(grad * n, axis=-1, keepdims=True)) * inv

    def total(rows):
        return jnp.sum(rows, axis=0, keepdims=True)

    for m in range(group - 2, 0, -2):
        rs_out.last_link(m)
    need(7, 8, 9, 10, 11)
    for l in range(lat):
        at = rows_of(l)
        one = slice(l, l + 1)
        center, inv = stats(hidden_ref[at])
        n = center * inv
        d_in = d_in_ref[at]
        cot = cot_ref[at].astype(F32)
        back_b[at] = back(n, inv, d_in * (1.0 + mod_ref[4, one]))
        d_hidden = cot + back_b[at]
        d_attn[at] = (mod_ref[2, one] * d_hidden).astype(BF)
        dmod[3, one] = total(d_in)
        dmod[4, one] = total(d_in * n)
        dmod[2, one] = total(d_hidden * attn_out_ref[at])

    loads[2].wait()
    dm[...] = nt(d_attn[...], wbuf[0]).astype(BF)
    load_k = pltpu.make_async_copy(full_ref.at[1], wbuf.at[0], loc.at[2])
    load_k.start()
    chunk = 384

    def weight_grad(j, left, right):
        for c in range(0, width, chunk):
            to = slice(c, c + chunk)
            gbuf[j * width + c : j * width + c + chunk] = tn(left(to), right).astype(BF)

    need(6)
    weight_grad(3, lambda to: merged_ref[:, to], d_attn[...])

    heads = width // HEAD_SIZE

    def some_heads(step, _):
        for h in [step + i * (heads // 4) for i in range(4)]:
            win, own = head_window(h, width)
            for l in range(lat):
                at = pl.ds(l * slots, slots)
                q, k, v, dmh = q_ref[at, win], k_ref[at, win], v_ref[at, win], dm[at, win]
                s = nt((q.astype(F32) * own).astype(BF), k) * scale
                key = lax.broadcasted_iota(jnp.int32, (1, slots), 1)
                s = jnp.where(key < real[l], s, -1000000000.0)
                w = jnp.exp(s - jnp.max(s, axis=-1, keepdims=True))
                pr = w / jnp.sum(w, axis=-1, keepdims=True)
                dp = nt((dmh.astype(F32) * own).astype(BF), v)
                dsc = (pr * (dp - jnp.sum(pr * dp, axis=-1, keepdims=True))).astype(BF)
                for j, grad in enumerate(
                    (nn(dsc, k) * scale, tn(dsc, q) * scale, tn(pr.astype(BF), dmh))
                ):
                    d3[j, at, win] = jnp.where(own > 0, grad, d3[j, at, win].astype(F32)).astype(BF)
        return 0

    need(3, 4, 5)
    lax.fori_loop(0, heads // 8, some_heads, 0)
    for i in range(rs_out.links - 1, 0, -1):
        rs_out.link(i)
    relay_add()
    lax.fori_loop(heads // 8, heads // 4, some_heads, 0)
    rs_out.finish(mlp, half)
    mlp[...] += redb_ref[...].astype(F32).reshape(1, width)
    for l in range(lat):
        dmod[5, l : l + 1] = total(cot_ref[rows_of(l)].astype(F32) * mlp[rows_of(l)])
    rs_out.rs.wait_sent()

    need(2)
    for j in range(3):
        weight_grad(j, lambda to, j=j: d3[j, :, to], attn_in_ref[...])

    def wave_shard(w):
        return lax.rem(z + 1 + w, count)

    waves = []
    for w in range(count):
        def mine(m, p, w=w):
            at = flip(g, m) * rows_s
            lo, ln = parts[p]
            return gbuf.at[pl.ds(pl.multiple_of(at // ds * width + ds * wave_shard(w) + at % ds + lo, 16), ln)]

        def box(m, p, w=w):
            lo, ln = parts[p]
            return abox.at[w, m - 1, pl.ds(lo, ln)]

        def add(m, key, p, mine=mine, box=box):
            mine(m, p)[...] = (mine(m, p)[...].astype(F32) + box(key, p)[...].astype(F32)).astype(BF)

        waves.append(
            Scatter(b, z, group, mine, box, lambda m, p, w=w: ra_ss.at[w, p, m], lambda m, p, w=w: ra_rs.at[w, p, m], add)
        )
    links = len(waves[0].orders[0])

    def own_slice(shard):
        at = g * rows_s
        return gbuf.at[pl.ds(pl.multiple_of(at // ds * width + ds * shard + at % ds, 16), rows_s)]

    def line_a(w):
        return pltpu.make_async_remote_copy(
            src_ref=own_slice(wave_shard(w)), dst_ref=ar.at[w], send_sem=za_ss.at[w], recv_sem=za_rs.at[w],
            device_id=(b, wave_shard(w)), device_id_type=MESH,
        )

    def wave_step(w, st):
        rs = waves[w]
        if 0 <= st < links:
            for p in range(2):
                order = rs.orders[p]
                i = links - st
                for m in span(order[: i - 1]):
                    rs.fold(m ^ order[i - 1], p)
                    rs.send(m ^ order[i - 1], p)
        elif st == links:
            for p in range(2):
                rs.fold(0, p)
            if w < count - 1:
                line_a(w).start()

    for rs in waves:
        for m in range(group - 1, 0, -2):
            for p in range(2):
                rs.send(m, p)

    def wave_round(t):
        for w in reversed(range(count)):
            wave_step(w, t - w)

    loads[3].wait()
    dain[...] = nn(d3[0], wbuf[1])
    load_v = pltpu.make_async_copy(full_ref.at[2], wbuf.at[1], loc.at[3])
    load_v.start()
    wave_round(0)
    load_k.wait()
    dain[...] += nn(d3[1], wbuf[0])
    load_v.wait()
    dain[...] += nn(d3[2], wbuf[1])
    wave_round(1)

    def put(pick, rows):
        high = rows.astype(BF)
        return nn(pick, high) + nn(pick, (rows - high.astype(F32)).astype(BF))

    need(0, 1)
    for l in range(lat):
        at = rows_of(l)
        one = slice(l, l + 1)
        pick = placing(kept_ref[one], positions)
        center, inv = stats(tn(pick, tok_ref[l]))
        n = center * inv
        d_ai = dain[at]
        dmod[0, one] = total(d_ai)
        dmod[1, one] = total(d_ai * n)
        d_sel = back_b[at] + back(n, inv, d_ai * (1.0 + mod_ref[1, one]))
        dtok_o[l] = (cot_in_ref[l].astype(F32) + put(pick, d_sel)).astype(BF)

    gives[1].start()

    cols = 6 * width // count
    vectors = [
        sum(total((cot_ref[rows_of(l)].astype(F32) * mod_ref[5, l : l + 1]).astype(BF).astype(F32)) for l in range(lat)),
        total(d_attn[...].astype(F32)),
        total(d3[0].astype(F32)),
        total(d3[2].astype(F32)),
    ]
    for t in range(count):
        first = t * cols // width
        for i in range(2):
            sm_send[t, i] = dmod[min(first + i, 5)]
        for i in range(4):
            sm_send[t, 2 + i // 2, i % 2 : i % 2 + 1] = vectors[i]

    def small(d):
        peer = lax.rem(z + d, count)
        return pltpu.make_async_remote_copy(
            src_ref=sm_send.at[peer], dst_ref=sm_recv.at[z], send_sem=sz_ss.at[d], recv_sem=sz_rs.at[d],
            device_id=(b, peer), device_id_type=MESH,
        )

    for d in range(1, count):
        small(d).start()
    small_own = pltpu.make_async_copy(sm_send.at[z], sm_recv.at[z], loc.at[4])
    small_own.start()
    wave_round(2)
    for l in range(lat):
        at = rows_of(l)
        one = slice(l, l + 1)
        pick = placing(kept_ref[one], positions)
        delta = (mod_ref[2, one] * attn_out_ref[at] + mod_ref[5, one] * mlp[at]) * row_mask(real[l], slots)
        out_o[l] = (tok_ref[l].astype(F32) + put(pick, delta)).astype(BF)
    gives[0].start()
    def small_in():
        for d in range(1, count):
            ref = sm_recv.at[lax.rem(z - d + count, count)]
            pltpu.make_async_remote_copy(
                src_ref=ref, dst_ref=ref, send_sem=sz_ss.at[d], recv_sem=sz_rs.at[d],
                device_id=(b, lax.rem(z + d, count)), device_id_type=MESH,
            ).wait_recv()
        small_own.wait()
        small_o[0] = jnp.zeros(small_o.shape[1:], F32)
        for i in range(2):
            for t in range(count):
                small_o[0, i, lat * t : lat * (t + 1)] = sm_recv[t, i]
        for i in range(2):
            acc = sm_recv[0, 2 + i]
            for t in range(1, count):
                acc = acc + sm_recv[t, 2 + i]
            small_o[0, 2, lat * i : lat * (i + 1)] = acc
        cond = cond_ref[...].astype(F32)
        small_o[0, 3] = (cond / (1.0 + jnp.exp(-cond))).astype(BF).astype(F32)

    sp = Gather(
        b, z, group, lambda m, p, slot: small_o.at[slot], lambda m, p: sp_ss.at[m], lambda m, p: sp_rs.at[m], halves=1
    )

    def spread(out, ss, rs):
        def region(m, p, slot):
            lo, ln = parts[p]
            return out.at[pl.ds(pl.multiple_of(flip(g, m) * rows_s + lo, 16), ln)]

        return Gather(b, z, group, region, lambda m, p: ss.at[p, m], lambda m, p: rs.at[p, m])

    g_at = pl.ds(pl.multiple_of(g * rows_s, 16), rows_s)
    line_total()
    for own, out in ((gm1, gm1_o), (gm2, gm2_o)):
        out[g_at] = own[rows_for(z)]
    spread_1 = spread(gm1_o, gm_ss.at[0], gm_rs.at[0])
    spread_2 = spread(gm2_o, gm_ss.at[1], gm_rs.at[1])
    spread_1.step(0)
    spread_2.step(0)
    for t in range(3, count + links):
        wave_round(t)
        if t == 4:
            spread_1.step(1)
            spread_2.step(1)
            small_in()
            sp.step(0)
    acc = own_slice(z)[...].astype(F32)
    for w in range(count - 1):
        line_a(w).wait_recv()
        acc = acc + ar[w].astype(F32)
    ga_o[g_at] = acc.astype(BF)
    spread_a = spread(ga_o, ga_ss, ga_rs)
    spread_a.step(0)
    for i in range(1, spread_a.steps()):
        for item in (spread_1, spread_2):
            if i > 1:
                item.step(i)
        sp.step(i)
        spread_a.step(i)
    sp.wait_core()
    gives[2].start()
    for item, k in ((spread_1, 4), (spread_2, 5), (spread_a, 3)):
        item.wait_core()
        gives[k].start()
    for item in (sp, spread_a, spread_1, spread_2):
        item.wait_sent()
    for cp in gives:
        cp.wait()
    for rs in waves:
        rs.wait_sent()
    for w in range(count - 1):
        line_a(w).wait_send()
    for d in range(1, count):
        small(d).wait_send()
    line_sends(wait_out)
    line_relay(wait_out)


def run_backward(
    dims, lat, bucket, kept, tok, cot_in, attn_in, q, k, v, merged, attn_out, hidden, cot, mod, d_in, redb, cond,
    full, g1, g2, zp,
):
    group, count, rows_s, width = dims
    rows = attn_in.shape[0]
    vm = pl.BlockSpec(memory_space=pltpu.VMEM)
    hb = pl.BlockSpec(memory_space=pl.ANY)
    sm = pl.BlockSpec(memory_space=pltpu.SMEM)
    sd = jax.ShapeDtypeStruct
    dma = pltpu.SemaphoreType.DMA
    vmem = pltpu.VMEM
    ext = g1.shape[1]
    boxes = max(4, count - 1)
    small = (group, 4, cond.shape[0], width)
    held = (tok, cot_in, attn_in, q, k, v, merged, attn_out, hidden, cot, mod, d_in)
    return pl.pallas_call(
        functools.partial(backward_kernel, dims, lat),
        out_shape=(
            sd(tok.shape, BF), sd(tok.shape, BF), sd(small, F32),
            sd((group * rows_s, width), BF), sd((group * rows_s, ext), BF), sd((group * rows_s, width), BF),
        ),
        in_specs=[sm] + [vm] * 3 + [hb] * 16,
        out_specs=tuple([hb] * 6),
        scratch_shapes=[vmem(item.shape, item.dtype) for item in held] + [
            vmem(small, F32), vmem((group * rows_s, width), BF), vmem((group * rows_s, ext), BF),
            vmem((group * rows_s, width), BF),
            vmem((2, width, width), BF),
            vmem((4 * width, width), BF),
            vmem((count, group - 1, rows_s, width), BF),
            vmem((count - 1, rows_s, width), BF),
            vmem(g1.shape, BF), vmem(g2.shape, BF),
            vmem((boxes, rows_s, ext), BF), vmem((boxes, rows_s, width), BF),
            vmem((rows, width), F32),
            vmem((3, rows, width), BF),
            vmem((rows, width), BF), vmem((rows, width), BF),
            vmem((group - 1, rows, width), BF),
            vmem((count, 4, lat, width), F32), vmem((count, 4, lat, width), F32),
            vmem((6, lat, width), F32),
            dma((6,)), dma((12,)), dma((6,)),
            dma((2, group)), dma((2, group)),
            dma((count, 2, group)), dma((count, 2, group)),
            dma((count,)), dma((count,)),
            dma((2, boxes)), dma((2, boxes)),
            dma((2, 2, group)), dma((2, 2, group)),
            dma((2, group)), dma((2, group)),
            dma((count,)), dma((count,)),
            dma((group,)), dma((group,)),
        ],
        compiler_params=pltpu.CompilerParams(collective_id=3, has_side_effects=True, vmem_limit_bytes=63 * MIB),
        name="backward_attention",
    )(bucket, kept, redb, cond, *held, full, g1, g2, zp)


def widen_kernel(dims, ga_h, gm1_h, gm2_h, small_h, out_h, dtok_h, out_o, dtok_o, qkv_o, proj_o, exp_o, red_o, ada_o, adab_o, pair_o, projb_o, redb_o, expb_o,
                 ga_ref, gm1_ref, gm2_ref, small_ref, out_ref, dtok_ref, qkv, proj, exp, red, ada, sem):
    group, count, rows_s, width = dims
    ds = width // count
    cols = ada.shape[0]
    members = small_ref.shape[0] * small_ref.shape[2]
    z = lax.axis_index("tp")

    def move(src, dst, k):
        cp = pltpu.make_async_copy(src, dst, sem.at[k])
        cp.start()
        return cp

    loads = [
        move(gm2_h, gm2_ref, 6), move(small_h, small_ref, 5), move(gm1_h, gm1_ref, 7), move(ga_h, ga_ref, 8),
        move(out_h, out_ref, 9), move(dtok_h, dtok_ref, 10),
    ]

    def item(k):
        return small_ref[:, k].reshape(members, width)

    loads[0].wait()
    red[...] = gm2_ref[...].astype(F32)
    done = [move(red, red_o, 1)]
    loads[1].wait()
    pair = jnp.concatenate([item(0), item(1)], axis=1)
    start = lax.rem(z * cols, width)
    pair = pltpu.roll(pair, lax.rem(2 * width - start, 2 * width), 1)[:, 0:cols]
    ada[...] = tn(pair.astype(BF), item(3).astype(BF))
    done.append(move(ada, ada_o, 0))
    loads[2].wait()
    exp[...] = gm1_ref[:, 0:width].T.astype(F32)
    done.append(move(exp, exp_o, 2))
    loads[3].wait()
    qkv[...] = ga_ref[0 : 3 * ds].astype(F32)
    done.append(move(qkv, qkv_o, 3))
    proj[...] = ga_ref[3 * ds :].astype(F32)
    done.append(move(proj, proj_o, 4))
    loads[4].wait()
    done.append(move(out_ref, out_o, 11))
    loads[5].wait()
    done.append(move(dtok_ref, dtok_o, 12))
    adab_o[...] = jnp.sum(pair, axis=0)
    acc = small_ref[0, 2]
    for i in range(1, small_ref.shape[0]):
        acc = acc + small_ref[i, 2]
    redb_o[...] = acc[0]
    projb_o[...] = acc[1]
    pair_o[...] = pltpu.roll(acc, lax.rem(width - z * ds, width), 1)[2:4, 0:ds]
    corner = lax.broadcasted_iota(jnp.int32, (8, 1), 0) + lax.broadcasted_iota(jnp.int32, (1, 128), 1)
    expb_o[...] = nt(jnp.where(corner == 0, 1.0, 0.0).astype(BF), gm1_ref[:, width:])[0]
    for cp in done:
        cp.wait()


def run_widen(dims, cols, ga, gm1, gm2, small, output, tokens_grad):
    group, count, rows_s, width = dims
    ds = width // count
    vm = pl.BlockSpec(memory_space=pltpu.VMEM)
    hb = pl.BlockSpec(memory_space=pl.ANY)
    hid_s = gm1.shape[0]
    big = [(3 * ds, width), (ds, width), (width, hid_s), gm2.shape, (cols, width)]
    vecs = [(cols,), (2, ds), (width,), (width,), (hid_s,)]
    given = (ga, gm1, gm2, small, output, tokens_grad)
    rows = jax.ShapeDtypeStruct(output.shape, BF)
    return pl.pallas_call(
        functools.partial(widen_kernel, dims),
        out_shape=(rows, rows) + tuple(jax.ShapeDtypeStruct(item, F32) for item in big + vecs),
        in_specs=[hb] * 6,
        out_specs=tuple([hb] * 7 + [vm] * 5),
        scratch_shapes=[pltpu.VMEM(item.shape, item.dtype) for item in given]
        + [pltpu.VMEM(item, F32) for item in big]
        + [pltpu.SemaphoreType.DMA((13,))],
        compiler_params=pltpu.CompilerParams(vmem_limit_bytes=60 * MIB),
        name="widen_gradients",
    )(*given)


def body(
    tokens, conditioning, bucket, kept_index, w_ada, ada_bias, w_qkv, qv_bias, w_proj, proj_bias,
    w_expand, expand_bias, w_reduce, reduce_bias, out_grad, count, batch,
):
    lat, positions, width = tokens.shape
    shard_w, shard_f = w_qkv.shape[2], w_expand.shape[1]
    group = group_size(shard_f, shard_w)
    dims = (group, count, shard_f // group, width)
    cols = ada_bias.shape[0]

    (attn_in, queries, key_rows, value_rows, merged, attn_out, hidden, cot, mod, d_in, zp, g1, g2, full) = run_forward(
        dims, lat, bucket, conditioning, tokens, out_grad, kept_index, proj_bias, qv_bias, ada_bias, expand_bias,
        w_ada.T, jnp.swapaxes(w_qkv, 1, 2), w_proj, w_expand, w_reduce,
    )
    output, tokens_grad, small, ga, gm1, gm2 = run_backward(
        dims, lat, bucket, kept_index, tokens, out_grad, attn_in, queries, key_rows, value_rows, merged,
        attn_out, hidden, cot, mod, d_in, reduce_bias, conditioning,
        full.reshape(4, width, width), g1, g2, zp.reshape(-1, width),
    )

    def over_batch(items):
        if batch > group:
            return tuple(lax.psum(item * (1.0 / group), "batch") for item in items)
        return items

    ga, gm1, gm2 = over_batch((ga, gm1, gm2))
    output, tokens_grad, qkv_grad, proj_grad, expand_grad, reduce_grad, *sums = run_widen(
        dims, cols, ga, gm1, gm2, small, output, tokens_grad
    )
    ada_grad, ada_add, pair_grad, proj_add, reduce_add = over_batch(tuple(sums[:5]))
    return (
        output,
        tokens_grad,
        ada_grad.T,
        ada_add,
        jnp.swapaxes(qkv_grad.reshape(3, shard_w, width), 1, 2),
        pair_grad,
        proj_grad,
        proj_add,
        expand_grad,
        sums[5],
        reduce_grad,
        reduce_add,
    )


def solution(mesh):
    rows = P(("batch", "tp"), None, None)
    return jax.shard_map(
        functools.partial(body, count=mesh.shape["tp"], batch=mesh.shape["batch"]),
        mesh=mesh,
        in_specs=(
            rows, P("batch", None), P("batch"), P(("batch", "tp"), None), P(None, "tp"), P("tp"),
            P(None, None, "tp"), P(None, "tp"), P("tp", None), P(), P(None, "tp"), P("tp"), P("tp", None), P(), rows,
        ),
        out_specs=(
            rows, rows, P(None, "tp"), P("tp"), P(None, None, "tp"), P(None, "tp"), P("tp", None), P(),
            P(None, "tp"), P("tp"), P("tp", None), P(),
        ),
        check_vma=False,
    )
```

```python
import functools
import jax
import jax.numpy as jnp
from jax import lax
from jax.experimental import pallas as pl
from jax.experimental.pallas import tpu as pltpu
from jax.sharding import PartitionSpec as P

HEAD_SIZE = 72
EPS = 1e-06
F32 = jnp.float32
BF = jnp.bfloat16
MESH = pl.DeviceIdType.MESH
MIB = 2**20


def nn(a, b):
    return lax.dot_general(a, b, (((1,), (0,)), ((), ())), preferred_element_type=F32)


def nt(a, b):
    return lax.dot_general(a, b, (((1,), (1,)), ((), ())), preferred_element_type=F32)


def tn(a, b):
    return lax.dot_general(a, b, (((0,), (0,)), ((), ())), preferred_element_type=F32)


def flip(b, mask):
    out, bit = b, 1
    while bit <= mask:
        if mask & bit:
            out = out + bit - 2 * bit * ((b // bit) % 2)
        bit *= 2
    return out


def group_size(ff_shard, width_shard):
    for size in (8, 4, 2):
        rows = ff_shard // size
        if ff_shard % size == 0 and rows % 16 == 0 and 4 * width_shard == size * rows:
            return size
    raise ValueError("no group")


def link_orders(group):
    bits = []
    bit = 2
    while bit < group:
        bits.append(bit)
        bit *= 2
    return bits, bits[::-1]


def span(bits):
    out = [0]
    for bit in bits:
        out = out + [item ^ bit for item in out]
    return out


def near_shard(z, k, count):
    low = jnp.minimum(z, count - 1 - z)
    both = z + (k // 2 + 1) * (1 - 2 * (k % 2))
    one = z + jnp.where(2 * z < count - 1, 1, -1) * (k - low + 1)
    return jnp.where(k < 2 * low, both, one)


class Gather:
    def __init__(self, b, z, group, region, send_sem, recv_sem, halves=2):
        self.b, self.z = b, z
        self.region, self.send_sem, self.recv_sem = region, send_sem, recv_sem
        self.orders = link_orders(group)[:halves] if halves == 2 else link_orders(group)[:1]
        self.group = group
        self.sent = []

    def copy(self, m, bit, p):
        return pltpu.make_async_remote_copy(
            src_ref=self.region(m, p, m),
            dst_ref=self.region(m, p, m ^ bit),
            send_sem=self.send_sem(m ^ bit, p),
            recv_sem=self.recv_sem(m ^ bit, p),
            device_id=(flip(self.b, bit), self.z),
            device_id_type=MESH,
        )

    def send(self, m, bit, p):
        cp = self.copy(m, bit, p)
        cp.start()
        self.sent.append(cp)

    def wait(self, m, p):
        ref = self.region(m, p, m)
        pltpu.make_async_remote_copy(
            src_ref=ref, dst_ref=ref, send_sem=self.send_sem(m, p), recv_sem=self.recv_sem(m, p),
            device_id=(flip(self.b, 1), self.z), device_id_type=MESH,
        ).wait_recv()

    def step(self, i, only=None):
        for p, order in enumerate(self.orders):
            if only is not None and p != only:
                continue
            if i == 0:
                fresh = [0]
            elif i <= len(order):
                fresh = [item ^ order[i - 1] for item in span(order[: i - 1])]
                for m in fresh:
                    self.wait(m, p)
            else:
                continue
            if i < len(order):
                for m in span(order[:i]):
                    self.send(m, order[i], p)
            for m in fresh:
                self.send(m, 1, p)

    def steps(self):
        return len(self.orders[0]) + 1

    def wait_core(self, m=None):
        for p in range(len(self.orders)):
            for item in range(1, self.group, 2):
                if m is None or item == m:
                    self.wait(item, p)

    def wait_sent(self):
        for cp in self.sent:
            cp.wait_send()


class Scatter:
    def __init__(self, b, z, group, mine, inbox, send_sem, recv_sem, add):
        self.b, self.z, self.group = b, z, group
        self.mine, self.inbox, self.add = mine, inbox, add
        self.send_sem, self.recv_sem = send_sem, recv_sem
        self.orders = link_orders(group)
        self.sent = []

    def top(self, m, p):
        if m & 1:
            return 1
        for bit in reversed(self.orders[p]):
            if m & bit:
                return bit

    def copy(self, m, p):
        return pltpu.make_async_remote_copy(
            src_ref=self.mine(m, p),
            dst_ref=self.inbox(m, p),
            send_sem=self.send_sem(m, p),
            recv_sem=self.recv_sem(m, p),
            device_id=(flip(self.b, self.top(m, p)), self.z),
            device_id_type=MESH,
        )

    def keys(self, m, p):
        if m & 1:
            return []
        out = [m ^ 1]
        order = self.orders[p]
        above = order if m == 0 else order[order.index(self.top(m, p)) + 1 :]
        return out + [m ^ bit for bit in reversed(above)]

    def fold(self, m, p):
        for key in self.keys(m, p):
            self.copy(key, p).wait_recv()
            self.add(m, key, p)

    def send(self, m, p):
        cp = self.copy(m, p)
        cp.start()
        self.sent.append(cp)

    def wait_sent(self):
        for cp in self.sent:
            cp.wait_send()


def barrier(b, z, group, count):
    sem = pltpu.get_barrier_semaphore()
    for m in range(1, group):
        pl.semaphore_signal(sem, 1, device_id=(flip(b, m), z), device_id_type=MESH)
    for d in range(1, count):
        pl.semaphore_signal(sem, 1, device_id=(b, lax.rem(z + d, count)), device_id_type=MESH)
    pl.semaphore_wait(sem, group - 1 + count - 1)


def stats(rows):
    center = rows - jnp.mean(rows, axis=-1, keepdims=True)
    return center, lax.rsqrt(jnp.mean(center * center, axis=-1, keepdims=True) + EPS)


def head_window(h, width):
    start = jnp.minimum(h * HEAD_SIZE // 128, width // 128 - 2) * 128
    lane = lax.broadcasted_iota(jnp.int32, (1, 256), 1) + (start - h * HEAD_SIZE)
    own = jnp.where((lane >= 0) & (lane < HEAD_SIZE), 1.0, 0.0)
    return pl.ds(pl.multiple_of(start, 128), 256), own


def kept_half(bucket, positions):
    return jnp.where(bucket > 0, (positions - positions // 16) // 2, positions // 2)


def row_mask(count, slots):
    return jnp.where(lax.broadcasted_iota(jnp.int32, (slots, 1), 0) < count, 1.0, 0.0)


def placing(kept_row, positions):
    place = lax.broadcasted_iota(jnp.int32, (positions, kept_row.shape[1]), 0)
    return jnp.where(place == kept_row, 1.0, 0.0).astype(BF)


GELU_C = 0.7978845608028654


def gelu_pair(v):
    sq = v * v
    t = jnp.tanh(GELU_C * v * (1.0 + 0.044715 * sq))
    half = 0.5 + 0.5 * t
    slope = half + 0.5 * GELU_C * v * (1.0 - t * t) * (1.0 + 3 * 0.044715 * sq)
    return v * half, slope


class Steps:
    def __init__(self, rs):
        self.rs = rs
        self.links = len(rs.orders[0])

    def send_core(self, make=None):
        for m in range(self.rs.group - 1, 0, -2):
            if make is not None:
                make(m)
            for p in range(2):
                self.rs.send(m, p)

    def last_link(self, m):
        for p in range(2):
            if self.rs.top(m, p) == self.rs.orders[p][-1]:
                self.rs.fold(m, p)
                self.rs.send(m, p)

    def link(self, i):
        for p in range(2):
            order = self.rs.orders[p]
            for m in span(order[: i - 1]):
                self.rs.fold(m ^ order[i - 1], p)
                self.rs.send(m ^ order[i - 1], p)

    def finish(self, out, half):
        for p in range(2):
            total = self.rs.mine(0, p)[...].astype(F32)
            for key in self.rs.keys(0, p):
                self.rs.copy(key, p).wait_recv()
                total = total + self.rs.inbox(key, p)[...].astype(F32)
            out[p * half : (p + 1) * half] = total


def forward_kernel(
    dims, lat, bucket_ref, cond_ref, tok_ref, cot_in_ref, kept_ref, projb_ref, qvb_ref, adab_ref, expb_ref,
    wada_hbm, own_qkv, own_proj, own_1, own_2, *rest,
):
    outs, rest = rest[:14], rest[14:]
    kept, rest = rest[:13], rest[13:]
    (attn_in_o, q_o, k_o, v_o, merged_o, attn_out_o, hidden_o, cot_o, mod_o, din_o, zp_o, g1_o, g2_o) = kept
    (full, sm_send, sm_recv, nrm, sel, mg, mod8, all_1, all_2, d_all, xb, act, dpre, y, inbox, wexp, qvs,
     sm_ss, sm_rs, za_ss, za_rs, zm_ss, zm_rs, ga_ss, ga_rs, gd_ss, gd_rs, ag_ss, ag_rs, rs_ss, rs_rs, loc, out_sem) = rest
    full_o = outs[13]
    given = []

    def give(first, last):
        for k in range(first, last):
            cp = pltpu.make_async_copy(kept[k], outs[k], out_sem.at[k])
            cp.start()
            given.append(cp)

    group, count, rows_s, width = dims
    b, z = lax.axis_index("batch"), lax.axis_index("tp")
    g = b % group
    ds = width // count
    slots = kept_ref.shape[1]
    positions = tok_ref.shape[1]
    rows = lat * slots
    half = rows // 2
    cols = wada_hbm.shape[0]
    load_ada = pltpu.make_async_copy(wada_hbm, y.at[0:cols], loc.at[1])
    load_ada.start()
    hid_s = expb_ref.shape[0]
    if hid_s == width:
        wexp = y.at[0:width]
    load_exp = pltpu.make_async_copy(own_1, wexp, loc.at[2])
    real = [kept_half(bucket_ref[z * lat + l], positions) for l in range(lat)]
    barrier(b, z, group, count)

    cut = (rows_s // 2 + 15) // 16 * 16
    parts = ((0, cut), (cut, rows_s - cut))

    def piece(member, shard, p):
        at = member * rows_s
        lo, ln = parts[p] if p is not None else (0, rows_s)
        return full.at[at // ds, shard, pl.ds(at % ds + lo, ln)]

    own_copy = [
        pltpu.make_async_copy(own_qkv, full.at[0:3, z], loc.at[0]),
        pltpu.make_async_copy(own_proj, full.at[3, z], loc.at[5]),
    ]
    for cp in own_copy:
        cp.start()

    def line_a(shard, step, k, p):
        ref = piece(g, shard, p)
        return pltpu.make_async_remote_copy(
            src_ref=ref, dst_ref=ref, send_sem=za_ss.at[p, k], recv_sem=za_rs.at[p, shard],
            device_id=(b, z + step), device_id_type=MESH,
        )

    def line_m(shard, step, k, i):
        ref = (all_1, all_2)[i].at[shard]
        return pltpu.make_async_remote_copy(
            src_ref=ref, dst_ref=ref, send_sem=zm_ss.at[i, k], recv_sem=zm_rs.at[i, shard],
            device_id=(b, z + step), device_id_type=MESH,
        )

    def passes_on(shard):
        return ((shard < z) & (z < count - 1)) | ((shard > z) & (z > 0))

    def pass_on(shard, fn):
        @pl.when((shard < z) & (z < count - 1))
        def _():
            fn(1)

        @pl.when((shard > z) & (z > 0))
        def _():
            fn(-1)

    slice_at = pl.ds(pl.multiple_of(g * rows_s, 16), rows_s)
    own_m = [pltpu.make_async_copy(own_2.at[slice_at], all_2.at[z], loc.at[3])]
    for cp in own_m:
        cp.start()

    def both_ways(fn):
        @pl.when(z < count - 1)
        def _():
            fn(1, 0)

        @pl.when(z > 0)
        def _():
            fn(-1, 1)

    for cp in own_copy:
        cp.wait()
    def start_own_a(step, k):
        for p in range(2):
            line_a(z, step, k, p).start()

    both_ways(start_own_a)

    cond = cond_ref[...].astype(F32)
    silu = (cond / (1.0 + jnp.exp(-cond))).astype(BF)
    mod8[...] = jnp.zeros_like(mod8)
    mod8[:, 0:cols] = adab_ref[...].astype(F32).reshape(1, cols) + jnp.zeros((mod8.shape[0], cols), F32)
    qvs[...] = jnp.zeros_like(qvs)
    qvs[0:2, 0:ds] = qvb_ref[...].astype(F32)
    qv_own = pltpu.roll(qvs[...], z * ds, 1)[0:2]
    load_ada.wait()
    mod8[:, 0:cols] += nt(silu, y[0:cols])
    load_exp.start()
    framed = pltpu.roll(mod8[...], (z * cols) % width, 1)
    for t in range(count):
        for i in range(2):
            sm_send[t, i] = framed[lat * t : lat * (t + 1), i * width : (i + 1) * width]
        sm_send[t, 2] = qv_own

    def small(d):
        peer = lax.rem(z + d, count)
        return pltpu.make_async_remote_copy(
            src_ref=sm_send.at[peer], dst_ref=sm_recv.at[z], send_sem=sm_ss.at[d], recv_sem=sm_rs.at[d],
            device_id=(b, peer), device_id_type=MESH,
        )

    for d in range(1, count):
        small(d).start()
    small_own = pltpu.make_async_copy(sm_send.at[z], sm_recv.at[z], loc.at[6])
    small_own.start()

    for l in range(lat):
        pick = placing(kept_ref[l : l + 1], positions)
        at = slice(l * slots, (l + 1) * slots)
        picked = tn(pick, tok_ref[l])
        sel[at] = picked
        center, inv = stats(picked)
        nrm[at] = center * inv
        cot_o[at] = (tn(pick, cot_in_ref[l]) * row_mask(real[l], slots)).astype(BF)

    take = lax.broadcasted_iota(jnp.int32, (rows_s, hid_s), 1) - lax.broadcasted_iota(jnp.int32, (rows_s, hid_s), 0)
    take = jnp.where(take == g * rows_s, 1.0, 0.0).astype(BF)
    load_exp.wait()
    all_1[z, :, 0:width] = nt(take, wexp[...]).astype(BF)
    bias_row = jnp.where(
        lax.broadcasted_iota(jnp.int32, (128, 1), 0) == 0, expb_ref[...].astype(F32).reshape(1, hid_s), 0.0
    )
    all_1[z, :, width:] = nt(take, bias_row.astype(BF)).astype(BF)

    gathers = []
    for k in range(count - 1):
        shard = near_shard(z, k, count)

        def region(m, p, slot, shard=shard):
            return piece(flip(g, m), shard, p)

        gathers.append(
            Gather(b, z, group, region, lambda m, p, k=k: ga_ss.at[k, p, m], lambda m, p, shard=shard: ga_rs.at[shard, p, m])
        )

    def arrive_a(k):
        shard = near_shard(z, k, count)
        for p in range(2):
            line_a(shard, 0, 2 + k, p).wait_recv()
            pass_on(shard, lambda step, p=p: line_a(shard, step, 2 + k, p).start())
            gathers[k].step(0, p)

    four = count == 4
    inner = (z > 0) & (z < count - 1)
    across = lax.rem(z + 2, count)

    def far_m(i):
        return line_m(z, across - z, 2, i)

    def relay_m(i):
        return line_m(across, 2 * z - 3, 3, i)

    def arrive_m(k, i):
        if four:
            return
        shard = near_shard(z, k, count)

        @pl.when(passes_on(shard))
        def _():
            line_m(shard, 0, 2 + k, i).wait_recv()

        pass_on(shard, lambda step: line_m(shard, step, 2 + k, i).start())

    def send_far():
        if four:
            for i in range(2):
                far_m(i).start()

    def relay():
        if four:

            @pl.when(inner)
            def _():
                for i in range(2):
                    relay_m(i).wait_recv()
                    relay_m(i).start()

    def send_m(step, k):
        for i in range(2):
            line_m(z, step, k, i).start()

    ends = (z == 0) | (z == count - 1)
    arrive_a(0)
    for cp in own_m:
        cp.wait()

    @pl.when(ends)
    def _():
        both_ways(send_m)

    for d in range(1, count):
        peer = lax.rem(z + d, count)
        ref = sm_recv.at[lax.rem(z - d + count, count)]
        pltpu.make_async_remote_copy(
            src_ref=ref, dst_ref=ref, send_sem=sm_ss.at[d], recv_sem=sm_rs.at[d], device_id=(b, peer),
            device_id_type=MESH,
        ).wait_recv()
    small_own.wait()
    blocks = [None] * 6
    for t in range(count):
        first = t * cols // width
        for i in range(2):
            if first + i < 6:
                part = sm_recv[t, i]
                blocks[first + i] = part if blocks[first + i] is None else blocks[first + i] + part
    for i in range(6):
        mod_o[i] = blocks[i]
    qv_bias = sm_recv[0, 2]
    for t in range(1, count):
        qv_bias = qv_bias + sm_recv[t, 2]
    for l in range(lat):
        at = slice(l * slots, (l + 1) * slots)
        attn_in_o[at] = (nrm[at] * (1.0 + mod_o[1, l : l + 1]) + mod_o[0, l : l + 1]).astype(BF)
        d_all[0, at] = (cot_o[at].astype(F32) * mod_o[5, l : l + 1]).astype(BF)

    for k in range(1, count - 1):
        arrive_a(k)
        if k == count - 2:

            @pl.when(jnp.logical_not(ends))
            def _():
                both_ways(send_m)

            send_far()

        gathers[k - 1].step(1)
    depth = gathers[0].steps()
    todo = [(i, k) for k in range(count - 1) for i in range(1, depth) if not (i == 1 and k < count - 2)]
    def dm_region(m, p, slot):
        return d_all.at[slot, pl.ds(p * half, half)]

    dm = Gather(b, z, group, dm_region, lambda m, p: gd_ss.at[p, m], lambda m, p: gd_rs.at[p, m])
    links = depth - 1
    todo.sort(key=lambda item: (item[0] >= links, item[0] + item[1], item[1]))
    started = False
    for i, k in todo:
        if i >= links and not started:
            dm.step(0)

            arrive_m(0, 0)
            arrive_m(0, 1)
            started = True
        if (i, k) == todo[-1]:
            relay()
        gathers[k].step(i)
    for k in range(count - 1):
        gathers[k].wait_core()
    full_out = pltpu.make_async_copy(full, full_o, loc.at[4])
    full_out.start()

    if count > 2:
        arrive_m(1, 0)
        arrive_m(1, 1)
    dm.step(1)

    x = attn_in_o[...]
    for j, out in enumerate((q_o, k_o, v_o)):
        part_j = nt(x, full[j].reshape(width, width))
        if j != 1:
            part_j = part_j + qv_bias[j // 2 : j // 2 + 1]
        out[...] = part_j.astype(BF)

    scale = HEAD_SIZE**-0.5

    heads = width // HEAD_SIZE

    def some_heads(step, _):
        for h in (step, step + heads // 2):
            win, own = head_window(h, width)
            for l in range(lat):
                at = pl.ds(l * slots, slots)
                q = (q_o[at, win].astype(F32) * own).astype(BF)
                s = nt(q, k_o[at, win]) * scale
                key = lax.broadcasted_iota(jnp.int32, (1, slots), 1)
                s = jnp.where(key < real[l], s, -1000000000.0)
                w = jnp.exp(s - jnp.max(s, axis=-1, keepdims=True))
                pr = (w / jnp.sum(w, axis=-1, keepdims=True)).astype(BF)
                o = nn(pr, v_o[at, win])
                mg[at, win] = jnp.where(own > 0, o, mg[at, win])
        return 0

    lax.fori_loop(0, heads // 4, some_heads, 0)
    for k in range(2, count - 1):
        arrive_m(k, 0)
    for i in range(2, dm.steps()):
        dm.step(i)
    lax.fori_loop(heads // 4, heads // 2, some_heads, 0)
    for k in range(2, count - 1):
        arrive_m(k, 1)
    merged_o[...] = mg[...].astype(BF)
    a_out = nn(merged_o[...], full[3].reshape(width, width)) + projb_ref[...].astype(F32).reshape(1, width)
    attn_out_o[...] = a_out
    for l in range(lat):
        at = slice(l * slots, (l + 1) * slots)
        mixed = sel[at] + mod_o[2, l : l + 1] * attn_out_o[at]
        hidden_o[at] = mixed
        center, inv = stats(mixed)
        xb[0, at] = (center * inv * (1.0 + mod_o[4, l : l + 1]) + mod_o[3, l : l + 1]).astype(BF)

    give(0, 9)

    def part(ref):
        return lambda m, p: ref.at[m, pl.ds(p * half, half)]

    gather = Gather(
        b, z, group, lambda m, p, slot: part(xb)(slot, p), lambda m, p: ag_ss.at[p, m], lambda m, p: ag_rs.at[p, m]
    )
    gather.step(0)
    gather.step(1)
    for k in range(count - 1):
        shard = near_shard(z, k, count)

        @pl.when(jnp.logical_not(inner & (shard == across)) if four else jnp.logical_not(passes_on(shard)))
        def _():
            for i in range(2):
                line_m(shard, 0, 2 + k, i).wait_recv()

    hid = count * rows_s
    bias = nt(jnp.ones((8, all_1.shape[2] - width), BF), all_1[:, :, width:].reshape(hid, all_1.shape[2] - width))[0:1]

    def forward(pair):
        (m0, p0), (m1, p1) = pair
        at = [(m0, slice(p0 * half, (p0 + 1) * half)), (m1, slice(p1 * half, (p1 + 1) * half))]
        x = jnp.concatenate([xb[m, s] for m, s in at], axis=0)
        d = jnp.concatenate([d_all[m, s] for m, s in at], axis=0)
        a, slope = gelu_pair(nt(x, all_1[:, :, 0:width].reshape(hid, width)) + bias)
        dp = (slope * nt(d, all_2[...].reshape(hid, width))).astype(BF)
        a = a.astype(BF)
        for i, (m, s) in enumerate(at):
            to = slice(m * rows + s.start, m * rows + s.stop)
            act[to] = a[i * half : (i + 1) * half]
            dpre[to] = dp[i * half : (i + 1) * half]

    forward(((0, 0), (0, 1)))
    for p in range(2):
        gather.wait(1, p)
        dm.wait(1, p)
    forward(((1, 0), (1, 1)))
    links = gather.steps() - 1

    def fresh_pairs(i):
        fresh = [[m ^ order[i - 1] for m in span(order[: i - 1])] for order in gather.orders]
        return list(zip(*fresh))

    def forward_both(m0, m1):
        forward(((m0, 0), (m1, 1)))
        for item in (gather, dm):
            item.wait(m0 ^ 1, 0)
            item.wait(m1 ^ 1, 1)
        forward(((m0 ^ 1, 0), (m1 ^ 1, 1)))

    for i in range(1, links):
        for m0, m1 in fresh_pairs(i):
            forward_both(m0, m1)
        gather.step(i + 1)

    mine = lambda m, p: y.at[pl.ds(m * rows + p * half, half)]
    arrived = lambda m, p: inbox.at[m - 1, pl.ds(p * half, half)]

    def add(m, key, p):
        mine(m, p)[...] = (mine(m, p)[...].astype(F32) + arrived(key, p)[...].astype(F32)).astype(BF)

    rs = Steps(Scatter(b, z, group, mine, arrived, lambda m, p: rs_ss.at[p, m], lambda m, p: rs_rs.at[p, m], add))

    def part_in(m):
        at = slice(m * rows, (m + 1) * rows)
        y[at] = nn(dpre[at], all_1[:, :, 0:width].reshape(hid, width)).astype(BF)

    chunks = [slice(c, min(c + 128, hid)) for c in range(0, hid, 128)]
    def to_sibling(m):
        part_in(m)
        for p in range(2):
            rs.rs.send(m, p)

    whole = [m for m in range(group - 2, 0, -2) if all(rs.rs.top(m, p) == rs.rs.orders[p][-1] for p in range(2))]
    pairs = fresh_pairs(links)
    for m in whole:
        forward_both(m, m)
        to_sibling(m ^ 1)
        part_in(m)
        rs.last_link(m)
    for m0, m1 in pairs:
        if m0 not in whole:
            forward_both(m0, m1)
    for m in range(group - 1, 0, -2):
        if m ^ 1 not in whole:
            to_sibling(m)
    for m in range(group - 2, 0, -2):
        if m not in whole:
            part_in(m)
            rs.last_link(m)
    part_in(0)
    ones = jnp.ones((group * rows, g1_o.shape[1] - width), BF)
    for c in chunks:
        g1_o[c, 0:width] = tn(dpre[:, c], xb[...].reshape(group * rows, width)).astype(BF)
        g1_o[c, width:] = tn(dpre[:, c], ones).astype(BF)
    for i in range(rs.links - 1, 0, -1):
        rs.link(i)
    for c in chunks:
        g2_o[c] = tn(act[:, c], d_all[...].reshape(group * rows, width)).astype(BF)
    for m in range(group):
        zp_o[m] = nn(act[m * rows : (m + 1) * rows], all_2[...].reshape(hid, width)).astype(BF)
    give(10, 13)
    rs.finish(din_o, half)
    give(9, 10)
    gather.wait_sent()
    rs.rs.wait_sent()

    for d in range(1, count):
        small(d).wait_send()

    def sent_own(step, k):
        for i in range(2):
            line_a(z, step, k, i).wait_send()
            line_m(z, step, k, i).wait_send()

    both_ways(sent_own)
    if four:
        for i in range(2):
            far_m(i).wait_send()

        @pl.when(inner)
        def _():
            for i in range(2):
                relay_m(i).wait_send()

    for k in range(count - 1):
        shard = near_shard(z, k, count)

        @pl.when(passes_on(shard))
        def _():
            for i in range(2):
                line_a(shard, 0, 2 + k, i).wait_send()
                if not four:
                    line_m(shard, 0, 2 + k, i).wait_send()

        gathers[k].wait_sent()
    dm.wait_sent()
    full_out.wait()
    for cp in given:
        cp.wait()


def run_forward(dims, lat, bucket, cond, tok, cot, kept, projb, qvb, adab, expb, wada, own_qkv, own_proj, own_1, own_2):
    group, count, rows_s, width = dims
    slots = kept.shape[1]
    rows = lat * slots
    hid = count * rows_s
    ext = width + 128
    vm = pl.BlockSpec(memory_space=pltpu.VMEM)
    hb = pl.BlockSpec(memory_space=pl.ANY)
    sm = pl.BlockSpec(memory_space=pltpu.SMEM)
    sd = jax.ShapeDtypeStruct
    row_bf, row_f = sd((rows, width), BF), sd((rows, width), F32)
    blocks = sd((group, rows, width), BF)
    dma = pltpu.SemaphoreType.DMA
    vmem = pltpu.VMEM
    outs = (
        row_bf, row_bf, row_bf, row_bf, row_bf, row_f, row_f, row_bf, sd((6, lat, width), F32),
        row_f, blocks, sd((hid, ext), BF), sd((hid, width), BF), sd((4, count, width // count, width), BF),
    )
    return pl.pallas_call(
        functools.partial(forward_kernel, dims, lat),
        out_shape=outs,
        in_specs=[sm] + [vm] * 8 + [hb] * 5,
        out_specs=tuple([hb] * 14),
        scratch_shapes=[vmem(item.shape, item.dtype) for item in outs[:13]] + [
            vmem((4, count, width // count, width), BF),
            vmem((count, 3, lat, width), F32), vmem((count, 3, lat, width), F32),
            vmem((rows, width), F32), vmem((rows, width), F32), vmem((rows, width), F32),
            vmem((cond.shape[0], 2 * width), F32),
            vmem((count, rows_s, ext), BF), vmem((count, rows_s, width), BF),
            vmem((group, rows, width), BF), vmem((group, rows, width), BF),
            vmem((group * rows, hid), BF), vmem((group * rows, hid), BF),
            vmem((group * rows, width), BF), vmem((group - 1, rows, width), BF),
            vmem((16, 128) if own_1.shape[1] == width else own_1.shape, BF), vmem((8, width), F32),
            dma((count,)), dma((count,)),
            dma((2, count + 1)), dma((2, count)),
            dma((2, count + 1)), dma((2, count)),
            dma((count - 1, 2, group)), dma((count, 2, group)),
            dma((2, group)), dma((2, group)), dma((2, group)), dma((2, group)), dma((2, group)), dma((2, group)),
            dma((7,)), dma((14,)),
        ],
        compiler_params=pltpu.CompilerParams(collective_id=1, has_side_effects=True, vmem_limit_bytes=63 * MIB),
        name="forward_attention",
    )(bucket, cond, tok, cot, kept, projb, qvb, adab, expb, wada, own_qkv, own_proj, own_1, own_2)


def backward_kernel(dims, lat, bucket_ref, kept_ref, redb_ref, cond_ref, *rest):
    held, rest = rest[:12], rest[12:]
    (full_ref, g1_ref, g2_ref, zp_ref), rest = rest[:4], rest[4:]
    outs, rest = rest[:6], rest[6:]
    local, rest = rest[:12], rest[12:]
    (tok_ref, cot_in_ref, attn_in_ref, q_ref, k_ref, v_ref, merged_ref, attn_out_ref, hidden_ref, cot_ref, mod_ref,
     d_in_ref) = local
    (small_o, ga_o, gm1_o, gm2_o), rest = rest[:4], rest[4:]
    out_o, dtok_o, dain, mlp = tok_ref, cot_in_ref, d_in_ref, hidden_ref
    (wbuf, gbuf, abox, ar, gm1, gm2, mr1, mr2, back_b, d3, d_attn, dm, inbox, sm_send, sm_recv, dmod,
     loc, in_sem, out_sem, ro_ss, ro_rs, ra_ss, ra_rs, za_ss, za_rs, zm_ss, zm_rs, gm_ss, gm_rs, ga_ss, ga_rs, sz_ss, sz_rs,
     sp_ss, sp_rs) = rest
    takes = [pltpu.make_async_copy(held[k], local[k], in_sem.at[k]) for k in range(12)]

    def need(*which):
        for k in which:
            takes[k].wait()

    gives = [
        pltpu.make_async_copy(src, dst, out_sem.at[k])
        for k, (src, dst) in enumerate(zip((out_o, dtok_o, small_o, ga_o, gm1_o, gm2_o), outs))
    ]
    group, count, rows_s, width = dims
    b, z = lax.axis_index("batch"), lax.axis_index("tp")
    g = b % group
    ds = width // count
    slots = kept_ref.shape[1]
    positions = tok_ref.shape[1]
    rows = lat * slots
    half = rows // 2
    scale = HEAD_SIZE**-0.5
    loads = [
        pltpu.make_async_copy(g1_ref, gm1, loc.at[0]),
        pltpu.make_async_copy(g2_ref, gm2, loc.at[1]),
        pltpu.make_async_copy(full_ref.at[3], wbuf.at[0], loc.at[2]),
        pltpu.make_async_copy(full_ref.at[0], wbuf.at[1], loc.at[3]),
        pltpu.make_async_copy(zp_ref, gbuf.at[0 : group * rows], loc.at[5]),
    ]
    for cp in (loads[4], loads[0], loads[1], takes[8], takes[9], takes[10], takes[11], takes[7], loads[2]):
        cp.start()
    for k in (6, 3, 4, 5, 2, 0, 1):
        takes[k].start()
    loads[3].start()
    real = [kept_half(bucket_ref[z * lat + l], positions) for l in range(lat)]
    barrier(b, z, group, count)

    mine_out = lambda m, p: gbuf.at[pl.ds(m * rows + p * half, half)]
    box_out = lambda m, p: inbox.at[m - 1, pl.ds(p * half, half)]

    def add_out(m, key, p):
        mine_out(m, p)[...] = (mine_out(m, p)[...].astype(F32) + box_out(key, p)[...].astype(F32)).astype(BF)

    rs_out = Steps(
        Scatter(b, z, group, mine_out, box_out, lambda m, p: ro_ss.at[p, m], lambda m, p: ro_rs.at[p, m], add_out)
    )
    loads[4].wait()
    rs_out.send_core()
    cut = (rows_s // 2 + 15) // 16 * 16
    parts = ((0, cut), (cut, rows_s - cut))

    loads[0].wait()
    loads[1].wait()

    four = count == 4
    inner = (z > 0) & (z < count - 1)
    across = lax.rem(z + 2, count)
    sums = ((gm1, mr1), (gm2, mr2))

    def rows_for(shard):
        return pl.ds(pl.multiple_of(shard * rows_s, 16), rows_s)

    def line_m(shard, peer, box, k):
        return [
            pltpu.make_async_remote_copy(
                src_ref=src.at[rows_for(shard)], dst_ref=dst.at[box], send_sem=zm_ss.at[i, k], recv_sem=zm_rs.at[i, box],
                device_id=(b, peer), device_id_type=MESH,
            )
            for i, (src, dst) in enumerate(sums)
        ]

    def start(copies):
        for cp in copies:
            cp.start()

    def wait_in(box):
        for cp in line_m(z, z, box, 0):
            cp.wait_recv()

    def wait_out(copies):
        for cp in copies:
            cp.wait_send()

    def line_sends(fn):
        if not four:
            for d in range(1, count):
                peer = lax.rem(z + d, count)
                fn(line_m(peer, peer, d - 1, d - 1))
            return

        @pl.when(jnp.logical_not(inner))
        def _():
            fn(line_m(count - 1 - z, jnp.where(z == 0, 1, count - 2), 3, 3))
            fn(line_m(across, across, 2, 2))

        @pl.when(z < count - 1)
        def _():
            fn(line_m(z + 1, z + 1, 0, 0))

        @pl.when(z > 0)
        def _():
            fn(line_m(z - 1, z - 1, 1, 1))

    def line_relay(fn):
        if four:

            @pl.when(inner)
            def _():
                fn(line_m(across, across, 2, 2))

    def relay_add():
        if four:

            @pl.when(inner)
            def _():
                wait_in(3)
                for src, box in sums:
                    at = rows_for(across)
                    src[at] = (src[at].astype(F32) + box[3].astype(F32)).astype(BF)

        line_relay(start)

    def line_total():
        def take(box):
            wait_in(box)
            for src, boxes in sums:
                at = rows_for(z)
                src[at] = (src[at].astype(F32) + boxes[box].astype(F32)).astype(BF)

        if four:
            pl.when(z > 0)(lambda: take(0))
            pl.when(z < count - 1)(lambda: take(1))
            take(2)
        else:
            for d in range(count - 1):
                take(d)

    line_sends(start)

    def rows_of(l):
        return slice(l * slots, (l + 1) * slots)

    def back(n, inv, grad):
        return (grad - jnp.mean(grad, axis=-1, keepdims=True) - n * jnp.mean(grad * n, axis=-1, keepdims=True)) * inv

    def total(rows):
        return jnp.sum(rows, axis=0, keepdims=True)

    for m in range(group - 2, 0, -2):
        rs_out.last_link(m)
    need(7, 8, 9, 10, 11)
    for l in range(lat):
        at = rows_of(l)
        one = slice(l, l + 1)
        center, inv = stats(hidden_ref[at])
        n = center * inv
        d_in = d_in_ref[at]
        cot = cot_ref[at].astype(F32)
        back_b[at] = back(n, inv, d_in * (1.0 + mod_ref[4, one]))
        d_hidden = cot + back_b[at]
        d_attn[at] = (mod_ref[2, one] * d_hidden).astype(BF)
        dmod[3, one] = total(d_in)
        dmod[4, one] = total(d_in * n)
        dmod[2, one] = total(d_hidden * attn_out_ref[at])

    loads[2].wait()
    dm[...] = nt(d_attn[...], wbuf[0]).astype(BF)
    load_k = pltpu.make_async_copy(full_ref.at[1], wbuf.at[0], loc.at[2])
    load_k.start()
    chunk = 384

    def weight_grad(j, left, right):
        for c in range(0, width, chunk):
            to = slice(c, c + chunk)
            gbuf[j * width + c : j * width + c + chunk] = tn(left(to), right).astype(BF)

    need(6)
    weight_grad(3, lambda to: merged_ref[:, to], d_attn[...])

    heads = width // HEAD_SIZE

    def some_heads(step, _):
        for h in [step + i * (heads // 4) for i in range(4)]:
            win, own = head_window(h, width)
            for l in range(lat):
                at = pl.ds(l * slots, slots)
                q, k, v, dmh = q_ref[at, win], k_ref[at, win], v_ref[at, win], dm[at, win]
                s = nt((q.astype(F32) * own).astype(BF), k) * scale
                key = lax.broadcasted_iota(jnp.int32, (1, slots), 1)
                s = jnp.where(key < real[l], s, -1000000000.0)
                w = jnp.exp(s - jnp.max(s, axis=-1, keepdims=True))
                pr = w / jnp.sum(w, axis=-1, keepdims=True)
                dp = nt((dmh.astype(F32) * own).astype(BF), v)
                dsc = (pr * (dp - jnp.sum(pr * dp, axis=-1, keepdims=True))).astype(BF)
                for j, grad in enumerate(
                    (nn(dsc, k) * scale, tn(dsc, q) * scale, tn(pr.astype(BF), dmh))
                ):
                    d3[j, at, win] = jnp.where(own > 0, grad, d3[j, at, win].astype(F32)).astype(BF)
        return 0

    need(3, 4, 5)
    lax.fori_loop(0, heads // 8, some_heads, 0)
    for i in range(rs_out.links - 1, 0, -1):
        rs_out.link(i)
    relay_add()
    lax.fori_loop(heads // 8, heads // 4, some_heads, 0)
    rs_out.finish(mlp, half)
    mlp[...] += redb_ref[...].astype(F32).reshape(1, width)
    for l in range(lat):
        dmod[5, l : l + 1] = total(cot_ref[rows_of(l)].astype(F32) * mlp[rows_of(l)])
    rs_out.rs.wait_sent()

    need(2)
    for j in range(3):
        weight_grad(j, lambda to, j=j: d3[j, :, to], attn_in_ref[...])

    def wave_shard(w):
        return lax.rem(z + 1 + w, count)

    waves = []
    for w in range(count):
        def mine(m, p, w=w):
            at = flip(g, m) * rows_s
            lo, ln = parts[p]
            return gbuf.at[pl.ds(pl.multiple_of(at // ds * width + ds * wave_shard(w) + at % ds + lo, 16), ln)]

        def box(m, p, w=w):
            lo, ln = parts[p]
            return abox.at[w, m - 1, pl.ds(lo, ln)]

        def add(m, key, p, mine=mine, box=box):
            mine(m, p)[...] = (mine(m, p)[...].astype(F32) + box(key, p)[...].astype(F32)).astype(BF)

        waves.append(
            Scatter(b, z, group, mine, box, lambda m, p, w=w: ra_ss.at[w, p, m], lambda m, p, w=w: ra_rs.at[w, p, m], add)
        )
    links = len(waves[0].orders[0])

    def own_slice(shard):
        at = g * rows_s
        return gbuf.at[pl.ds(pl.multiple_of(at // ds * width + ds * shard + at % ds, 16), rows_s)]

    def line_a(w):
        return pltpu.make_async_remote_copy(
            src_ref=own_slice(wave_shard(w)), dst_ref=ar.at[w], send_sem=za_ss.at[w], recv_sem=za_rs.at[w],
            device_id=(b, wave_shard(w)), device_id_type=MESH,
        )

    def wave_step(w, st):
        rs = waves[w]
        if 0 <= st < links:
            for p in range(2):
                order = rs.orders[p]
                i = links - st
                for m in span(order[: i - 1]):
                    rs.fold(m ^ order[i - 1], p)
                    rs.send(m ^ order[i - 1], p)
        elif st == links:
            for p in range(2):
                rs.fold(0, p)
            if w < count - 1:
                line_a(w).start()

    for rs in waves:
        for m in range(group - 1, 0, -2):
            for p in range(2):
                rs.send(m, p)

    def wave_round(t):
        for w in reversed(range(count)):
            wave_step(w, t - w)

    loads[3].wait()
    dain[...] = nn(d3[0], wbuf[1])
    load_v = pltpu.make_async_copy(full_ref.at[2], wbuf.at[1], loc.at[3])
    load_v.start()
    wave_round(0)
    load_k.wait()
    dain[...] += nn(d3[1], wbuf[0])
    load_v.wait()
    dain[...] += nn(d3[2], wbuf[1])
    wave_round(1)

    def put(pick, rows):
        high = rows.astype(BF)
        return nn(pick, high) + nn(pick, (rows - high.astype(F32)).astype(BF))

    need(0, 1)
    for l in range(lat):
        at = rows_of(l)
        one = slice(l, l + 1)
        pick = placing(kept_ref[one], positions)
        center, inv = stats(tn(pick, tok_ref[l]))
        n = center * inv
        d_ai = dain[at]
        dmod[0, one] = total(d_ai)
        dmod[1, one] = total(d_ai * n)
        d_sel = back_b[at] + back(n, inv, d_ai * (1.0 + mod_ref[1, one]))
        dtok_o[l] = (cot_in_ref[l].astype(F32) + put(pick, d_sel)).astype(BF)

    gives[1].start()

    cols = 6 * width // count
    vectors = [
        sum(total((cot_ref[rows_of(l)].astype(F32) * mod_ref[5, l : l + 1]).astype(BF).astype(F32)) for l in range(lat)),
        total(d_attn[...].astype(F32)),
        total(d3[0].astype(F32)),
        total(d3[2].astype(F32)),
    ]
    for t in range(count):
        first = t * cols // width
        for i in range(2):
            sm_send[t, i] = dmod[min(first + i, 5)]
        for i in range(4):
            sm_send[t, 2 + i // 2, i % 2 : i % 2 + 1] = vectors[i]

    def small(d):
        peer = lax.rem(z + d, count)
        return pltpu.make_async_remote_copy(
            src_ref=sm_send.at[peer], dst_ref=sm_recv.at[z], send_sem=sz_ss.at[d], recv_sem=sz_rs.at[d],
            device_id=(b, peer), device_id_type=MESH,
        )

    for d in range(1, count):
        small(d).start()
    small_own = pltpu.make_async_copy(sm_send.at[z], sm_recv.at[z], loc.at[4])
    small_own.start()
    wave_round(2)
    for l in range(lat):
        at = rows_of(l)
        one = slice(l, l + 1)
        pick = placing(kept_ref[one], positions)
        delta = (mod_ref[2, one] * attn_out_ref[at] + mod_ref[5, one] * mlp[at]) * row_mask(real[l], slots)
        out_o[l] = (tok_ref[l].astype(F32) + put(pick, delta)).astype(BF)
    gives[0].start()
    def small_in():
        for d in range(1, count):
            ref = sm_recv.at[lax.rem(z - d + count, count)]
            pltpu.make_async_remote_copy(
                src_ref=ref, dst_ref=ref, send_sem=sz_ss.at[d], recv_sem=sz_rs.at[d],
                device_id=(b, lax.rem(z + d, count)), device_id_type=MESH,
            ).wait_recv()
        small_own.wait()
        small_o[0] = jnp.zeros(small_o.shape[1:], F32)
        for i in range(2):
            for t in range(count):
                small_o[0, i, lat * t : lat * (t + 1)] = sm_recv[t, i]
        for i in range(2):
            acc = sm_recv[0, 2 + i]
            for t in range(1, count):
                acc = acc + sm_recv[t, 2 + i]
            small_o[0, 2, lat * i : lat * (i + 1)] = acc
        cond = cond_ref[...].astype(F32)
        small_o[0, 3] = (cond / (1.0 + jnp.exp(-cond))).astype(BF).astype(F32)

    sp = Gather(
        b, z, group, lambda m, p, slot: small_o.at[slot], lambda m, p: sp_ss.at[m], lambda m, p: sp_rs.at[m], halves=1
    )

    def spread(out, ss, rs):
        def region(m, p, slot):
            lo, ln = parts[p]
            return out.at[pl.ds(pl.multiple_of(flip(g, m) * rows_s + lo, 16), ln)]

        return Gather(b, z, group, region, lambda m, p: ss.at[p, m], lambda m, p: rs.at[p, m])

    g_at = pl.ds(pl.multiple_of(g * rows_s, 16), rows_s)
    line_total()
    for own, out in ((gm1, gm1_o), (gm2, gm2_o)):
        out[g_at] = own[rows_for(z)]
    spread_1 = spread(gm1_o, gm_ss.at[0], gm_rs.at[0])
    spread_2 = spread(gm2_o, gm_ss.at[1], gm_rs.at[1])
    spread_1.step(0)
    spread_2.step(0)
    for t in range(3, count + links):
        wave_round(t)
        if t == 4:
            spread_1.step(1)
            spread_2.step(1)
            small_in()
            sp.step(0)
    acc = own_slice(z)[...].astype(F32)
    for w in range(count - 1):
        line_a(w).wait_recv()
        acc = acc + ar[w].astype(F32)
    ga_o[g_at] = acc.astype(BF)
    spread_a = spread(ga_o, ga_ss, ga_rs)
    spread_a.step(0)
    for i in range(1, spread_a.steps()):
        for item in (spread_1, spread_2):
            if i > 1:
                item.step(i)
        sp.step(i)
        spread_a.step(i)
    sp.wait_core()
    gives[2].start()
    for item, k in ((spread_1, 4), (spread_2, 5), (spread_a, 3)):
        item.wait_core()
        gives[k].start()
    for item in (sp, spread_a, spread_1, spread_2):
        item.wait_sent()
    for cp in gives:
        cp.wait()
    for rs in waves:
        rs.wait_sent()
    for w in range(count - 1):
        line_a(w).wait_send()
    for d in range(1, count):
        small(d).wait_send()
    line_sends(wait_out)
    line_relay(wait_out)


def run_backward(
    dims, lat, bucket, kept, tok, cot_in, attn_in, q, k, v, merged, attn_out, hidden, cot, mod, d_in, redb, cond,
    full, g1, g2, zp,
):
    group, count, rows_s, width = dims
    rows = attn_in.shape[0]
    vm = pl.BlockSpec(memory_space=pltpu.VMEM)
    hb = pl.BlockSpec(memory_space=pl.ANY)
    sm = pl.BlockSpec(memory_space=pltpu.SMEM)
    sd = jax.ShapeDtypeStruct
    dma = pltpu.SemaphoreType.DMA
    vmem = pltpu.VMEM
    ext = g1.shape[1]
    boxes = max(4, count - 1)
    small = (group, 4, cond.shape[0], width)
    held = (tok, cot_in, attn_in, q, k, v, merged, attn_out, hidden, cot, mod, d_in)
    return pl.pallas_call(
        functools.partial(backward_kernel, dims, lat),
        out_shape=(
            sd(tok.shape, BF), sd(tok.shape, BF), sd(small, F32),
            sd((group * rows_s, width), BF), sd((group * rows_s, ext), BF), sd((group * rows_s, width), BF),
        ),
        in_specs=[sm] + [vm] * 3 + [hb] * 16,
        out_specs=tuple([hb] * 6),
        scratch_shapes=[vmem(item.shape, item.dtype) for item in held] + [
            vmem(small, F32), vmem((group * rows_s, width), BF), vmem((group * rows_s, ext), BF),
            vmem((group * rows_s, width), BF),
            vmem((2, width, width), BF),
            vmem((4 * width, width), BF),
            vmem((count, group - 1, rows_s, width), BF),
            vmem((count - 1, rows_s, width), BF),
            vmem(g1.shape, BF), vmem(g2.shape, BF),
            vmem((boxes, rows_s, ext), BF), vmem((boxes, rows_s, width), BF),
            vmem((rows, width), F32),
            vmem((3, rows, width), BF),
            vmem((rows, width), BF), vmem((rows, width), BF),
            vmem((group - 1, rows, width), BF),
            vmem((count, 4, lat, width), F32), vmem((count, 4, lat, width), F32),
            vmem((6, lat, width), F32),
            dma((6,)), dma((12,)), dma((6,)),
            dma((2, group)), dma((2, group)),
            dma((count, 2, group)), dma((count, 2, group)),
            dma((count,)), dma((count,)),
            dma((2, boxes)), dma((2, boxes)),
            dma((2, 2, group)), dma((2, 2, group)),
            dma((2, group)), dma((2, group)),
            dma((count,)), dma((count,)),
            dma((group,)), dma((group,)),
        ],
        compiler_params=pltpu.CompilerParams(collective_id=3, has_side_effects=True, vmem_limit_bytes=63 * MIB),
        name="backward_attention",
    )(bucket, kept, redb, cond, *held, full, g1, g2, zp)


def widen_kernel(dims, ga_h, gm1_h, gm2_h, small_h, out_h, dtok_h, out_o, dtok_o, qkv_o, proj_o, exp_o, red_o, ada_o, adab_o, pair_o, projb_o, redb_o, expb_o,
                 ga_ref, gm1_ref, gm2_ref, small_ref, out_ref, dtok_ref, qkv, proj, exp, red, ada, sem):
    group, count, rows_s, width = dims
    ds = width // count
    cols = ada.shape[0]
    members = small_ref.shape[0] * small_ref.shape[2]
    z = lax.axis_index("tp")

    def move(src, dst, k):
        cp = pltpu.make_async_copy(src, dst, sem.at[k])
        cp.start()
        return cp

    loads = [
        move(gm2_h, gm2_ref, 6), move(small_h, small_ref, 5), move(gm1_h, gm1_ref, 7), move(ga_h, ga_ref, 8),
        move(out_h, out_ref, 9), move(dtok_h, dtok_ref, 10),
    ]

    def item(k):
        return small_ref[:, k].reshape(members, width)

    loads[0].wait()
    red[...] = gm2_ref[...].astype(F32)
    done = [move(red, red_o, 1)]
    loads[1].wait()
    pair = jnp.concatenate([item(0), item(1)], axis=1)
    start = lax.rem(z * cols, width)
    pair = pltpu.roll(pair, lax.rem(2 * width - start, 2 * width), 1)[:, 0:cols]
    ada[...] = tn(pair.astype(BF), item(3).astype(BF))
    done.append(move(ada, ada_o, 0))
    loads[2].wait()
    exp[...] = gm1_ref[:, 0:width].T.astype(F32)
    done.append(move(exp, exp_o, 2))
    loads[3].wait()
    qkv[...] = ga_ref[0 : 3 * ds].astype(F32)
    done.append(move(qkv, qkv_o, 3))
    proj[...] = ga_ref[3 * ds :].astype(F32)
    done.append(move(proj, proj_o, 4))
    loads[4].wait()
    done.append(move(out_ref, out_o, 11))
    loads[5].wait()
    done.append(move(dtok_ref, dtok_o, 12))
    adab_o[...] = jnp.sum(pair, axis=0)
    acc = small_ref[0, 2]
    for i in range(1, small_ref.shape[0]):
        acc = acc + small_ref[i, 2]
    redb_o[...] = acc[0]
    projb_o[...] = acc[1]
    pair_o[...] = pltpu.roll(acc, lax.rem(width - z * ds, width), 1)[2:4, 0:ds]
    corner = lax.broadcasted_iota(jnp.int32, (8, 1), 0) + lax.broadcasted_iota(jnp.int32, (1, 128), 1)
    expb_o[...] = nt(jnp.where(corner == 0, 1.0, 0.0).astype(BF), gm1_ref[:, width:])[0]
    for cp in done:
        cp.wait()


def run_widen(dims, cols, ga, gm1, gm2, small, output, tokens_grad):
    group, count, rows_s, width = dims
    ds = width // count
    vm = pl.BlockSpec(memory_space=pltpu.VMEM)
    hb = pl.BlockSpec(memory_space=pl.ANY)
    hid_s = gm1.shape[0]
    big = [(3 * ds, width), (ds, width), (width, hid_s), gm2.shape, (cols, width)]
    vecs = [(cols,), (2, ds), (width,), (width,), (hid_s,)]
    given = (ga, gm1, gm2, small, output, tokens_grad)
    rows = jax.ShapeDtypeStruct(output.shape, BF)
    return pl.pallas_call(
        functools.partial(widen_kernel, dims),
        out_shape=(rows, rows) + tuple(jax.ShapeDtypeStruct(item, F32) for item in big + vecs),
        in_specs=[hb] * 6,
        out_specs=tuple([hb] * 7 + [vm] * 5),
        scratch_shapes=[pltpu.VMEM(item.shape, item.dtype) for item in given]
        + [pltpu.VMEM(item, F32) for item in big]
        + [pltpu.SemaphoreType.DMA((13,))],
        compiler_params=pltpu.CompilerParams(vmem_limit_bytes=60 * MIB),
        name="widen_gradients",
    )(*given)


def body(
    tokens, conditioning, bucket, kept_index, w_ada, ada_bias, w_qkv, qv_bias, w_proj, proj_bias,
    w_expand, expand_bias, w_reduce, reduce_bias, out_grad, count, batch,
):
    lat, positions, width = tokens.shape
    shard_w, shard_f = w_qkv.shape[2], w_expand.shape[1]
    group = group_size(shard_f, shard_w)
    dims = (group, count, shard_f // group, width)
    cols = ada_bias.shape[0]

    (attn_in, queries, key_rows, value_rows, merged, attn_out, hidden, cot, mod, d_in, zp, g1, g2, full) = run_forward(
        dims, lat, bucket, conditioning, tokens, out_grad, kept_index, proj_bias, qv_bias, ada_bias, expand_bias,
        w_ada.T, jnp.swapaxes(w_qkv, 1, 2), w_proj, w_expand, w_reduce,
    )
    output, tokens_grad, small, ga, gm1, gm2 = run_backward(
        dims, lat, bucket, kept_index, tokens, out_grad, attn_in, queries, key_rows, value_rows, merged,
        attn_out, hidden, cot, mod, d_in, reduce_bias, conditioning,
        full.reshape(4, width, width), g1, g2, zp.reshape(-1, width),
    )

    def over_batch(items):
        if batch > group:
            return tuple(lax.psum(item * (1.0 / group), "batch") for item in items)
        return items

    ga, gm1, gm2 = over_batch((ga, gm1, gm2))
    output, tokens_grad, qkv_grad, proj_grad, expand_grad, reduce_grad, *sums = run_widen(
        dims, cols, ga, gm1, gm2, small, output, tokens_grad
    )
    ada_grad, ada_add, pair_grad, proj_add, reduce_add = over_batch(tuple(sums[:5]))
    return (
        output,
        tokens_grad,
        ada_grad.T,
        ada_add,
        jnp.swapaxes(qkv_grad.reshape(3, shard_w, width), 1, 2),
        pair_grad,
        proj_grad,
        proj_add,
        expand_grad,
        sums[5],
        reduce_grad,
        reduce_add,
    )


def solution(mesh):
    rows = P(("batch", "tp"), None, None)
    return jax.shard_map(
        functools.partial(body, count=mesh.shape["tp"], batch=mesh.shape["batch"]),
        mesh=mesh,
        in_specs=(
            rows, P("batch", None), P("batch"), P(("batch", "tp"), None), P(None, "tp"), P("tp"),
            P(None, None, "tp"), P(None, "tp"), P("tp", None), P(), P(None, "tp"), P("tp"), P("tp", None), P(), rows,
        ),
        out_specs=(
            rows, rows, P(None, "tp"), P("tp"), P(None, None, "tp"), P(None, "tp"), P("tp", None), P(),
            P(None, "tp"), P("tp"), P("tp", None), P(),
        ),
        check_vma=False,
    )
```
